32 devices in a mesh: section: 2 (over y), dp: 16 (over z, x, core).
Axes of the slice: x: 2, y: 2, z: 4, core: 2. Of those that a mesh axis runs over, the one named last changes fastest.
Arguments:
- inputs: bfloat16 [32, 512, 768], P('dp'), may hold values from -6 to 6
- cotangent: bfloat16 [32, 512, 768], P('dp'), may hold values from -6 to 6
- lengths: int32 [32], P('dp'), may hold values from 128 to 512, as said below
- first_gain: bfloat16 [2, 768], P('section', 'dp'), may hold values from 0.099609375 to 1.8984375
- first_shift: bfloat16 [2, 768], P('section', 'dp'), may hold values from -3 to 3
- value_weight: bfloat16 [2, 768, 768], P('section', 'dp'), may hold values from -0.21875 to 0.21875
- out_weight: bfloat16 [2, 768, 768], P('section', 'dp'), may hold values from -0.875 to 0.875
- out_bias: bfloat16 [2, 768], P('section', 'dp'), may hold values from -3 to 3
- second_gain: bfloat16 [2, 768], P('section', 'dp'), may hold values from 0.099609375 to 1.8984375
- second_shift: bfloat16 [2, 768], P('section', 'dp'), may hold values from -3 to 3
- up_weight: bfloat16 [2, 768, 3072], P('section', 'dp'), may hold values from -0.21875 to 0.21875
- up_bias: bfloat16 [2, 3072], P('section', 'dp'), may hold values from -3 to 3
- down_weight: bfloat16 [2, 3072, 768], P('section', 'dp'), may hold values from -0.109375 to 0.109375
- down_bias: bfloat16 [2, 768], P('section', 'dp'), may hold values from -3 to 3
- synth_first: bfloat16 [768, 768], P(('section', 'dp')), may hold values from -0.21875 to 0.21875
- synth_bias: bfloat16 [768], P(('section', 'dp')), may hold values from -3 to 3
- synth_second: bfloat16 [768, 6144], P(('section', 'dp')), may hold values from -0.625 to 0.625
- random_logits: bfloat16 [12, 512, 512], replicated, may hold values from -8 to 8
Outputs:
- states: bfloat16 [2, 32, 512, 768], P('section', 'dp')
- input_grads: bfloat16 [2, 32, 512, 768], P('section', 'dp')
- grad_first_gain: float32 [2, 768], P('section', 'dp')
- grad_first_shift: float32 [2, 768], P('section', 'dp')
- grad_value_weight: float32 [2, 768, 768], P('section', 'dp')
- grad_out_weight: float32 [2, 768, 768], P('section', 'dp')
- grad_out_bias: float32 [2, 768], P('section', 'dp')
- grad_second_gain: float32 [2, 768], P('section', 'dp')
- grad_second_shift: float32 [2, 768], P('section', 'dp')
- grad_up_weight: float32 [2, 768, 3072], P('section', 'dp')
- grad_up_bias: float32 [2, 3072], P('section', 'dp')
- grad_down_weight: float32 [2, 3072, 768], P('section', 'dp')
- grad_down_bias: float32 [2, 768], P('section', 'dp')
- grad_synth_first: float32 [768, 768], P(('section', 'dp'))
- grad_synth_bias: float32 [768], P(('section', 'dp'))
- grad_synth_second: float32 [768, 6144], P(('section', 'dp'))
- grad_random_logits: float32 [12, 512, 512], replicated
The draws below stay inside these ranges and needn't reach their ends.
Inputs may be any that keep to these rules, and one draw needn't show every extreme that they name: `lengths`: each item's length is 128, 256 or 512; rows from the length on are padding.
All inputs are finite; a program needn't handle non-finite values.
Results may differ from the reference program's by a relative error of at most 0.015.
Values may be sent and summed in bfloat16 or wider, within the bound.
A program may use at most 320 MiB of HBM per device.

```python
from functools import partial
import jax
import jax.numpy as jnp
from jax import lax

D = 768
H = 12
HD = 64
FF = 3072
LMAX = 512
ITEMS = 32


def draw_lengths(key, part):
    key = jax.random.fold_in(key, 11)
    pick_key, place_key = jax.random.split(key)
    bucket_code = jax.random.randint(pick_key, (ITEMS,), 0, 5)
    sizes_drawn = jnp.where(bucket_code == 0, LMAX, jnp.where(bucket_code <= 2, LMAX // 2, LMAX // 4))
    order_drawn = jax.random.permutation(place_key, ITEMS)
    sizes_drawn = sizes_drawn.at[order_drawn[0]].set(LMAX).at[order_drawn[1]].set(LMAX // 4)
    return sizes_drawn.astype(jnp.int32)


def levels(own_key, extent, pieces, smallest, top_value):
    factor_of = 1.0
    for position, blocks in pieces:
        draws = jax.random.uniform(jax.random.fold_in(jax.random.fold_in(own_key, 6), position), (blocks,), jnp.float32, smallest / len(pieces), top_value / len(pieces))
        factor_of = factor_of * jnp.repeat(jnp.exp(draws), extent[position] // blocks).reshape((-1,) + (1,) * (len(extent) - 1 - position))
    return factor_of


def noise(stream_key, dims, scale, most, pieces=(), kind=jnp.bfloat16):
    level = levels(stream_key, dims, pieces, -0.22, 0.18) if pieces else 1.0
    values = jax.random.normal(stream_key, dims, jnp.float32) * scale * level
    return jnp.minimum(jnp.maximum(values, -most), most).astype(kind)


def setup_inputs(seed: int = 0) -> dict:
    arg_keys = jax.random.split(jax.random.key(seed), 19)
    inputs = noise(arg_keys[0], (ITEMS, LMAX, D), 1.0, 6.0, ((0, 16),))
    cotangent = noise(arg_keys[1], (ITEMS, LMAX, D), 1.0, 6.0, ((0, 16),))
    lengths = draw_lengths(jax.random.fold_in(arg_keys[18], 71), 0)
    first_gain = jnp.clip(1.0 + 0.18 * jax.random.normal(arg_keys[3], (2, D), jnp.float32), 0.099609375, 1.8984375).astype(jnp.bfloat16)
    first_shift = noise(arg_keys[4], (2, D), 0.5, 3.0, ((0, 2), (1, 16)))
    value_weight = noise(arg_keys[5], (2, D, D), D ** -0.5, 0.21875, ((0, 2), (1, 16)))
    out_weight = noise(arg_keys[6], (2, D, D), (D // 16) ** -0.5, 0.875, ((0, 2), (1, 16)))
    out_bias = noise(arg_keys[7], (2, D), 0.5, 3.0, ((0, 2), (1, 16)))
    second_gain = jnp.clip(1.0 + 0.18 * jax.random.normal(arg_keys[8], (2, D), jnp.float32), 0.099609375, 1.8984375).astype(jnp.bfloat16)
    second_shift = noise(arg_keys[9], (2, D), 0.5, 3.0, ((0, 2), (1, 16)))
    up_weight = noise(arg_keys[10], (2, D, FF), D ** -0.5, 0.21875, ((0, 2), (1, 16)))
    up_bias = noise(arg_keys[11], (2, FF), 0.5, 3.0, ((0, 2), (1, 16)))
    down_weight = noise(arg_keys[12], (2, FF, D), FF ** -0.5, 0.109375, ((0, 2), (1, 16)))
    down_bias = noise(arg_keys[13], (2, D), 0.5, 3.0, ((0, 2), (1, 16)))
    synth_first = noise(arg_keys[14], (D, D), D ** -0.5, 0.21875, ((0, 32),))
    synth_bias = noise(arg_keys[15], (D,), 0.5, 3.0, ((0, 32),))
    synth_second = noise(arg_keys[16], (D, H * LMAX), (D // 8) ** -0.5, 0.625, ((0, 32),))
    random_logits = noise(arg_keys[17], (H, LMAX, LMAX), 2.0, 8.0)
    return dict(inputs=inputs, cotangent=cotangent, lengths=lengths, first_gain=first_gain, first_shift=first_shift, value_weight=value_weight, out_weight=out_weight, out_bias=out_bias, second_gain=second_gain, second_shift=second_shift, up_weight=up_weight, up_bias=up_bias, down_weight=down_weight, down_bias=down_bias, synth_first=synth_first, synth_bias=synth_bias, synth_second=synth_second, random_logits=random_logits)


@jax.custom_vjp
def low(v):
    return lax.optimization_barrier(v.astype(jnp.bfloat16)).astype(jnp.float32)

@jax.custom_vjp
def low_back(v):
    return v

def low_keep(v):
    return (low(v), None)

def low_pass(kept, grad):
    return (grad,)

def back_keep(v):
    return (v, None)

def back_low(kept, grad):
    return (low(grad),)
low.defvjp(low_keep, low_pass)
low_back.defvjp(back_keep, back_low)
norm_eps = 1e-05
masked_score = -1e+30

def product(left_side, right_side):
    return jnp.dot(left_side, right_side, precision=lax.Precision.HIGHEST)

def norm_rows(values, gain_row, shift_row):
    centre = values - lax.optimization_barrier(jnp.mean(values, axis=-1, keepdims=True))
    spread = lax.optimization_barrier(jnp.mean(centre * centre, axis=-1, keepdims=True))
    return centre * lax.rsqrt(spread + norm_eps) * gain_row + shift_row

def smooth_act(values):
    return jax.nn.gelu(values, approximate=True)

def dense_scores(normed, mixer_params):
    first_w, first_b, second_w, random_w = mixer_params
    hidden_pre = low_back(product(normed, first_w) + first_b)
    hidden = low(smooth_act(hidden_pre))
    flat_scores = low_back(product(hidden, second_w))
    return flat_scores.reshape(LMAX, H, LMAX).transpose(1, 0, 2)

def random_scores(normed, mixer_params):
    return mixer_params[3]

def encoder_layer(values_in, length, common, section_pos, mixer_params, score_fn):
    first_gain, first_shift, w_value, w_out, b_out, second_gain, second_shift, w_up, b_up, w_down, b_down = [stacked[section_pos] for stacked in common]
    normed = low(norm_rows(values_in, first_gain, first_shift))
    scores = score_fn(normed, mixer_params)
    keys_ok = jnp.arange(LMAX)[None, None, :] < length
    masked = jnp.where(keys_ok, scores, masked_score)
    exponent = jnp.exp(masked - lax.optimization_barrier(jnp.max(masked, axis=-1, keepdims=True)))
    attention = low(exponent / lax.optimization_barrier(jnp.sum(exponent, axis=-1, keepdims=True)))
    head_values = low(low_back(product(normed, w_value))).reshape(LMAX, H, HD)
    mixed_rows = jnp.einsum('hqk,khd->qhd', attention, head_values, precision=lax.Precision.HIGHEST)
    mixed_rows = low(low_back(mixed_rows.reshape(LMAX, D)))
    branch = low_back(product(mixed_rows, w_out) + b_out)
    residual = values_in + branch
    inner_rows = low(norm_rows(residual, second_gain, second_shift))
    up_pre = low_back(product(inner_rows, w_up) + b_up)
    ffn_out = low_back(product(low(smooth_act(up_pre)), w_down) + b_down)
    row_weight = (jnp.arange(LMAX) < length).astype(jnp.float32)[:, None]
    return (residual + ffn_out) * row_weight

def whole_block(values_in, offset, common, mixer_params, length):
    first_out = encoder_layer(values_in, length, common, 0, mixer_params, dense_scores)
    second_in = low_back(low(first_out)) + offset
    second_out = encoder_layer(second_in, length, common, 1, mixer_params, random_scores)
    return (second_out, first_out)

def reference(inputs, cotangent, lengths, first_gain, first_shift, value_weight, out_weight, out_bias, second_gain, second_shift, up_weight, up_bias, down_weight, down_bias, synth_first, synth_bias, synth_second, random_logits):
    common = tuple((stacked.astype(jnp.float32) for stacked in (first_gain, first_shift, value_weight, out_weight, out_bias, second_gain, second_shift, up_weight, up_bias, down_weight, down_bias)))
    mixer_params = tuple((stacked.astype(jnp.float32) for stacked in (synth_first, synth_bias, synth_second, random_logits)))

    def per_item(totals, item_data):
        values_in, item_cot, length = item_data
        start_rows = values_in.astype(jnp.float32)
        offset = jnp.zeros_like(start_rows)
        second_out, pull_back, first_out = jax.vjp(partial(whole_block, length=length), start_rows, offset, common, mixer_params, has_aux=True)
        grad_in, grad_offset, grad_common, grad_mixer = pull_back(item_cot.astype(jnp.float32))
        totals = jax.tree.map(jnp.add, totals, (grad_common, grad_mixer))
        outputs = (first_out.astype(jnp.bfloat16), second_out.astype(jnp.bfloat16), grad_in.astype(jnp.bfloat16), grad_offset.astype(jnp.bfloat16))
        return (totals, outputs)
    zeros_init = jax.tree.map(jnp.zeros_like, (common, mixer_params))
    totals, outputs = lax.scan(per_item, zeros_init, (inputs, cotangent, lengths))
    states = jnp.stack([outputs[0], outputs[1]])
    input_grads = jnp.stack([outputs[2], outputs[3]])
    grad_common, grad_mixer = totals
    return (states, input_grads, grad_common[0], grad_common[1], grad_common[2], grad_common[3], grad_common[4], grad_common[5], grad_common[6], grad_common[7], grad_common[8], grad_common[9], grad_common[10], grad_mixer[0], grad_mixer[1], grad_mixer[2], grad_mixer[3])
```

```python
import functools
from typing import Any, NamedTuple

import jax
import jax.numpy as jnp
from jax import lax
from jax.experimental import pallas as pl
from jax.experimental.pallas import tpu as pltpu
from jax.sharding import PartitionSpec as P

MESH = pl.DeviceIdType.MESH


class Place:
    def __init__(self, dp):
        self.chips = dp // 2
        self.reach = self.chips // 2
        self.section = lax.axis_index(section_axis)
        index = lax.axis_index(dp_axis)
        self.core = lax.rem(index, 2)
        self.chip = index // 2
        column = lax.rem(self.chip, 2)
        row = self.chip // 2
        self.position = row + column * (self.chips - 1 - 2 * row)

    def chip_at(self, steps):
        spot = lax.rem(self.position + steps + 2 * self.chips, self.chips)
        column = spot // self.reach
        row = spot + column * (self.chips - 1 - 2 * spot)
        return 2 * row + column

    def along(self, steps):
        return (self.section, 2 * self.chip_at(steps) + self.core)

    def sibling(self):
        return (self.section, 2 * self.chip + 1 - self.core)

    def across(self):
        return (1 - self.section, 2 * self.chip + self.core)

    def greet_late(self, early):
        barrier = pltpu.get_barrier_semaphore()
        near = (self.along(1), self.along(-1), self.sibling())
        for other in near:
            pl.semaphore_signal(barrier, inc=1, device_id=other, device_id_type=MESH)

        @pl.when(early)
        def _():
            pl.semaphore_wait(barrier, len(near))
            pl.semaphore_signal(barrier, inc=1, device_id=self.across(), device_id_type=MESH)

        @pl.when(jnp.logical_not(early))
        def _():
            pl.semaphore_wait(barrier, len(near) + 1)
            pl.semaphore_signal(barrier, inc=1, device_id=self.across(), device_id_type=MESH)

    def greet(self, *others):
        barrier = pltpu.get_barrier_semaphore()
        others = (self.along(1), self.along(-1), self.sibling()) + others
        for other in others:
            pl.semaphore_signal(barrier, inc=1, device_id=other, device_id_type=MESH)
        pl.semaphore_wait(barrier, len(others))


def remote(src, dst, send_sem, recv_sem, device):
    return pltpu.make_async_remote_copy(
        src_ref=src, dst_ref=dst, send_sem=send_sem, recv_sem=recv_sem,
        device_id=device, device_id_type=MESH,
    )


def hint(value, unit):
    return pl.multiple_of(value, unit)


PIECES = (
    ("second_a", 0, True),
    ("second_b", 1, True),
    ("first", 0, True),
    ("value", 0, False),
    ("out", 1, False),
    ("up", 0, False),
    ("down", 1, False),
    ("small", 0, True),
)
(FIRST_GAIN, FIRST_SHIFT, OUT_BIAS, SECOND_GAIN, SECOND_SHIFT, DOWN_BIAS, UP_BIAS, SYNTH_BIAS) = range(8)
vector_count = 8
up_row, synth_row = UP_BIAS, SYNTH_BIAS
section_axis, dp_axis = "section", "dp"
small_block = (8, 256)


def piece_view(refs, name, chip, core, section, sizes):
    rows, ff_rows, dense_rows, dense_cols, second_cols, chips = sizes
    who = 2 * chip + core
    if name in ("value", "out", "up"):
        return refs[name].at[pl.ds(hint(who * rows, rows), rows)]
    if name == "down":
        return refs[name].at[pl.ds(hint(who * ff_rows, ff_rows), ff_rows)]
    if name == "small":
        return refs[name].at[section, who]
    top = hint((section * chips + chip) * dense_rows, dense_rows)
    if name == "first":
        return refs[name].at[pl.ds(top, dense_rows), pl.ds(hint(core * dense_cols, dense_cols), dense_cols)]
    half = second_cols // 2
    left = core * second_cols + (half if name == "second_b" else 0)
    return refs["second"].at[pl.ds(top, dense_rows), pl.ds(hint(left, half), half)]


def gather_kernel(
    dp, sizes,
    value_in, out_in, up_in, down_in, first_in, second_in, *rest,
):
    vectors = rest[: vector_count]
    (
        value_ref, out_ref, up_ref, down_ref, first_ref, second_ref, table_ref,
        small_in, small_ref, first_wide, second_wide, first_stage, second_stage, wide_sems,         own_sems, ring_send, ring_recv, sib_send, sib_recv, across_send, across_recv, pass_send, pass_recv,
    ) = rest[vector_count :]
    rows, ff_rows, dense_rows, dense_cols, second_cols, chips = sizes
    place = Place(dp)
    reach = place.reach
    quarter = dense_rows // 2
    refs = dict(value=value_ref, out=out_ref, up=up_ref, down=down_ref, small=small_ref, first=first_ref, second=second_ref)
    half = second_cols // 2
    sources = dict(
        value=value_in, out=out_in, up=up_in, down=down_in, small=small_in, first=first_stage,
        second_a=second_stage.at[:, pl.ds(0, half)], second_b=second_stage.at[:, pl.ds(half, half)],
    )
    order = tuple(range(len(PIECES)))
    dense = tuple(i for i in order if PIECES[i][2])
    plain = tuple(i for i in order if not PIECES[i][2])

    def view(i, steps, section):
        return piece_view(refs, PIECES[i][0], place.chip_at(steps), place.core, section, sizes)

    def carried(i, way, step):
        return step < reach - 1 or (step == reach - 1 and PIECES[i][1] == way)

    def ring_copy(i, way, step):
        turn = 1 if way == 0 else -1
        target = view(i, -turn * step, place.section)
        source = sources[PIECES[i][0]] if step == 0 else target
        return remote(source, target, ring_send.at[way, step, i], ring_recv.at[way, step, i], place.along(turn))

    def slot(way, step):
        return 0 if step < 0 else 1 + 2 * step + way

    def sibling_copy(i, way, step):
        turn = 1 if way == 0 else -1
        target = view(i, -turn * (step + 1) if step >= 0 else 0, place.section)
        source = sources[PIECES[i][0]] if step < 0 else target
        at = slot(way, step)
        return remote(source, target, sib_send.at[at, i], sib_recv.at[at, i], place.sibling())

    def across_copy(i, way, step):
        turn = 1 if way == 0 else -1
        target = view(i, -turn * (step + 1) if step >= 0 else 0, place.section)
        source = sources[PIECES[i][0]] if step < 0 else target
        at = slot(way, step)
        return remote(source, target, across_send.at[at, i], across_recv.at[at, i], place.across())

    def pass_copy(i, way, step):
        turn = 1 if way == 0 else -1
        target = view(i, -turn * (step + 1) if step >= 0 else 0, 1 - place.section)
        at = slot(way, step)
        return remote(target, target, pass_send.at[at, i], pass_recv.at[at, i], place.sibling())

    def own_copy(i):
        return pltpu.make_async_copy(sources[PIECES[i][0]], view(i, 0, place.section), own_sems.at[i])

    def begin(i):
        for way in (0, 1):
            if carried(i, way, 0):
                ring_copy(i, way, 0).start()
        sibling_copy(i, 0, -1).start()
        if PIECES[i][2]:
            across_copy(i, 0, -1).start()
        own_copy(i).start()

    small_in[...] = jnp.zeros(small_block, jnp.float32)
    for row, ref in enumerate(vectors):
        small_in[row : row + 1, : ref.shape[1]] = ref[...].astype(jnp.float32)
    mine = hint(place.core * quarter, 8)
    first_wide[pl.ds(mine, quarter)] = first_in[...].astype(jnp.float32)
    second_wide[pl.ds(mine, quarter)] = second_in[...].astype(jnp.float32)
    place.greet(place.across())
    wide = [
        remote(ref.at[pl.ds(mine, quarter)], ref.at[pl.ds(mine, quarter)], wide_sems.at[0, n], wide_sems.at[1, n], place.sibling())
        for n, ref in enumerate((first_wide, second_wide))
    ]
    for copy in wide:
        copy.start()
    for copy in wide:
        copy.wait()
    first_stage[...] = first_wide[:, pl.ds(hint(place.core * dense_cols, dense_cols), dense_cols)].astype(jnp.bfloat16)
    second_stage[...] = second_wide[:, pl.ds(hint(place.core * second_cols, second_cols), second_cols)].astype(jnp.bfloat16)
    for i in dense + plain:
        begin(i)

    events = [(i, way, step) for step in range(reach) for i in order for way in (0, 1) if carried(i, way, step)]
    crossing = [(i, 0, -1) for i in dense] + [e for e in events if e[0] in dense]
    passed = 0

    def pass_on(count):
        nonlocal passed
        while passed < min(count, len(crossing)):
            e = crossing[passed]
            across_copy(*e).wait_recv()
            pass_copy(*e).start()
            passed += 1

    for i, way, step in events:
        ring_copy(i, way, step).wait_recv()
        if carried(i, way, step + 1):
            ring_copy(i, way, step + 1).start()
        sibling_copy(i, way, step).start()
        if i in dense:
            across_copy(i, way, step).start()
        if i == order[-1] and way == 0:
            pass_on(len(dense) + 2 * len(dense) * step)
    pass_on(len(crossing))
    for i in order:
        own_copy(i).wait()
        sibling_copy(i, 0, -1).wait()
        for way in (0, 1):
            if carried(i, way, 0):
                ring_copy(i, way, 0).wait_send()
    for i, way, step in events:
        sibling_copy(i, way, step).wait()
        if step > 0:
            ring_copy(i, way, step).wait_send()
    for e in crossing:
        across_copy(*e).wait_send()
        pass_copy(*e).wait()
    shares = [ref.shape[1] for ref in vectors]
    share = shares[0]

    def side_by_side(blocks):
        return jnp.concatenate(blocks, axis=1)

    table_ref[:up_row, : dp * share] = side_by_side([small_ref[place.section, d, :up_row, :share] for d in range(dp)])
    up_share = shares[up_row]
    table_ref[up_row : up_row + 1, :] = side_by_side(
        [small_ref[place.section, d, up_row : up_row + 1, :up_share] for d in range(dp)]
    )
    synth_share = shares[synth_row]
    table_ref[synth_row : synth_row + 1, : 2 * dp * synth_share] = side_by_side(
        [small_ref[s, d, synth_row : synth_row + 1, :synth_share] for s in range(2) for d in range(dp)]
    )


def gather_weights(dp, value, out, up, down, first, second, vectors):
    rows, width = value.shape
    ff_rows = down.shape[0]
    ff = up.shape[1]
    chips = dp // 2
    dense_rows = 2 * first.shape[0]
    dense_cols = first.shape[1] // 2
    second_cols = second.shape[1] // 2
    sizes = (rows, ff_rows, dense_rows, dense_cols, second_cols, chips)
    reach = chips // 2
    count = len(PIECES)
    bf = jnp.bfloat16
    anywhere = pl.BlockSpec(memory_space=pl.ANY)
    inside = pl.BlockSpec(memory_space=pltpu.VMEM)
    dma = pltpu.SemaphoreType.DMA
    return pl.pallas_call(
        functools.partial(gather_kernel, dp, sizes),
        out_shape=(
            jax.ShapeDtypeStruct((rows * dp, width), bf),
            jax.ShapeDtypeStruct((rows * dp, width), bf),
            jax.ShapeDtypeStruct((rows * dp, ff), bf),
            jax.ShapeDtypeStruct((ff_rows * dp, width), bf),
            jax.ShapeDtypeStruct((2 * dp * first.shape[0], first.shape[1]), bf),
            jax.ShapeDtypeStruct((2 * dp * second.shape[0], second.shape[1]), bf),
            jax.ShapeDtypeStruct((vector_count, ff), jnp.float32),
        ),
        in_specs=[anywhere] * 4 + [inside] * (2 + len(vectors)),
        out_specs=[anywhere] * 6 + [inside],
        scratch_shapes=[
            pltpu.VMEM(small_block, jnp.float32),
            pltpu.VMEM((2, dp) + small_block, jnp.float32),
            pltpu.VMEM((dense_rows, 2 * dense_cols), jnp.float32),
            pltpu.VMEM((dense_rows, 2 * second_cols), jnp.float32),
            pltpu.VMEM((dense_rows, dense_cols), bf),
            pltpu.VMEM((dense_rows, second_cols), bf),
            dma((2, 2)),
            dma((count,)),
            dma((2, reach, count)),
            dma((2, reach, count)),
            dma((1 + 2 * reach, count)),
            dma((1 + 2 * reach, count)),
            dma((1 + 2 * reach, count)),
            dma((1 + 2 * reach, count)),
            dma((1 + 2 * reach, count)),
            dma((1 + 2 * reach, count)),
        ],
        compiler_params=pltpu.CompilerParams(
            collective_id=0, has_side_effects=True, vmem_limit_bytes=63 << 20
        ),
        name="gather_weights",
    )(value, out, up, down, first, second, *vectors)


def store_sum(target, terms, rows):
    if rows == 0:
        total = terms[0][...]
        for term in terms[1:]:
            total = total + term[...]
        target[...] = total
        return

    def some(n, carry):
        at = pl.ds(pl.multiple_of(n * 16, 16), 16)
        total = terms[0][at, :].astype(jnp.float32)
        for term in terms[1:]:
            total = total + term[at, :].astype(jnp.float32)
        target[at, :] = total.astype(target.dtype)
        return carry

    lax.fori_loop(0, rows // 16, some, 0)


def reduce_kernel(dp, sizes, shares, tables, value_in, out_in, up_in, down_in, first_in, second_in, random_in, *rest):
    dense_tables, random_tables = rest[:tables], rest[tables : 2 * tables]
    (
    value_ref, out_ref, up_ref, down_ref, small_ref, first_ref, second_ref, random_ref,
    small_in, own_value, own_out, own_up, own_down, own_small, own_first, own_second,
    sib_value, sib_out, sib_up, sib_down, sib_small, sib_first, sib_second,
    ring_value, ring_out, ring_up, ring_down, ring_small, ring_first, ring_second,
    across_small, across_first, across_second, first_wide, second_wide, first_part, second_part,
    own_sems, sib_send, sib_recv, ring_send, ring_recv, across_send, across_recv, wide_sems,
    random_sems, turn_send, turn_recv, pass_send, pass_recv,
    ) = rest[2 * tables :]
    rows, ff_rows, dense_rows, dense_cols, second_cols, chips = sizes
    place = Place(dp)
    reach = place.reach
    half = second_cols // 2
    quarter = dense_rows // 2
    is_dense = place.section == 0
    full = dict(value=value_in, out=out_in, up=up_in, down=down_in, small=small_in, first=first_in, second=second_in)
    own = dict(value=own_value, out=own_out, up=own_up, down=own_down, small=own_small, first=own_first, second=own_second)
    sib = dict(value=sib_value, out=sib_out, up=sib_up, down=sib_down, small=sib_small, first=sib_first, second=sib_second)
    ring = dict(value=ring_value, out=ring_out, up=ring_up, down=ring_down, small=ring_small, first=ring_first, second=ring_second)
    crossed = dict(first=across_first, second=across_second, small=across_small)
    order = tuple(range(len(PIECES)))
    small = len(PIECES) - 1
    crossing = tuple(i for i in order if PIECES[i][2])
    dense = crossing[:-1]
    plain = tuple(i for i in order if not PIECES[i][2])
    piece_rows = dict(value=rows, out=rows, up=rows, down=ff_rows, small=0, first=dense_rows, second_a=dense_rows, second_b=dense_rows)
    away = (reach,) + tuple(o for t in range(reach - 1, 0, -1) for o in (t, -t)) + (0,)
    spot_of = {o: n for n, o in enumerate(away)}
    spot_of[-reach] = 0

    def part(table, i, *at):
        name = PIECES[i][0]
        if name == "second_a":
            return table["second"].at[(*at, slice(None), pl.ds(0, half))]
        if name == "second_b":
            return table["second"].at[(*at, slice(None), pl.ds(half, half))]
        return table[name].at[at]

    def held(table, i, o, plane):
        spot = spot_of[o]
        return part(table, i, plane, spot) if PIECES[i][2] else part(table, i, spot)

    def source(i, o, core, plane):
        section = place.section if plane == 0 else 1 - place.section
        return piece_view(full, PIECES[i][0], place.chip_at(o), core, section, sizes)

    def load(i, o, plane):
        return pltpu.make_async_copy(
            source(i, o, place.core, plane), held(own, i, o, plane), own_sems.at[plane, spot_of[o], i]
        )

    def lend(i, o, plane):
        at = (plane, spot_of[o], i)
        return remote(source(i, o, 1 - place.core, plane), held(sib, i, o, plane), sib_send.at[at], sib_recv.at[at], place.sibling())

    def ring_copy(i, way, step):
        turn = 1 if way == 0 else -1
        o = turn * (reach - step)
        return remote(held(own, i, o, 0), part(ring, i, way, step), ring_send.at[way, step, i], ring_recv.at[way, step, i], place.along(turn))

    def across_copy(i, o):
        at = (spot_of[o], i)
        return remote(held(own, i, o, 1), part(crossed, i, spot_of[o]), across_send.at[at], across_recv.at[at], place.across())

    def carried(i, way, step):
        return step > 0 or PIECES[i][1] == way

    def local_terms(i, o):
        load(i, o, 0).wait()
        lend(i, o, 0).wait_recv()
        return [held(own, i, o, 0), held(sib, i, o, 0)]

    def total(target, i, o, arrived):
        if i == small:
            terms = local_terms(i, o) + arrived

            @pl.when(is_dense)
            def _():
                store_sum(target, terms, 0)

            @pl.when(jnp.logical_not(is_dense))
            def _():
                across_copy(i, o).wait_recv()
                store_sum(target, terms + [part(crossed, i, spot_of[o])], 0)
        elif PIECES[i][2]:

            @pl.when(is_dense)
            def _():
                store_sum(target, local_terms(i, o) + arrived, piece_rows[PIECES[i][0]])

            @pl.when(jnp.logical_not(is_dense))
            def _():
                across_copy(i, o).wait_recv()
                store_sum(target, [part(crossed, i, spot_of[o])] + arrived, piece_rows[PIECES[i][0]])
        else:
            store_sum(target, local_terms(i, o) + arrived, piece_rows[PIECES[i][0]])

    def arrivals(i, o):
        ways = (0, 1) if o == 0 else ((0,) if o > 0 else (1,))
        found = []
        for way in ways:
            step = reach - abs(o) - 1
            if step >= 0 and carried(i, way, step):
                ring_copy(i, way, step).wait_recv()
                found.append(part(ring, i, way, step))
        return found

    small_in[...] = jnp.zeros(small_in.shape, jnp.float32)

    def blocks_of(got, section, names):
        whole = got[0][...]
        for more in got[1:]:
            whole = whole + more[...]
        for d in range(dp):
            if names:
                share = shares[0]
                small_in[section, d, :up_row, :share] = whole[:up_row, d * share : (d + 1) * share]
                share = shares[up_row]
                small_in[section, d, up_row : up_row + 1, :share] = whole[up_row : up_row + 1, d * share : (d + 1) * share]
            if got is dense_tables:
                share = shares[synth_row]
                left = (section * dp + d) * share
                small_in[section, d, synth_row : synth_row + 1, :share] = whole[synth_row : synth_row + 1, left : left + share]

    @pl.when(is_dense)
    def _():
        blocks_of(dense_tables, 0, True)
        blocks_of(dense_tables, 1, False)

    @pl.when(jnp.logical_not(is_dense))
    def _():
        blocks_of(random_tables, 1, True)

    place.greet_late(jnp.logical_not(is_dense))
    for o in away:
        for i in plain + (small,):
            lend(i, o, 0).start()
            load(i, o, 0).start()

        @pl.when(is_dense)
        def _():
            for plane in (1, 0):
                for i in dense + ((small,) if plane == 1 else ()):
                    lend(i, o, plane).start()
                    load(i, o, plane).start()

    block = random_ref.shape[0] // (2 * chips)
    strip = block // 2

    def view(i, o, core):
        top = (core * chips + place.chip_at(o)) * block + i * strip
        return random_ref.at[pl.ds(pl.multiple_of(top, strip), strip)]

    def spread(i, way, step):
        return step < reach - 1 or i == way

    def turn_copy(i, way, step):
        turn = 1 if way == 0 else -1
        target = view(i, -turn * step, place.core)
        source = random_in.at[pl.ds(i * strip, strip)] if step == 0 else target
        return remote(source, target, turn_send.at[way, step, i], turn_recv.at[way, step, i], place.along(turn))

    def pass_copy(i, way, step):
        turn = 1 if way == 0 else -1
        target = view(i, -turn * (step + 1) if step >= 0 else 0, place.core)
        source = random_in.at[pl.ds(i * strip, strip)] if step < 0 else target
        at = 0 if step < 0 else 1 + 2 * step + way
        return remote(source, target, pass_send.at[at, i], pass_recv.at[at, i], place.sibling())

    def keep_copy(i):
        return pltpu.make_async_copy(random_in.at[pl.ds(i * strip, strip)], view(i, 0, place.core), random_sems.at[1, 1, i])

    def across_strip(o, device, way):
        top = pl.multiple_of((place.core * chips + place.chip_at(o)) * block, block)
        part_of = random_ref.at[pl.ds(top, block)]
        return remote(part_of, part_of, random_sems.at[way, 0, 2 + spot_of[o]], random_sems.at[way, 1, 2 + spot_of[o]], device)

    events = [(i, way, step) for step in range(reach) for i in (0, 1) for way in (0, 1) if spread(i, way, step)]

    @pl.when(jnp.logical_not(is_dense))
    def _():
        for i in (0, 1):
            for way in (0, 1):
                if spread(i, way, 0):
                    turn_copy(i, way, 0).start()
            pass_copy(i, 0, -1).start()
            keep_copy(i).start()
        for i, way, step in events:
            turn_copy(i, way, step).wait_recv()
            if step + 1 < reach and spread(i, way, step + 1):
                turn_copy(i, way, step + 1).start()
            pass_copy(i, way, step).start()
        for i in (0, 1):
            keep_copy(i).wait()
        pl.semaphore_wait(pltpu.get_barrier_semaphore(), 1)
        for o in away:
            across_strip(o, place.across(), 0).start()

    def cross(o):
        @pl.when(is_dense)
        def _():
            for i in crossing:
                load(i, o, 1).wait()
                lend(i, o, 1).wait_recv()
                store_sum(held(own, i, o, 1), [held(own, i, o, 1), held(sib, i, o, 1)], piece_rows[PIECES[i][0]])
                across_copy(i, o).start()

    for step in range(reach):
        for i in plain + crossing:
            for way in (0, 1):
                if carried(i, way, step):
                    o = (reach - step) * (1 if way == 0 else -1)
                    total(held(own, i, o, 0), i, o, arrivals(i, o))
                    ring_copy(i, way, step).start()
            if i == plain[-1]:
                for o in away[(0 if step == 0 else 2 * step - 1) : 2 * step + 1]:
                    cross(o)
    cross(0)

    @pl.when(is_dense)
    def _():
        for o in away:
            across_strip(o, place.across(), 0).wait_recv()
            across_strip(o, place.sibling(), 1).start()

    outs = dict(value=value_ref, out=out_ref, up=up_ref, down=down_ref, small=small_ref)
    for i in plain + (small,):
        total(outs[PIECES[i][0]], i, 0, arrivals(i, 0))
    wides = dict(first=first_wide, second_a=second_wide.at[:, pl.ds(0, half)], second_b=second_wide.at[:, pl.ds(half, half)])
    for i in dense:
        total(wides[PIECES[i][0]], i, 0, arrivals(i, 0))
    mine = pl.multiple_of(place.core * quarter, 8)
    theirs = pl.multiple_of((1 - place.core) * quarter, 8)
    last = [
        remote(wide.at[pl.ds(theirs, quarter)], got, wide_sems.at[0, n], wide_sems.at[1, n], place.sibling())
        for n, (wide, got) in enumerate(((first_wide, first_part), (second_wide, second_part)))
    ]
    for copy in last:
        copy.start()
    for copy in last:
        copy.wait()
    for ref, wide, got, cols in ((first_ref, first_wide, first_part, dense_cols), (second_ref, second_wide, second_part, second_cols)):
        ref[:, pl.ds(pl.multiple_of(place.core * cols, cols), cols)] = wide[pl.ds(mine, quarter), :]
        ref[:, pl.ds(pl.multiple_of((1 - place.core) * cols, cols), cols)] = got[...]

    for o in away:
        for i in plain + (small,):
            lend(i, o, 0).wait_send()

        @pl.when(is_dense)
        def _():
            for i in dense:
                lend(i, o, 0).wait_send()
            for i in crossing:
                lend(i, o, 1).wait_send()
                across_copy(i, o).wait_send()

    @pl.when(is_dense)
    def _():
        for o in away:
            across_strip(o, place.sibling(), 1).wait()

    @pl.when(jnp.logical_not(is_dense))
    def _():
        for o in away:
            across_strip(o, place.across(), 0).wait_send()
        for i in (0, 1):
            pass_copy(i, 0, -1).wait()
            for way in (0, 1):
                for step in range(reach):
                    if spread(i, way, step):
                        turn_copy(i, way, step).wait_send()
        for e in events:
            pass_copy(*e).wait()

    for step in range(reach):
        for i in order:
            for way in (0, 1):
                if carried(i, way, step):
                    ring_copy(i, way, step).wait_send()


def reduce_grads(dp, value, out, up, down, first, second, random, dense_tables, random_tables, shares):
    chips = dp // 2
    rows, width = value.shape[0] // dp, value.shape[1]
    ff_rows = down.shape[0] // dp
    ff = up.shape[1]
    dense_rows = first.shape[0] // dp
    dense_cols = first.shape[1] // 2
    second_cols = second.shape[1] // 2
    sizes = (rows, ff_rows, dense_rows, dense_cols, second_cols, chips)
    reach = chips // 2
    count = len(PIECES)
    bf, f32 = jnp.bfloat16, jnp.float32
    anywhere = pl.BlockSpec(memory_space=pl.ANY)
    inside = pl.BlockSpec(memory_space=pltpu.VMEM)
    dma = pltpu.SemaphoreType.DMA
    blocks = ((rows, width), (rows, width), (rows, ff), (ff_rows, width))
    wide = ((dense_rows, dense_cols), (dense_rows, second_cols))
    scratch = [pltpu.VMEM((2, dp) + small_block, f32)]
    for _ in range(2):
        scratch += [pltpu.VMEM((chips,) + b, bf) for b in blocks]
        scratch += [pltpu.VMEM((2, chips) + small_block, f32)]
        scratch += [pltpu.VMEM((2, chips) + w, bf) for w in wide]
    scratch += [pltpu.VMEM((2, reach) + b, bf) for b in blocks]
    scratch += [pltpu.VMEM((2, reach) + small_block, f32)]
    scratch += [pltpu.VMEM((2, reach) + w, bf) for w in wide]
    scratch += [pltpu.VMEM((chips,) + small_block, f32)]
    scratch += [pltpu.VMEM((chips,) + w, bf) for w in wide]
    scratch += [pltpu.VMEM(w, f32) for w in wide]
    scratch += [pltpu.VMEM((dense_rows // 2, w[1]), f32) for w in wide]
    scratch += [
        dma((2, chips, count)),
        dma((2, chips, count)),
        dma((2, chips, count)),
        dma((2, reach, count)),
        dma((2, reach, count)),
        dma((chips, count)),
        dma((chips, count)),
        dma((2, 2)),
        dma((2, 2, 2 + chips)),
        dma((2, reach, 2)),
        dma((2, reach, 2)),
        dma((1 + 2 * reach, 2)),
        dma((1 + 2 * reach, 2)),
    ]
    tables = len(dense_tables)
    return pl.pallas_call(
        functools.partial(reduce_kernel, dp, sizes, shares, tables),
        out_shape=tuple(jax.ShapeDtypeStruct(b, f32) for b in blocks + (small_block,))
        + (
            jax.ShapeDtypeStruct((dense_rows // 2, first.shape[1]), f32),
            jax.ShapeDtypeStruct((dense_rows // 2, second.shape[1]), f32),
            jax.ShapeDtypeStruct((dp * random.shape[0], random.shape[1]), bf),
        ),
        in_specs=[anywhere] * 7 + [inside] * (2 * tables),
        out_specs=[inside] * 7 + [anywhere],
        scratch_shapes=scratch,
        compiler_params=pltpu.CompilerParams(
            collective_id=1, has_side_effects=True, vmem_limit_bytes=63 << 20
        ),
        name="reduce_grads",
    )(value, out, up, down, first, second, random, *dense_tables, *random_tables)


norm_eps = 1e-05
masked_score = -1e30
gelu_scale = 0.7978845608028654
gelu_cube = 0.044715
bf16, f32 = jnp.bfloat16, jnp.float32


def dot_rows(a, b):
    return lax.dot_general(a, b, (((1,), (0,)), ((), ())), preferred_element_type=f32)


def dot_back(a, b):
    return lax.dot_general(a, b, (((1,), (1,)), ((), ())), preferred_element_type=f32)


def dot_down(a, b):
    return lax.dot_general(a, b, (((0,), (0,)), ((), ())), preferred_element_type=f32)


def gelu_tanh(v):
    return jnp.tanh(gelu_scale * (v + gelu_cube * (v * v * v)))


def gelu(v):
    return 0.5 * v * (1.0 + gelu_tanh(v))


def gelu_both(v):
    t = gelu_tanh(v)
    value = 0.5 * v * (1.0 + t)
    slope = 0.5 * (1.0 + t) + 0.5 * v * (1.0 - t * t) * (gelu_scale * (1.0 + 3.0 * gelu_cube * (v * v)))
    return value, slope


def standard(v):
    centre = v - jnp.mean(v, axis=-1, keepdims=True)
    inverse = lax.rsqrt(jnp.mean(centre * centre, axis=-1, keepdims=True) + norm_eps)
    return centre * inverse, inverse


def standard_back(unit, inverse, grad):
    middle = jnp.mean(grad, axis=-1, keepdims=True)
    slant = jnp.mean(grad * unit, axis=-1, keepdims=True)
    return inverse * (grad - middle - unit * slant)


def column_sum(v):
    return jnp.sum(v.astype(f32), axis=0, keepdims=True)


class Bench:
    def __init__(self, **refs):
        self.__dict__.update(refs)
        self.waiting = {}
        self.used = 0
        self.sent = []
        self.last_tiles = []

    def vector(self, name, at):
        row = name
        return self.vectors[row : row + 1, at]

    def put_vector(self, name, at, value):
        row = name
        self.vector_grads[row : row + 1, at] = value

    def fetch(self, name, source, target):
        copy = pltpu.make_async_copy(source, target, self.sems.at[self.used])
        self.used += 1
        copy.start()
        self.waiting[name] = copy

    def need(self, *names):
        for name in names:
            copy = self.waiting.pop(name, None)
            if copy is not None:
                copy.wait()

    def send(self, source, target):
        copy = pltpu.make_async_copy(source, target, self.sems.at[self.used])
        self.used += 1
        copy.start()
        self.sent.append(copy)

    def settle(self):
        for copy in self.last_tiles:
            copy.wait()
        self.last_tiles = []

    def finish(self):
        self.settle()
        for copy in self.sent:
            copy.wait()

    def plan(self, added, *grads):
        self.added = added
        self.planned = list(grads)
        self.ahead()

    def tile_copies(self, grad, cols):
        across = grad.shape[1] // cols
        count = grad.shape[0] // unit_cols * across

        def place(t):
            top = pl.multiple_of(t // across * unit_cols, unit_cols)
            left = pl.multiple_of(lax.rem(t, across) * cols, cols)
            return grad.at[pl.ds(top, unit_cols), pl.ds(left, cols)]

        def result(t):
            slot = lax.rem(t, tile_slots)
            return pltpu.make_async_copy(self.stage.at[slot, :, pl.ds(0, cols)], place(t), self.stage_sems.at[slot])

        def prior(t):
            slot = lax.rem(t, tile_slots)
            return pltpu.make_async_copy(place(t), self.prior_stage.at[slot, :, pl.ds(0, cols)], self.prior_sems.at[slot])

        return count, across, result, prior

    def ahead(self):
        if self.added and self.planned:
            count, _, _, prior = self.tile_copies(*self.planned[0])
            for t in range(min(count, tile_slots - 1)):
                prior(t).start()

    def emit(self, tile):
        grad, cols = self.planned.pop(0)
        added = self.added
        count, across, result, prior = self.tile_copies(grad, cols)
        reach = tile_slots - 1
        self.settle()

        def turn(t, carry):
            slot = lax.rem(t, tile_slots)
            if added:

                @pl.when(t + reach < count)
                def _():
                    prior(t + reach).start()

                prior(t).wait()

            @pl.when(t >= tile_slots)
            def _():
                result(t - tile_slots).wait()

            def write(value, lanes=None):
                at = (slot, slice(None), pl.ds(0, cols) if lanes is None else lanes)
                if value is None:
                    self.stage[at] = self.prior_stage[at] if added else jnp.zeros((unit_cols, lanes.size), bf16)
                else:
                    if added:
                        value = value + self.prior_stage[at].astype(f32)
                    self.stage[at] = value.astype(bf16)

            tile(t // across, lax.rem(t, across), write)
            result(t).start()
            return carry

        lax.fori_loop(0, count, turn, 0)
        self.last_tiles = [result(t) for t in range(max(0, count - tile_slots), count)]
        self.ahead()


tile_slots = 6
unit_cols = 256
unit_rows = 128


def cols_at(t):
    return pl.ds(pl.multiple_of(t * unit_cols, unit_cols), unit_cols)


def by_cols(n, extent, body):
    def turn(t, carry):
        body(pl.ds(0, n), cols_at(t), t)
        return carry

    lax.fori_loop(0, extent // unit_cols, turn, 0)


def by_rows(n, body, start=0):
    def turn(t, carry):
        return body(pl.ds(pl.multiple_of(t * unit_rows, unit_rows), unit_rows), carry)

    return lax.fori_loop(0, n // unit_rows, turn, start)


def lanes_of_first(n, size):
    return lax.broadcasted_iota(jnp.int32, (n, 2 * size), 1) < size


def send_padded(b, n, **targets):
    for name, target in targets.items():
        ref = getattr(b, name)
        if n < b.slots:
            ref[n:] = jnp.zeros((b.slots - n, ref.shape[1]), bf16)
        b.send(ref, target)


def softmax(b, n, scores):
    if n < b.slots:
        scores = jnp.where(in_item(b, (n, n), 1), scores, masked_score)
    e = jnp.exp(scores - jnp.max(scores, axis=-1, keepdims=True))
    return (e * (1.0 / jnp.sum(e, axis=-1, keepdims=True))).astype(bf16)


def forward_part(b, n, dense):
    width, ff, heads, slots = b.width, b.ff, b.heads, b.slots
    size = width // heads
    whole = slice(0, width)
    rows = pl.ds(0, n)

    def first_norm(at, carry):
        unit, _ = standard(b.x[at, :].astype(f32))
        b.a[at, :] = (unit * b.vector(FIRST_GAIN, whole) + b.vector(FIRST_SHIFT, whole)).astype(bf16)
        return carry

    b.need("x")
    by_rows(n, first_norm)
    if dense:
        b.need("first")

        def hidden(rows, at, t):
            p = dot_rows(b.a[rows], b.first[:, at]) + b.vector(SYNTH_BIAS, at)
            b.p[rows, at] = p
            b.s[rows, at] = gelu(p).astype(bf16)

        by_cols(n, width, hidden)
        b.send(b.p.at[rows], b.p_out.at[rows])
    b.need("value")

    def project(rows, at, t):
        b.v[rows, at] = dot_rows(b.a[rows], b.value[:, at]).astype(bf16)

    by_cols(n, width, project)
    b.need("second" if dense else "att")

    def pair(i, carry):
        here = pl.ds(pl.multiple_of(i * 2 * size, 2 * size), 2 * size)
        values = b.v[:n, here]
        got = []
        for j in range(2):
            h = 2 * i + j
            if dense:
                scores = dot_rows(b.s[:n], b.second[:, pl.ds(pl.multiple_of(h * slots, slots), n)])
                b.att[h, :n, :n] = softmax(b, n, scores)
            got.append(dot_rows(b.att[h, :n, :n], values))
        b.o[:n, here] = jnp.where(lanes_of_first(n, size), got[0], got[1]).astype(bf16)
        return carry

    lax.fori_loop(0, heads // 2, pair, 0)
    if dense:
        b.send(b.att.at[:, rows, rows], b.att_out.at[:, rows, rows])
        b.send(b.v.at[rows], b.v_out.at[rows])
        b.send(b.o.at[rows], b.o_out.at[rows])
    b.need("out")

    def branch(rows, at, t):
        b.y[rows, at] = b.x[rows, at].astype(f32) + (dot_rows(b.o[rows], b.out[:, at]) + b.vector(OUT_BIAS, at))

    by_cols(n, width, branch)
    if dense:
        b.send(b.y.at[rows], b.y_out.at[rows])

    def second_norm(at, carry):
        unit, _ = standard(b.y[at, :])
        b.u[at, :] = (unit * b.vector(SECOND_GAIN, whole) + b.vector(SECOND_SHIFT, whole)).astype(bf16)
        return carry

    by_rows(n, second_norm)
    b.need("up")

    def up(rows, at, t):
        m = dot_rows(b.u[rows], b.up[:, at]) + b.vector(UP_BIAS, at)
        b.m[rows, at] = m.astype(b.m.dtype)
        b.r[rows, at] = gelu(m).astype(bf16)

    by_cols(n, ff, up)
    if dense:
        b.send(b.m.at[rows], b.m_out.at[rows])
    b.need("down")

    def down(rows, at, t):
        z = b.y[rows, at] + (dot_rows(b.r[rows], b.down[:, at]) + b.vector(DOWN_BIAS, at))
        if n < slots:
            z = jnp.where(in_item(b, (n, unit_cols), 0), z, 0.0)
        b.z[rows, at] = z.astype(bf16)

    by_cols(n, width, down)
    if n < slots:
        b.z[n:] = jnp.zeros((slots - n, width), bf16)
    b.send(b.z, b.states.at[b.item])
    if dense:
        b.send(b.z, b.z_out)
    else:
        send_padded(b, n, r=b.r_out, o=b.o_out, a=b.a_out)


def plan_grads(b, dense, added):
    wide = 2 * b.width
    grads = [(b.down_grad, b.width), (b.up_grad, wide), (b.out_grad, b.width), (b.value_grad, b.width)]
    if dense:
        grads += [(b.second_grad, wide), (b.first_grad, b.width)]
    b.plan(added, *grads)


def random_copies(b, n):
    part = pl.ds(0, n)

    def prior(i):
        slot = lax.rem(i, 2)
        return pltpu.make_async_copy(
            b.random_grad.at[pl.ds(2 * i, 2), part, part], b.random_old.at[slot, :, part, part], b.random_sems.at[0, slot]
        )

    def result(i):
        slot = lax.rem(i, 2)
        return pltpu.make_async_copy(
            b.random_stage.at[slot, :, part, part], b.random_grad.at[pl.ds(2 * i, 2), part, part], b.random_sems.at[1, slot]
        )

    return prior, result


def backward_part(b, n, dense, added):
    width, ff, heads, slots = b.width, b.ff, b.heads, b.slots
    size = width // heads
    wide = 2 * width
    whole = slice(0, width)
    b.need("c", "m", "down")
    if not dense and n < slots:
        b.c[:n] = jnp.where(in_item(b, (n, width), 0), b.c[:n], jnp.zeros((), bf16))

    def down_rows(rows, at, t):
        dr = dot_back(b.c[rows], b.down_rows(t))
        value, slope = gelu_both(b.m[rows, at].astype(f32))
        gm = (slope * dr).astype(bf16)
        b.gm[rows, at] = gm
        b.put_vector(UP_BIAS, at, column_sum(gm))
        return value

    def down_tile(t, _, write):
        value = down_rows(pl.ds(0, n), cols_at(t), t)
        write(dot_down(value.astype(bf16), b.c[:n]))

    if dense:
        b.emit(down_tile)
    else:
        by_cols(n, ff, down_rows)
        send_padded(b, n, gm=b.gm_out, c=b.c_out)
    b.need("up", "y")

    def up_back(rows, at, t):
        b.wide[rows, at] = dot_back(b.gm[rows], b.up[at, :ff])

    by_cols(n, width, up_back)
    if dense:
        b.fetch("second", b.second_in, b.up)
    none = jnp.zeros((1, width), f32)

    def second_back(at, carry):
        unit, inverse = standard(b.y[at, :])
        gain = b.vector(SECOND_GAIN, whole)
        b.u[at, :] = (unit * gain + b.vector(SECOND_SHIFT, whole)).astype(bf16)
        du = b.wide[at, :]
        gf = b.c[at, :].astype(f32)
        gy = gf + standard_back(unit, inverse, du * gain)
        b.gy[at, :] = gy
        gb = gy.astype(bf16)
        b.gb[at, :] = gb
        found = (column_sum(du * unit), column_sum(du), column_sum(gb), column_sum(gf))
        return tuple(a + f for a, f in zip(carry, found))

    sums = by_rows(n, second_back, (none,) * 4)
    for name, total in zip((SECOND_GAIN, SECOND_SHIFT, OUT_BIAS, DOWN_BIAS), sums):
        b.put_vector(name, whole, total)
    if dense:
        b.emit(
            lambda t, s, write: write(dot_down(b.u[:n, cols_at(t)], b.gm[:n, pl.ds(pl.multiple_of(s * wide, wide), wide)])),
        )
    else:
        send_padded(b, n, u=b.u_out, gb=b.gb_out)
    b.need("o", "out")
    if dense:
        b.emit(lambda t, s, write: write(dot_down(b.o[:n, cols_at(t)], b.gb[:n])))

    def out_back(rows, at, t):
        b.go[rows, at] = dot_back(b.gb[rows], b.out[at, :]).astype(bf16)

    by_cols(n, width, out_back)
    b.need("v", "att")

    def pair_back(i, keep):
        here = pl.ds(pl.multiple_of(i * 2 * size, 2 * size), 2 * size)
        values, grads = b.v[:n, here], b.go[:n, here]
        first = lanes_of_first(n, size)
        got = []
        for j in range(2):
            own = jnp.where(first if j == 0 else jnp.logical_not(first), grads, jnp.zeros_like(grads))
            weight = b.att[2 * i + j, :n, :n]
            mixed = weight.astype(f32) * dot_back(own, values)
            keep(2 * i + j, j, mixed - weight.astype(f32) * jnp.sum(mixed, axis=-1, keepdims=True))
            got.append(dot_down(weight, grads))
        b.gv[:n, here] = jnp.where(first, got[0], got[1]).astype(bf16)

    if dense:

        def keep_dense(h, j, ds):
            b.gs[:n, pl.ds(pl.multiple_of(h * slots, slots), n)] = ds.astype(bf16)

        def loop(i, carry):
            pair_back(i, keep_dense)
            return carry

        lax.fori_loop(0, heads // 2, loop, 0)
    else:

        prior, result = random_copies(b, n if added else slots)

        def loop(i, carry):
            slot = lax.rem(i, 2)
            if added:

                @pl.when(i + 1 < heads // 2)
                def _():
                    prior(i + 1).start()

                prior(i).wait()

            @pl.when(i >= 2)
            def _():
                result(i - 2).wait()

            def keep_random(h, j, ds):
                if added:
                    ds = ds + b.random_old[slot, j, :n, :n].astype(f32)
                elif n < slots:
                    b.random_stage[slot, j] = jnp.zeros((slots, slots), bf16)
                b.random_stage[slot, j, :n, :n] = ds.astype(bf16)

            pair_back(i, keep_random)
            result(i).start()
            return carry

        lax.fori_loop(0, heads // 2, loop, 0)
        for i in (heads // 2 - 2, heads // 2 - 1):
            result(i).wait()
    b.need("x")
    if dense:

        def first_norm(at, carry):
            unit, _ = standard(b.x[at, :].astype(f32))
            b.a[at, :] = (unit * b.vector(FIRST_GAIN, whole) + b.vector(FIRST_SHIFT, whole)).astype(bf16)
            return carry

        by_rows(n, first_norm)
        b.emit(lambda t, s, write: write(dot_down(b.a[:n, cols_at(t)], b.gv[:n])))
    else:
        send_padded(b, n, gv=b.gv_out)
    if dense:
        b.need("p")

        def slopes(rows, at, t):
            value, slope = gelu_both(b.p[rows, at])
            b.s[rows, at] = value.astype(bf16)
            b.wide[rows, at] = slope

        by_cols(n, width, slopes)
        group = wide // slots

        def second_tile(t, s, write):
            tile = b.s[:n, cols_at(t)]
            if n == slots:
                write(dot_down(tile, b.gs[:n, pl.ds(pl.multiple_of(s * wide, wide), wide)]))
                return
            for q in range(group):
                left = pl.multiple_of(s * wide + q * slots, slots)
                write(dot_down(tile, b.gs[:n, pl.ds(left, n)]), pl.ds(q * slots, n))
                write(None, pl.ds(q * slots + n, slots - n))

        b.emit(second_tile)
        b.need("second")

        def hidden_back(rows, at, t):
            if n == slots:
                hidden = dot_back(b.gs[rows], b.up[at, :])
            else:
                hidden = jnp.zeros((rows.size, unit_cols), f32)
                for h in range(heads):
                    part = slice(h * slots, h * slots + n)
                    hidden = hidden + dot_back(b.gs[rows, part], b.up[at, part])
            gp = (b.wide[rows, at] * hidden).astype(bf16)
            b.gp[rows, at] = gp
            b.put_vector(SYNTH_BIAS, at, column_sum(gp))

        by_cols(n, width, hidden_back)
        b.emit(lambda t, s, write: write(dot_down(b.a[:n, cols_at(t)], b.gp[:n])))
    b.need("value", "first")

    def normed_back(rows, at, t):
        ga = dot_back(b.gv[rows], b.value[at, :])
        if dense:
            ga = ga + dot_back(b.gp[rows], b.first[at, :])
        b.wide[rows, at] = ga

    by_cols(n, width, normed_back)

    def first_back(at, carry):
        unit, inverse = standard(b.x[at, :].astype(f32))
        ga = b.wide[at, :]
        dx = b.gy[at, :] + standard_back(unit, inverse, ga * b.vector(FIRST_GAIN, whole))
        b.dx[at, :] = dx.astype(bf16)
        return carry[0] + column_sum(ga * unit), carry[1] + column_sum(ga)

    sums = by_rows(n, first_back, (none,) * 2)
    b.put_vector(FIRST_GAIN, whole, sums[0])
    b.put_vector(FIRST_SHIFT, whole, sums[1])
    if n < slots:
        b.dx[n:] = jnp.zeros((slots - n, width), bf16)
    if not dense:
        b.send(b.dx, b.dx_out)
    b.send(b.dx, b.grads_in.at[b.item])


def item_of(lengths, turn):
    if lengths.shape[0] == 2:
        return jnp.where(lengths[1] < lengths[0], 1 - turn, turn)
    return jnp.int32(turn)


def by_length(section, lengths, turn, slots, call):
    which = 1 + (lengths[item_of(lengths, turn)] > slots // 2).astype(jnp.int32)
    which = jnp.where(lax.axis_index(section_axis) == section, which, 0)
    return lax.switch(which, [functools.partial(call, n) for n in (0, slots // 2, slots)])


def in_item(b, shape, axis):
    return lax.broadcasted_iota(jnp.int32, shape, axis) < b.length


def shape_of(table):
    slots, width = table.x.shape
    return dict(width=width, ff=table.m.shape[1], heads=table.att.shape[0], slots=slots)


class ForwardRefs(NamedTuple):
    lengths: Any
    vectors: Any
    x_in: Any
    first_in: Any
    second_in: Any
    value_in: Any
    out_in: Any
    up_in: Any
    down_in: Any
    states: Any
    z_out: Any
    p_out: Any
    att_out: Any
    v_out: Any
    o_out: Any
    y_out: Any
    m_out: Any
    x: Any
    first: Any
    second: Any
    value: Any
    out: Any
    up: Any
    down: Any
    z: Any
    p: Any
    att: Any
    v: Any
    o: Any
    y: Any
    m: Any
    a: Any
    s: Any
    u: Any
    r: Any
    sems: Any


def dense_forward_kernel(n, turn, *refs):
    if n == 0:
        return
    refs = refs[:9] + refs[9 + (turn > 0) :]
    table = ForwardRefs(*refs)
    shape = shape_of(table)

    item = item_of(table.lengths, turn)
    b = Bench(item=item, length=table.lengths[item], **table._asdict(), **shape)
    rows = pl.ds(0, n)
    b.fetch("x", b.x_in.at[item, rows], b.x.at[rows])
    b.fetch("first", b.first_in, b.first)
    b.fetch("value", b.value_in, b.value)
    b.fetch("second", b.second_in, b.second)
    b.fetch("out", b.out_in, b.out)
    b.fetch("up", b.up_in, b.up)
    b.fetch("down", b.down_in, b.down)
    forward_part(b, n, True)
    b.finish()


class BackwardRefs(NamedTuple):
    lengths: Any
    vectors: Any
    x_in: Any
    c_in: Any
    p_in: Any
    att_in: Any
    v_in: Any
    o_in: Any
    y_in: Any
    m_in: Any
    first_in: Any
    second_in: Any
    value_in: Any
    out_in: Any
    up_in: Any
    down_in: Any
    grads_in: Any
    vector_grads: Any
    down_grad: Any
    up_grad: Any
    out_grad: Any
    value_grad: Any
    first_grad: Any
    second_grad: Any
    x: Any
    c: Any
    p: Any
    att: Any
    v: Any
    o: Any
    y: Any
    m: Any
    first: Any
    value: Any
    out: Any
    up: Any
    a: Any
    u: Any
    s: Any
    go: Any
    gv: Any
    gp: Any
    gb: Any
    gy: Any
    wide: Any
    dx: Any
    feed: Any
    stage: Any
    prior_stage: Any
    sems: Any
    stage_sems: Any
    prior_sems: Any


def dense_backward_kernel(n, turn, *refs):
    if n == 0:
        return
    refs = refs[:16] + refs[16 + (7 if turn > 0 else 5) :]
    table = BackwardRefs(*refs)
    shape = shape_of(table)
    ff, width = table.m.shape[1], table.x.shape[1]

    item = item_of(table.lengths, turn)
    b = Bench(item=item, length=table.lengths[item], **table._asdict(), **shape)
    b.gm, b.gs = b.feed.at[:, pl.ds(0, ff)], b.feed
    parts = width // unit_cols
    b.down_rows = lambda t: b.up[
        cols_at(lax.rem(t, parts)), pl.ds(pl.multiple_of(ff + t // parts * width, width), width)
    ]
    rows = pl.ds(0, n)
    b.fetch("c", b.c_in.at[rows], b.c.at[rows])
    b.fetch("m", b.m_in.at[rows], b.m.at[rows])
    for part in range(ff // width):
        b.fetch(f"down{part}", b.down_in.at[pl.ds(part * width, width)], b.up.at[:, pl.ds(ff + part * width, width)])
    b.fetch("up", b.up_in, b.up.at[:, pl.ds(0, ff)])
    b.fetch("y", b.y_in.at[rows], b.y.at[rows])
    b.fetch("o", b.o_in.at[rows], b.o.at[rows])
    b.fetch("out", b.out_in, b.out)
    b.fetch("v", b.v_in.at[rows], b.v.at[rows])
    b.fetch("att", b.att_in.at[:, rows, rows], b.att.at[:, rows, rows])
    b.fetch("x", b.x_in.at[item, rows], b.x.at[rows])
    b.fetch("p", b.p_in.at[rows], b.p.at[rows])
    b.fetch("value", b.value_in, b.value)
    b.fetch("first", b.first_in, b.first)
    plan_grads(b, True, turn > 0)
    b.need(*[f"down{part}" for part in range(ff // width)])
    backward_part(b, n, True, turn > 0)
    b.finish()


class RandomRefs(NamedTuple):
    lengths: Any
    vectors: Any
    x_in: Any
    c_in: Any
    att_in: Any
    value_in: Any
    out_in: Any
    up_in: Any
    down_in: Any
    states: Any
    grads_in: Any
    dx_out: Any
    vector_grads: Any
    random_grad: Any
    r_out: Any
    o_out: Any
    a_out: Any
    gm_out: Any
    u_out: Any
    gb_out: Any
    gv_out: Any
    c_out: Any
    x: Any
    c: Any
    att: Any
    v: Any
    o: Any
    y: Any
    m: Any
    value: Any
    out: Any
    up: Any
    down: Any
    a: Any
    u: Any
    go: Any
    gv: Any
    gb: Any
    gy: Any
    wide: Any
    z: Any
    dx: Any
    r: Any
    gm: Any
    random_stage: Any
    random_old: Any
    sems: Any
    random_sems: Any


def random_kernel(n, turn, *refs):
    if n == 0:
        return
    refs = refs[:9] + refs[9 + (3 if turn > 0 else 1) :]
    table = RandomRefs(*refs)
    shape = shape_of(table)

    item = item_of(table.lengths, turn)
    b = Bench(item=item, length=table.lengths[item], **table._asdict(), **shape)
    rows = pl.ds(0, n)
    b.fetch("x", b.x_in.at[rows], b.x.at[rows])
    b.fetch("value", b.value_in, b.value)
    b.fetch("att", b.att_in.at[:, rows, rows], b.att.at[:, rows, rows])
    b.fetch("out", b.out_in, b.out)
    b.fetch("up", b.up_in, b.up)
    b.fetch("down", b.down_in, b.down)
    b.down_rows = lambda t: b.down[cols_at(t), :]
    b.fetch("c", b.c_in.at[item, rows], b.c.at[rows])
    if turn > 0:
        random_copies(b, n)[0](0).start()
    forward_part(b, n, False)
    backward_part(b, n, False, turn > 0)
    b.finish()


class AttentionRefs(NamedTuple):
    lengths: Any
    logits_in: Any
    att_out: Any
    att: Any
    sems: Any


def random_attention_kernel(n, turn, *refs):
    if n == 0:
        return
    table = AttentionRefs(*refs)
    heads, slots, _ = table.att.shape
    b = Bench(length=table.lengths[item_of(table.lengths, turn)], slots=slots, **table._asdict())
    rows = pl.ds(0, n)
    half = heads // 2
    for k in (0, 1):
        part = pl.ds(k * half, half)
        b.fetch(k, b.logits_in.at[part, rows, rows], b.att.at[part, rows, rows])
    for k in (0, 1):
        b.need(k)

        def head(h, carry):
            b.att[h, :n, :n] = softmax(b, n, b.att[h, :n, :n].astype(f32))
            return carry

        lax.fori_loop(k * half, (k + 1) * half, head, 0)
        part = pl.ds(k * half, half)
        b.send(b.att.at[part, rows, rows], b.att_out.at[part, rows, rows])
    b.finish()


def random_attention(n, turn, lengths, logits):
    return pl.pallas_call(
        functools.partial(random_attention_kernel, n, turn),
        out_shape=S(logits.shape, bf16),
        in_specs=[scalars, anywhere],
        out_specs=anywhere,
        scratch_shapes=[] if n == 0 else [vmem(*logits.shape), pltpu.SemaphoreType.DMA((4,))],
        compiler_params=own_params(),
        name=f"random_attention_{n}",
    )(lengths, logits)


def weight_steps(kept, grads, c, r, o, a, gm, u, gb, gv, stage, sems, stage_sems):
    count = len(kept)
    slots = c.shape[0] // count
    b = Bench(stage=stage, sems=sems, stage_sems=stage_sems, width=c.shape[1])
    wide = 2 * b.width
    b.down_grad, b.up_grad, b.out_grad, b.value_grad = grads

    def need(*names):
        b.need(*[f"{name}{k}" for name in names for k in range(count)])

    def begin():
        for name, ref, at in (
            ("c", c, 7), ("r", r, 0), ("gm", gm, 3), ("u", u, 4), ("o", o, 1), ("gb", gb, 5), ("a", a, 2), ("gv", gv, 6),
        ):
            for k in range(count):
                b.fetch(f"{name}{k}", kept[k][at], ref.at[pl.ds(k * slots, slots)])
        plan_grads(b, False, False)

    def down():
        need("c", "r")
        b.emit(lambda t, s, write: write(dot_down(r[:, cols_at(t)], c[...])))

    def up():
        need("gm", "u")
        b.emit(lambda t, s, write: write(dot_down(u[:, cols_at(t)], gm[:, pl.ds(pl.multiple_of(s * wide, wide), wide)])))

    def rest():
        need("o", "gb")
        b.emit(lambda t, s, write: write(dot_down(o[:, cols_at(t)], gb[...])))
        need("a", "gv")
        b.emit(lambda t, s, write: write(dot_down(a[:, cols_at(t)], gv[...])))
        b.finish()

    return begin, down, up, rest


anywhere = pl.BlockSpec(memory_space=pl.ANY)
inside = pl.BlockSpec(memory_space=pltpu.VMEM)
scalars = pl.BlockSpec(memory_space=pltpu.SMEM)
S = jax.ShapeDtypeStruct


def vmem(*shape, dtype=bf16):
    return pltpu.VMEM(shape, dtype)


def own_params():
    return pltpu.CompilerParams(vmem_limit_bytes=63 << 20, has_side_effects=True)


def dense_forward(n, turn, lengths, vectors, inputs, weights, heads, states):
    _, slots, width = inputs.shape
    ff = weights["up"].shape[1]
    outs = (
        S(inputs.shape, bf16), S((slots, width), bf16), S((slots, width), f32), S((heads, slots, slots), bf16),
        S((slots, width), bf16), S((slots, width), bf16), S((slots, width), f32), S((slots, ff), bf16),
    )
    rows = vmem(slots, width)
    old = [] if states is None else [states]
    return pl.pallas_call(
        functools.partial(dense_forward_kernel, n, turn),
        out_shape=outs,
        in_specs=[scalars, inside] + [anywhere] * (7 + len(old)),
        out_specs=[anywhere] * 8,
        input_output_aliases={9: 0} if old else {},
        scratch_shapes=[] if n == 0 else [
            rows, vmem(width, width), vmem(width, heads * slots), vmem(width, width), vmem(width, width), vmem(width, ff),
            vmem(ff, width), rows, vmem(slots, width, dtype=f32), vmem(heads, slots, slots), rows, rows,
            vmem(slots, width, dtype=f32), vmem(slots, ff), rows, rows, rows, vmem(slots, ff), pltpu.SemaphoreType.DMA((20,)),
        ],
        compiler_params=own_params(),
        name=f"dense_forward_{n}",
    )(lengths, vectors, inputs, *[weights[k] for k in ("first", "second", "value", "out", "up", "down")], *old)


def dense_backward(n, turn, lengths, vectors, inputs, c, kept, weights, grads_in, old):
    p, att, v, o, y, m = kept
    heads = att.shape[0]
    _, slots, width = inputs.shape
    ff = weights["up"].shape[1]
    names = ("down", "up", "out", "value", "first", "second")
    outs = (S(inputs.shape, bf16), S(vectors.shape, f32)) + tuple(S(weights[name].shape, bf16) for name in names)
    rows = vmem(slots, width)
    square = vmem(width, width)
    aliases = {16: 0}
    aliases.update({17 + n: 2 + n for n in range(len(old))})
    return pl.pallas_call(
        functools.partial(dense_backward_kernel, n, turn),
        out_shape=outs,
        in_specs=[scalars, inside] + [anywhere] * (15 + len(old)),
        out_specs=[anywhere, inside] + [anywhere] * 6,
        input_output_aliases=aliases,
        scratch_shapes=[] if n == 0 else [
            rows, rows, vmem(slots, width, dtype=f32), vmem(heads, slots, slots), rows, rows,
            vmem(slots, width, dtype=f32), vmem(slots, ff), square, square, square, vmem(width, 2 * ff),
            rows, rows, rows, rows, rows, rows, rows, vmem(slots, width, dtype=f32), vmem(slots, width, dtype=f32), rows,
            vmem(slots, 2 * ff), vmem(tile_slots, unit_cols, 2 * width), vmem(tile_slots, unit_cols, 2 * width),
            pltpu.SemaphoreType.DMA((20,)), pltpu.SemaphoreType.DMA((tile_slots,)), pltpu.SemaphoreType.DMA((tile_slots,)),
        ],
        compiler_params=own_params(),
        name=f"dense_backward_{n}",
    )(
        lengths, vectors, inputs, c, p, att, v, o, y, m,
        *[weights[k] for k in ("first", "second", "value", "out", "up", "down")], grads_in, *old,
    )


def random_step(n, turn, lengths, vectors, x, cotangent, att, weights, states, old):
    heads, slots, _ = att.shape
    width = x.shape[1]
    ff = weights["up"].shape[1]
    narrow = S((slots, width), bf16)
    broad = S((slots, ff), bf16)
    outs = (
        S(cotangent.shape, bf16), S(cotangent.shape, bf16), narrow, S(vectors.shape, f32), S(att.shape, bf16),
        broad, narrow, narrow, broad, narrow, narrow, narrow, narrow,
    )
    rows = vmem(slots, width)
    square = vmem(width, width)
    deep = vmem(slots, width, dtype=f32)
    pair = vmem(2, 2, slots, slots)
    return pl.pallas_call(
        functools.partial(random_kernel, n, turn),
        out_shape=outs,
        in_specs=[scalars, inside] + [anywhere] * (8 + len(old)),
        out_specs=[anywhere] * 3 + [inside] + [anywhere] * 9,
        input_output_aliases={9: 0, 10: 1, 11: 4} if old else {9: 0},
        scratch_shapes=[] if n == 0 else [
            rows, rows, vmem(heads, slots, slots), rows, rows, deep, vmem(slots, ff), square, square,
            vmem(width, ff), vmem(ff, width), rows, rows, rows, rows, rows, deep, deep, rows, rows,
            vmem(slots, ff), vmem(slots, ff), pair, pair,
            pltpu.SemaphoreType.DMA((24,)), pltpu.SemaphoreType.DMA((2, 2)),
        ],
        compiler_params=own_params(),
        name=f"random_step_{n}",
    )(lengths, vectors, x, cotangent, att, *[weights[k] for k in ("value", "out", "up", "down")], states, *old)


def weight_scratch(count, slots, width, ff):
    tall = vmem(count * slots, width)
    broad = vmem(count * slots, ff)
    return [
        tall, broad, tall, tall, broad, tall, tall, tall, vmem(tile_slots, unit_cols, 2 * width),
        pltpu.SemaphoreType.DMA((8 * count,)), pltpu.SemaphoreType.DMA((tile_slots,)),
    ]


def weights_kernel(count, *refs):
    kept = [refs[8 * k : 8 * k + 8] for k in range(count)]

    @pl.when(lax.axis_index(section_axis) == 1)
    def _():
        for step in weight_steps(kept, refs[8 * count : 8 * count + 4], *refs[8 * count + 4 :]):
            step()


def random_weights(kept, weights):
    slots, width = kept[0][1].shape
    ff = kept[0][0].shape[1]
    names = ("down", "up", "out", "value")
    return pl.pallas_call(
        functools.partial(weights_kernel, len(kept)),
        out_shape=tuple(S(weights[name].shape, bf16) for name in names),
        in_specs=[anywhere] * (8 * len(kept)),
        out_specs=[anywhere] * 4,
        scratch_shapes=weight_scratch(len(kept), slots, width, ff),
        compiler_params=own_params(),
        name="random_weights",
    )(*[a for item in kept for a in item])


def deliver_kernel(arrays, random_in, small, *refs):
    ins, outs = refs[:arrays], refs[arrays + 1 : 2 * arrays + 1]
    random_ref = refs[arrays]
    vectors = refs[2 * arrays + 1 : 2 * arrays + 1 + vector_count]
    narrow, wide, sems, random_sems = refs[2 * arrays + 1 + vector_count :]
    slots, rows, _ = narrow.shape
    count = random_in.shape[0] // rows

    def part(n):
        return pl.ds(pl.multiple_of(n * rows, rows), rows)

    def load(n):
        slot = lax.rem(n, slots)
        return pltpu.make_async_copy(random_in.at[part(n)], narrow.at[slot], random_sems.at[0, slot])

    def store(n):
        slot = lax.rem(n, slots)
        return pltpu.make_async_copy(wide.at[slot], random_ref.at[part(n)], random_sems.at[1, slot])

    for n in range(slots - 1):
        load(n).start()
    copies = [pltpu.make_async_copy(a, b, sems.at[n]) for n, (a, b) in enumerate(zip(ins, outs))]
    for copy in copies:
        copy.start()
    for row, ref in enumerate(vectors):
        ref[...] = small[row : row + 1, : ref.shape[1]]

    def turn(n, carry):
        @pl.when(n + slots - 1 < count)
        def _():
            load(n + slots - 1).start()

        load(n).wait()

        @pl.when(n >= slots)
        def _():
            store(n - slots).wait()

        wide[lax.rem(n, slots)] = narrow[lax.rem(n, slots)].astype(f32)
        store(n).start()
        return carry

    lax.fori_loop(0, count, turn, 0)
    for n in range(count - slots, count):
        store(n).wait()
    for copy in copies:
        copy.wait()


def deliver(random, small, extents, arrays):
    rows, cols = random.shape
    slots = 4
    inside = pl.BlockSpec(memory_space=pltpu.VMEM)
    return pl.pallas_call(
        functools.partial(deliver_kernel, len(arrays)),
        out_shape=(S(random.shape, f32),)
        + tuple(S(a.shape, f32) for a in arrays)
        + tuple(S((1, extent), f32) for extent in extents),
        in_specs=[anywhere, inside] + [inside] * len(arrays),
        out_specs=[anywhere] * (1 + len(arrays)) + [inside] * len(extents),
        scratch_shapes=[
            vmem(slots, rows // 12, cols), vmem(slots, rows // 12, cols, dtype=f32),
            pltpu.SemaphoreType.DMA((len(arrays),)), pltpu.SemaphoreType.DMA((2, slots)),
        ],
        compiler_params=own_params(),
        name="deliver",
    )(random, small, *arrays)


def run_layers(inputs, cotangent, lengths, weights, vectors, logits, finish_random):
    count, slots, _ = inputs.shape
    heads = logits.shape[0]
    states = None
    firsts, seconds = [], []
    for turn in range(count):

        def forward(n):
            return dense_forward(n, turn, lengths, vectors, inputs, weights, heads, states)

        states, z, *kept = by_length(0, lengths, turn, slots, forward)
        firsts.append(kept)
        seconds.append(passed_along(z, section_axis, 1))
    atts = [
        by_length(1, lengths, turn, slots, lambda n: random_attention(n, turn, lengths, logits)) for turn in range(count)
    ]
    seconds[0], *atts = lax.optimization_barrier((seconds[0], *atts))
    old, backs, random_tables, random_kept = [], [], [], []
    for turn in range(count):

        def step(n):
            return random_step(n, turn, lengths, vectors, seconds[turn], cotangent, atts[turn], weights, states, old)

        states, grads_in, dx, table, random_grad, *kept = by_length(1, lengths, turn, slots, step)
        old = [grads_in, random_grad]
        backs.append(passed_along(dx, section_axis, -1))
        random_tables.append(table)
        random_kept.append(kept)
    random_grad, *grads = finish_random(random_grad, random_kept, weights)
    dense_tables = []
    for turn in range(count):

        def backward(n):
            return dense_backward(
                n, turn, lengths, vectors, inputs, backs[turn], firsts[turn], weights, grads_in, grads
            )

        grads_in, table, *grads = by_length(0, lengths, turn, slots, backward)
        dense_tables.append(table)
    grads = dict(zip(("down", "up", "out", "value", "first", "second"), grads))
    return states, grads_in, grads, random_grad, dense_tables, random_tables


def random_finish_kernel(dp, count, random_in, *refs):
    kept = [refs[8 * k : 8 * k + 8] for k in range(count)]
    refs = refs[8 * count :]
    random_ref, grads = refs[0], refs[1:5]
    (
        own, sib, ring, own_sems, sib_send, sib_recv, ring_send, ring_recv,
    ) = refs[5:13]
    begin, *meanwhile = weight_steps(kept, grads, *refs[13:])
    place = Place(dp)
    reach, chips = place.reach, place.chips
    block = random_in.shape[0] // (2 * chips)
    strip = block // 2
    away = (reach,) + tuple(o for t in range(reach - 1, 0, -1) for o in (t, -t)) + (0,)
    spot_of = {o: n for n, o in enumerate(away)}
    spot_of[-reach] = 0

    def part(ref, o, core):
        return ref.at[pl.ds(pl.multiple_of((core * chips + place.chip_at(o)) * block, block), block)]

    def load(o):
        return pltpu.make_async_copy(part(random_in, o, place.core), own.at[spot_of[o]], own_sems.at[spot_of[o]])

    def lend(o):
        at = spot_of[o]
        return remote(part(random_in, o, 1 - place.core), sib.at[at], sib_send.at[at], sib_recv.at[at], place.sibling())

    def carried(i, way, step):
        return step > 0 or i == way

    def ring_copy(i, way, step):
        turn = 1 if way == 0 else -1
        rows = pl.ds(i * strip, strip)
        return remote(
            own.at[spot_of[turn * (reach - step)], rows], ring.at[way, step, rows],
            ring_send.at[way, step, i], ring_recv.at[way, step, i], place.along(turn),
        )

    @pl.when(place.section == 1)
    def _():
        place.greet()
        for o in away:
            lend(o).start()
            load(o).start()
        begin()
        for step in range(reach + 1):
            for i in (0, 1):
                for way in (0, 1):
                    o = (reach - step) * (1 if way == 0 else -1)
                    if step < reach and not carried(i, way, step) or step == reach and way == 1:
                        continue
                    if i == 0:
                        load(o).wait()
                        lend(o).wait_recv()
                    rows = pl.ds(i * strip, strip)
                    terms = [own.at[spot_of[o], rows], sib.at[spot_of[o], rows]]
                    for back in (0, 1) if step == reach else (way,):
                        if step > 0 and carried(i, back, step - 1):
                            ring_copy(i, back, step - 1).wait_recv()
                            terms.append(ring.at[back, step - 1, rows])
                    store_sum(own.at[spot_of[o], rows], terms, strip)
                    if step < reach:
                        ring_copy(i, way, step).start()
            if meanwhile and step < reach:
                meanwhile.pop(0)()
        keep = pltpu.make_async_copy(own.at[spot_of[0]], random_ref, own_sems.at[chips])
        keep.start()
        for work in meanwhile:
            work()
        for o in away:
            lend(o).wait_send()
        keep.wait()
        for i in (0, 1):
            for way in (0, 1):
                for step in range(reach):
                    if carried(i, way, step):
                        ring_copy(i, way, step).wait_send()


def random_finish(dp, random, kept, weights):
    chips = dp // 2
    reach = chips // 2
    block = (random.shape[0] // dp, random.shape[1])
    slots, width = kept[0][1].shape
    ff = kept[0][0].shape[1]
    count = len(kept)
    dma = pltpu.SemaphoreType.DMA
    names = ("down", "up", "out", "value")
    return pl.pallas_call(
        functools.partial(random_finish_kernel, dp, count),
        out_shape=(S(block, random.dtype),) + tuple(S(weights[name].shape, bf16) for name in names),
        in_specs=[anywhere] * (1 + 8 * count),
        out_specs=[anywhere] * 5,
        scratch_shapes=[
            pltpu.VMEM((chips,) + block, random.dtype),
            pltpu.VMEM((chips,) + block, random.dtype),
            pltpu.VMEM((2, reach) + block, random.dtype),
            dma((chips + 1,)),
            dma((chips,)),
            dma((chips,)),
            dma((2, reach, 2)),
            dma((2, reach, 2)),
        ] + weight_scratch(count, slots, width, ff),
        compiler_params=pltpu.CompilerParams(
            collective_id=2, has_side_effects=True, vmem_limit_bytes=63 << 20
        ),
        name="random_finish",
    )(random, *[a for item in kept for a in item])


def passed_along(x, axis, by):
    size = lax.axis_size(axis)
    pairs = [(i, i + by) for i in range(size) if 0 <= i + by < size]
    return lax.ppermute(x, axis, pairs)


def table_of(vectors, ff):
    return jnp.stack([jnp.pad(v.astype(f32), (0, ff - v.shape[0])) for v in vectors])


def per_device(
    inputs,
    cotangent,
    lengths,
    first_gain,
    first_shift,
    value_weight,
    out_weight,
    out_bias,
    second_gain,
    second_shift,
    up_weight,
    up_bias,
    down_weight,
    down_bias,
    synth_first,
    synth_bias,
    synth_second,
    random_logits,
):
    dp = lax.axis_size(dp_axis)
    is_dense = lax.axis_index(section_axis) == 0
    value_share, out_share, up_share, down_share = value_weight[0], out_weight[0], up_weight[0], down_weight[0]
    ff = up_share.shape[1]
    shares = [
        a.reshape(1, -1)
        for a in (first_gain, first_shift, out_bias, second_gain, second_shift, down_bias, up_bias, synth_bias)
    ]
    extents = tuple(a.shape[1] for a in shares)
    ringed = (
        dp % 4 == 0 and dp > 4 and value_share.shape[0] % 16 == 0 and synth_first.shape[0] % 8 == 0
        and max(extents) <= small_block[1]
    )
    if ringed:
        value, out, up, down, first, second, table = gather_weights(
            dp, value_share, out_share, up_share, down_share, synth_first, synth_second, shares
        )
    else:
        value, out, up, down = (
            lax.all_gather(a, dp_axis, axis=0, tiled=True) for a in (value_share, out_share, up_share, down_share)
        )
        first, second = (lax.all_gather(a, (section_axis, dp_axis), axis=0, tiled=True) for a in (synth_first, synth_second))
        axes = [dp_axis] * synth_row + [(section_axis, dp_axis)]
        table = table_of([lax.all_gather(a[0], axis, axis=0, tiled=True) for a, axis in zip(shares, axes)], ff)
    weights = dict(value=value, out=out, up=up, down=down, first=first, second=second)

    def finish_random(grad, kept, of):
        flat = grad.reshape(-1, grad.shape[-1])
        return random_finish(dp, flat, kept, of) if ringed else (flat, *random_weights(kept, of))

    states, grads_in, grads, random_grad, dense_tables, random_tables = run_layers(
        inputs, cotangent, lengths, weights, table, random_logits, finish_random
    )
    arrays = [grads[name] for name in ("value", "out", "up", "down", "first", "second")]
    if ringed:
        g_value, g_out, g_up, g_down, small, g_first, g_second, random_grad = reduce_grads(
            dp, *arrays, random_grad, dense_tables, random_tables, extents
        )
        random_total, g_value, g_out, g_up, g_down, g_first, g_second, *g_vectors = deliver(
            random_grad, small, extents, (g_value, g_out, g_up, g_down, g_first, g_second)
        )
        g_vectors = [v.reshape(-1) for v in g_vectors]
    else:
        g_value, g_out, g_up, g_down = (
            lax.psum_scatter(a, dp_axis, scatter_dimension=0, tiled=True).astype(f32) for a in arrays[:4]
        )
        g_first, g_second = (
            lax.psum_scatter(jnp.where(is_dense, a, jnp.zeros_like(a)), (section_axis, dp_axis), scatter_dimension=0, tiled=True).astype(f32)
            for a in arrays[4:]
        )
        grad_table = jnp.where(is_dense, sum(dense_tables), sum(random_tables))
        g_vectors = [
            lax.psum_scatter(grad_table[row, : dp * extents[row]], dp_axis, scatter_dimension=0, tiled=True)
            for row in range(synth_row)
        ]
        synth_grad = jnp.where(is_dense, grad_table[synth_row, : 2 * dp * extents[synth_row]], 0.0)
        g_vectors.append(lax.psum_scatter(synth_grad, (section_axis, dp_axis), scatter_dimension=0, tiled=True))
        random_total = lax.psum(jnp.where(is_dense, jnp.zeros_like(random_grad), random_grad), (section_axis, dp_axis)).astype(f32)
    random_total = random_total.reshape(random_logits.shape)
    return (
        states[None],
        grads_in[None],
        g_vectors[FIRST_GAIN][None],
        g_vectors[FIRST_SHIFT][None],
        g_value[None],
        g_out[None],
        g_vectors[OUT_BIAS][None],
        g_vectors[SECOND_GAIN][None],
        g_vectors[SECOND_SHIFT][None],
        g_up[None],
        g_vectors[UP_BIAS][None],
        g_down[None],
        g_vectors[DOWN_BIAS][None],
        g_first,
        g_vectors[SYNTH_BIAS],
        g_second,
        random_total,
    )


def solution(mesh):
    in_specs = (
        P(dp_axis, None, None),
        P(dp_axis, None, None),
        P(dp_axis),
        P(section_axis, dp_axis),
        P(section_axis, dp_axis),
        P(section_axis, dp_axis, None),
        P(section_axis, dp_axis, None),
        P(section_axis, dp_axis),
        P(section_axis, dp_axis),
        P(section_axis, dp_axis),
        P(section_axis, dp_axis, None),
        P(section_axis, dp_axis),
        P(section_axis, dp_axis, None),
        P(section_axis, dp_axis),
        P((section_axis, dp_axis), None),
        P((section_axis, dp_axis)),
        P((section_axis, dp_axis), None),
        P(),
    )
    out_specs = (
        P(section_axis, dp_axis, None, None),
        P(section_axis, dp_axis, None, None),
        P(section_axis, dp_axis),
        P(section_axis, dp_axis),
        P(section_axis, dp_axis, None),
        P(section_axis, dp_axis, None),
        P(section_axis, dp_axis),
        P(section_axis, dp_axis),
        P(section_axis, dp_axis),
        P(section_axis, dp_axis, None),
        P(section_axis, dp_axis),
        P(section_axis, dp_axis, None),
        P(section_axis, dp_axis),
        P((section_axis, dp_axis), None),
        P((section_axis, dp_axis)),
        P((section_axis, dp_axis), None),
        P(),
    )
    return jax.shard_map(
        per_device, mesh=mesh, in_specs=in_specs, out_specs=out_specs, check_vma=False
    )
```

```python
import functools
from typing import Any, NamedTuple

import jax
import jax.numpy as jnp
from jax import lax
from jax.experimental import pallas as pl
from jax.experimental.pallas import tpu as pltpu
from jax.sharding import PartitionSpec as P

MESH = pl.DeviceIdType.MESH


class Place:
    def __init__(self, dp):
        self.chips = dp // 2
        self.reach = self.chips // 2
        self.section = lax.axis_index(section_axis)
        index = lax.axis_index(dp_axis)
        self.core = lax.rem(index, 2)
        self.chip = index // 2
        column = lax.rem(self.chip, 2)
        row = self.chip // 2
        self.position = row + column * (self.chips - 1 - 2 * row)

    def chip_at(self, steps):
        spot = lax.rem(self.position + steps + 2 * self.chips, self.chips)
        column = spot // self.reach
        row = spot + column * (self.chips - 1 - 2 * spot)
        return 2 * row + column

    def along(self, steps):
        return (self.section, 2 * self.chip_at(steps) + self.core)

    def sibling(self):
        return (self.section, 2 * self.chip + 1 - self.core)

    def across(self):
        return (1 - self.section, 2 * self.chip + self.core)

    def greet_late(self, early):
        barrier = pltpu.get_barrier_semaphore()
        near = (self.along(1), self.along(-1), self.sibling())
        for other in near:
            pl.semaphore_signal(barrier, inc=1, device_id=other, device_id_type=MESH)

        @pl.when(early)
        def _():
            pl.semaphore_wait(barrier, len(near))
            pl.semaphore_signal(barrier, inc=1, device_id=self.across(), device_id_type=MESH)

        @pl.when(jnp.logical_not(early))
        def _():
            pl.semaphore_wait(barrier, len(near) + 1)
            pl.semaphore_signal(barrier, inc=1, device_id=self.across(), device_id_type=MESH)

    def greet(self, *others):
        barrier = pltpu.get_barrier_semaphore()
        others = (self.along(1), self.along(-1), self.sibling()) + others
        for other in others:
            pl.semaphore_signal(barrier, inc=1, device_id=other, device_id_type=MESH)
        pl.semaphore_wait(barrier, len(others))


def remote(src, dst, send_sem, recv_sem, device):
    return pltpu.make_async_remote_copy(
        src_ref=src, dst_ref=dst, send_sem=send_sem, recv_sem=recv_sem,
        device_id=device, device_id_type=MESH,
    )


def hint(value, unit):
    return pl.multiple_of(value, unit)


PIECES = (
    ("second_a", 0, True),
    ("second_b", 1, True),
    ("first", 0, True),
    ("value", 0, False),
    ("out", 1, False),
    ("up", 0, False),
    ("down", 1, False),
    ("small", 0, True),
)
(FIRST_GAIN, FIRST_SHIFT, OUT_BIAS, SECOND_GAIN, SECOND_SHIFT, DOWN_BIAS, UP_BIAS, SYNTH_BIAS) = range(8)
vector_count = 8
up_row, synth_row = UP_BIAS, SYNTH_BIAS
section_axis, dp_axis = "section", "dp"
small_block = (8, 256)


def piece_view(refs, name, chip, core, section, sizes):
    rows, ff_rows, dense_rows, dense_cols, second_cols, chips = sizes
    who = 2 * chip + core
    if name in ("value", "out", "up"):
        return refs[name].at[pl.ds(hint(who * rows, rows), rows)]
    if name == "down":
        return refs[name].at[pl.ds(hint(who * ff_rows, ff_rows), ff_rows)]
    if name == "small":
        return refs[name].at[section, who]
    top = hint((section * chips + chip) * dense_rows, dense_rows)
    if name == "first":
        return refs[name].at[pl.ds(top, dense_rows), pl.ds(hint(core * dense_cols, dense_cols), dense_cols)]
    half = second_cols // 2
    left = core * second_cols + (half if name == "second_b" else 0)
    return refs["second"].at[pl.ds(top, dense_rows), pl.ds(hint(left, half), half)]


def gather_kernel(
    dp, sizes,
    value_in, out_in, up_in, down_in, first_in, second_in, *rest,
):
    vectors = rest[: vector_count]
    (
        value_ref, out_ref, up_ref, down_ref, first_ref, second_ref, table_ref,
        small_in, small_ref, first_wide, second_wide, first_stage, second_stage, wide_sems,         own_sems, ring_send, ring_recv, sib_send, sib_recv, across_send, across_recv, pass_send, pass_recv,
    ) = rest[vector_count :]
    rows, ff_rows, dense_rows, dense_cols, second_cols, chips = sizes
    place = Place(dp)
    reach = place.reach
    quarter = dense_rows // 2
    refs = dict(value=value_ref, out=out_ref, up=up_ref, down=down_ref, small=small_ref, first=first_ref, second=second_ref)
    half = second_cols // 2
    sources = dict(
        value=value_in, out=out_in, up=up_in, down=down_in, small=small_in, first=first_stage,
        second_a=second_stage.at[:, pl.ds(0, half)], second_b=second_stage.at[:, pl.ds(half, half)],
    )
    order = tuple(range(len(PIECES)))
    dense = tuple(i for i in order if PIECES[i][2])
    plain = tuple(i for i in order if not PIECES[i][2])

    def view(i, steps, section):
        return piece_view(refs, PIECES[i][0], place.chip_at(steps), place.core, section, sizes)

    def carried(i, way, step):
        return step < reach - 1 or (step == reach - 1 and PIECES[i][1] == way)

    def ring_copy(i, way, step):
        turn = 1 if way == 0 else -1
        target = view(i, -turn * step, place.section)
        source = sources[PIECES[i][0]] if step == 0 else target
        return remote(source, target, ring_send.at[way, step, i], ring_recv.at[way, step, i], place.along(turn))

    def slot(way, step):
        return 0 if step < 0 else 1 + 2 * step + way

    def sibling_copy(i, way, step):
        turn = 1 if way == 0 else -1
        target = view(i, -turn * (step + 1) if step >= 0 else 0, place.section)
        source = sources[PIECES[i][0]] if step < 0 else target
        at = slot(way, step)
        return remote(source, target, sib_send.at[at, i], sib_recv.at[at, i], place.sibling())

    def across_copy(i, way, step):
        turn = 1 if way == 0 else -1
        target = view(i, -turn * (step + 1) if step >= 0 else 0, place.section)
        source = sources[PIECES[i][0]] if step < 0 else target
        at = slot(way, step)
        return remote(source, target, across_send.at[at, i], across_recv.at[at, i], place.across())

    def pass_copy(i, way, step):
        turn = 1 if way == 0 else -1
        target = view(i, -turn * (step + 1) if step >= 0 else 0, 1 - place.section)
        at = slot(way, step)
        return remote(target, target, pass_send.at[at, i], pass_recv.at[at, i], place.sibling())

    def own_copy(i):
        return pltpu.make_async_copy(sources[PIECES[i][0]], view(i, 0, place.section), own_sems.at[i])

    def begin(i):
        for way in (0, 1):
            if carried(i, way, 0):
                ring_copy(i, way, 0).start()
        sibling_copy(i, 0, -1).start()
        if PIECES[i][2]:
            across_copy(i, 0, -1).start()
        own_copy(i).start()

    small_in[...] = jnp.zeros(small_block, jnp.float32)
    for row, ref in enumerate(vectors):
        small_in[row : row + 1, : ref.shape[1]] = ref[...].astype(jnp.float32)
    mine = hint(place.core * quarter, 8)
    first_wide[pl.ds(mine, quarter)] = first_in[...].astype(jnp.float32)
    second_wide[pl.ds(mine, quarter)] = second_in[...].astype(jnp.float32)
    place.greet(place.across())
    wide = [
        remote(ref.at[pl.ds(mine, quarter)], ref.at[pl.ds(mine, quarter)], wide_sems.at[0, n], wide_sems.at[1, n], place.sibling())
        for n, ref in enumerate((first_wide, second_wide))
    ]
    for copy in wide:
        copy.start()
    early = plain[:2]
    for i in early:
        begin(i)
    for copy in wide:
        copy.wait()
    first_stage[...] = first_wide[:, pl.ds(hint(place.core * dense_cols, dense_cols), dense_cols)].astype(jnp.bfloat16)
    second_stage[...] = second_wide[:, pl.ds(hint(place.core * second_cols, second_cols), second_cols)].astype(jnp.bfloat16)
    for i in dense + plain[len(early) :]:
        begin(i)

    events = [(i, way, step) for step in range(reach) for i in order for way in (0, 1) if carried(i, way, step)]
    crossing = [(i, 0, -1) for i in dense] + [e for e in events if e[0] in dense]
    passed = 0

    def pass_on(count):
        nonlocal passed
        while passed < min(count, len(crossing)):
            e = crossing[passed]
            across_copy(*e).wait_recv()
            pass_copy(*e).start()
            passed += 1

    for i, way, step in events:
        ring_copy(i, way, step).wait_recv()
        if carried(i, way, step + 1):
            ring_copy(i, way, step + 1).start()
        sibling_copy(i, way, step).start()
        if i in dense:
            across_copy(i, way, step).start()
        if i == order[-1] and way == 0:
            pass_on(len(dense) + 2 * len(dense) * step)
    pass_on(len(crossing))
    for i in order:
        own_copy(i).wait()
        sibling_copy(i, 0, -1).wait()
        for way in (0, 1):
            if carried(i, way, 0):
                ring_copy(i, way, 0).wait_send()
    for i, way, step in events:
        sibling_copy(i, way, step).wait()
        if step > 0:
            ring_copy(i, way, step).wait_send()
    for e in crossing:
        across_copy(*e).wait_send()
        pass_copy(*e).wait()
    shares = [ref.shape[1] for ref in vectors]
    share = shares[0]

    def side_by_side(blocks):
        return jnp.concatenate(blocks, axis=1)

    table_ref[:up_row, : dp * share] = side_by_side([small_ref[place.section, d, :up_row, :share] for d in range(dp)])
    up_share = shares[up_row]
    table_ref[up_row : up_row + 1, :] = side_by_side(
        [small_ref[place.section, d, up_row : up_row + 1, :up_share] for d in range(dp)]
    )
    synth_share = shares[synth_row]
    table_ref[synth_row : synth_row + 1, : 2 * dp * synth_share] = side_by_side(
        [small_ref[s, d, synth_row : synth_row + 1, :synth_share] for s in range(2) for d in range(dp)]
    )


def gather_weights(dp, value, out, up, down, first, second, vectors):
    rows, width = value.shape
    ff_rows = down.shape[0]
    ff = up.shape[1]
    chips = dp // 2
    dense_rows = 2 * first.shape[0]
    dense_cols = first.shape[1] // 2
    second_cols = second.shape[1] // 2
    sizes = (rows, ff_rows, dense_rows, dense_cols, second_cols, chips)
    reach = chips // 2
    count = len(PIECES)
    bf = jnp.bfloat16
    anywhere = pl.BlockSpec(memory_space=pl.ANY)
    inside = pl.BlockSpec(memory_space=pltpu.VMEM)
    dma = pltpu.SemaphoreType.DMA
    return pl.pallas_call(
        functools.partial(gather_kernel, dp, sizes),
        out_shape=(
            jax.ShapeDtypeStruct((rows * dp, width), bf),
            jax.ShapeDtypeStruct((rows * dp, width), bf),
            jax.ShapeDtypeStruct((rows * dp, ff), bf),
            jax.ShapeDtypeStruct((ff_rows * dp, width), bf),
            jax.ShapeDtypeStruct((2 * dp * first.shape[0], first.shape[1]), bf),
            jax.ShapeDtypeStruct((2 * dp * second.shape[0], second.shape[1]), bf),
            jax.ShapeDtypeStruct((vector_count, ff), jnp.float32),
        ),
        in_specs=[anywhere] * 4 + [inside] * (2 + len(vectors)),
        out_specs=[anywhere] * 6 + [inside],
        scratch_shapes=[
            pltpu.VMEM(small_block, jnp.float32),
            pltpu.VMEM((2, dp) + small_block, jnp.float32),
            pltpu.VMEM((dense_rows, 2 * dense_cols), jnp.float32),
            pltpu.VMEM((dense_rows, 2 * second_cols), jnp.float32),
            pltpu.VMEM((dense_rows, dense_cols), bf),
            pltpu.VMEM((dense_rows, second_cols), bf),
            dma((2, 2)),
            dma((count,)),
            dma((2, reach, count)),
            dma((2, reach, count)),
            dma((1 + 2 * reach, count)),
            dma((1 + 2 * reach, count)),
            dma((1 + 2 * reach, count)),
            dma((1 + 2 * reach, count)),
            dma((1 + 2 * reach, count)),
            dma((1 + 2 * reach, count)),
        ],
        compiler_params=pltpu.CompilerParams(
            collective_id=0, has_side_effects=True, vmem_limit_bytes=63 << 20
        ),
        name="gather_weights",
    )(value, out, up, down, first, second, *vectors)


def store_sum(target, terms, rows):
    if rows == 0:
        total = terms[0][...]
        for term in terms[1:]:
            total = total + term[...]
        target[...] = total
        return

    def some(n, carry):
        at = pl.ds(pl.multiple_of(n * 16, 16), 16)
        total = terms[0][at, :].astype(jnp.float32)
        for term in terms[1:]:
            total = total + term[at, :].astype(jnp.float32)
        target[at, :] = total.astype(target.dtype)
        return carry

    lax.fori_loop(0, rows // 16, some, 0)


def reduce_kernel(dp, sizes, shares, tables, value_in, out_in, up_in, down_in, first_in, second_in, random_in, *rest):
    dense_tables, random_tables = rest[:tables], rest[tables : 2 * tables]
    (
    value_ref, out_ref, up_ref, down_ref, small_ref, first_ref, second_ref, random_ref,
    small_in, own_value, own_out, own_up, own_down, own_small, own_first, own_second,
    sib_value, sib_out, sib_up, sib_down, sib_small, sib_first, sib_second,
    ring_value, ring_out, ring_up, ring_down, ring_small, ring_first, ring_second,
    across_small, across_first, across_second, first_wide, second_wide, first_part, second_part,
    own_sems, sib_send, sib_recv, ring_send, ring_recv, across_send, across_recv, wide_sems,
    random_sems, turn_send, turn_recv, pass_send, pass_recv,
    ) = rest[2 * tables :]
    rows, ff_rows, dense_rows, dense_cols, second_cols, chips = sizes
    place = Place(dp)
    reach = place.reach
    half = second_cols // 2
    quarter = dense_rows // 2
    is_dense = place.section == 0
    full = dict(value=value_in, out=out_in, up=up_in, down=down_in, small=small_in, first=first_in, second=second_in)
    own = dict(value=own_value, out=own_out, up=own_up, down=own_down, small=own_small, first=own_first, second=own_second)
    sib = dict(value=sib_value, out=sib_out, up=sib_up, down=sib_down, small=sib_small, first=sib_first, second=sib_second)
    ring = dict(value=ring_value, out=ring_out, up=ring_up, down=ring_down, small=ring_small, first=ring_first, second=ring_second)
    crossed = dict(first=across_first, second=across_second, small=across_small)
    order = tuple(range(len(PIECES)))
    small = len(PIECES) - 1
    crossing = tuple(i for i in order if PIECES[i][2])
    dense = crossing[:-1]
    plain = tuple(i for i in order if not PIECES[i][2])
    piece_rows = dict(value=rows, out=rows, up=rows, down=ff_rows, small=0, first=dense_rows, second_a=dense_rows, second_b=dense_rows)
    away = (reach,) + tuple(o for t in range(reach - 1, 0, -1) for o in (t, -t)) + (0,)
    spot_of = {o: n for n, o in enumerate(away)}
    spot_of[-reach] = 0

    def part(table, i, *at):
        name = PIECES[i][0]
        if name == "second_a":
            return table["second"].at[(*at, slice(None), pl.ds(0, half))]
        if name == "second_b":
            return table["second"].at[(*at, slice(None), pl.ds(half, half))]
        return table[name].at[at]

    def held(table, i, o, plane):
        spot = spot_of[o]
        return part(table, i, plane, spot) if PIECES[i][2] else part(table, i, spot)

    def source(i, o, core, plane):
        section = place.section if plane == 0 else 1 - place.section
        return piece_view(full, PIECES[i][0], place.chip_at(o), core, section, sizes)

    def load(i, o, plane):
        return pltpu.make_async_copy(
            source(i, o, place.core, plane), held(own, i, o, plane), own_sems.at[plane, spot_of[o], i]
        )

    def lend(i, o, plane):
        at = (plane, spot_of[o], i)
        return remote(source(i, o, 1 - place.core, plane), held(sib, i, o, plane), sib_send.at[at], sib_recv.at[at], place.sibling())

    def ring_copy(i, way, step):
        turn = 1 if way == 0 else -1
        o = turn * (reach - step)
        return remote(held(own, i, o, 0), part(ring, i, way, step), ring_send.at[way, step, i], ring_recv.at[way, step, i], place.along(turn))

    def across_copy(i, o):
        at = (spot_of[o], i)
        return remote(held(own, i, o, 1), part(crossed, i, spot_of[o]), across_send.at[at], across_recv.at[at], place.across())

    def carried(i, way, step):
        return step > 0 or PIECES[i][1] == way

    def local_terms(i, o):
        load(i, o, 0).wait()
        lend(i, o, 0).wait_recv()
        return [held(own, i, o, 0), held(sib, i, o, 0)]

    def total(target, i, o, arrived):
        if i == small:
            terms = local_terms(i, o) + arrived

            @pl.when(is_dense)
            def _():
                store_sum(target, terms, 0)

            @pl.when(jnp.logical_not(is_dense))
            def _():
                across_copy(i, o).wait_recv()
                store_sum(target, terms + [part(crossed, i, spot_of[o])], 0)
        elif PIECES[i][2]:

            @pl.when(is_dense)
            def _():
                store_sum(target, local_terms(i, o) + arrived, piece_rows[PIECES[i][0]])

            @pl.when(jnp.logical_not(is_dense))
            def _():
                across_copy(i, o).wait_recv()
                store_sum(target, [part(crossed, i, spot_of[o])] + arrived, piece_rows[PIECES[i][0]])
        else:
            store_sum(target, local_terms(i, o) + arrived, piece_rows[PIECES[i][0]])

    def arrivals(i, o):
        ways = (0, 1) if o == 0 else ((0,) if o > 0 else (1,))
        found = []
        for way in ways:
            step = reach - abs(o) - 1
            if step >= 0 and carried(i, way, step):
                ring_copy(i, way, step).wait_recv()
                found.append(part(ring, i, way, step))
        return found

    small_in[...] = jnp.zeros(small_in.shape, jnp.float32)

    def blocks_of(got, section, names):
        whole = got[0][...]
        for more in got[1:]:
            whole = whole + more[...]
        for d in range(dp):
            if names:
                share = shares[0]
                small_in[section, d, :up_row, :share] = whole[:up_row, d * share : (d + 1) * share]
                share = shares[up_row]
                small_in[section, d, up_row : up_row + 1, :share] = whole[up_row : up_row + 1, d * share : (d + 1) * share]
            if got is dense_tables:
                share = shares[synth_row]
                left = (section * dp + d) * share
                small_in[section, d, synth_row : synth_row + 1, :share] = whole[synth_row : synth_row + 1, left : left + share]

    @pl.when(is_dense)
    def _():
        blocks_of(dense_tables, 0, True)
        blocks_of(dense_tables, 1, False)

    @pl.when(jnp.logical_not(is_dense))
    def _():
        blocks_of(random_tables, 1, True)

    place.greet_late(jnp.logical_not(is_dense))
    for o in away:
        for i in plain + (small,):
            lend(i, o, 0).start()
            load(i, o, 0).start()

        @pl.when(is_dense)
        def _():
            for plane in (1, 0):
                for i in dense + ((small,) if plane == 1 else ()):
                    lend(i, o, plane).start()
                    load(i, o, plane).start()

    block = random_ref.shape[0] // (2 * chips)
    strip = block // 2

    def view(i, o, core):
        top = (core * chips + place.chip_at(o)) * block + i * strip
        return random_ref.at[pl.ds(pl.multiple_of(top, strip), strip)]

    def spread(i, way, step):
        return step < reach - 1 or i == way

    def turn_copy(i, way, step):
        turn = 1 if way == 0 else -1
        target = view(i, -turn * step, place.core)
        source = random_in.at[pl.ds(i * strip, strip)] if step == 0 else target
        return remote(source, target, turn_send.at[way, step, i], turn_recv.at[way, step, i], place.along(turn))

    def pass_copy(i, way, step):
        turn = 1 if way == 0 else -1
        target = view(i, -turn * (step + 1) if step >= 0 else 0, place.core)
        source = random_in.at[pl.ds(i * strip, strip)] if step < 0 else target
        at = 0 if step < 0 else 1 + 2 * step + way
        return remote(source, target, pass_send.at[at, i], pass_recv.at[at, i], place.sibling())

    def keep_copy(i):
        return pltpu.make_async_copy(random_in.at[pl.ds(i * strip, strip)], view(i, 0, place.core), random_sems.at[1, 1, i])

    def across_strip(o, device, way):
        top = pl.multiple_of((place.core * chips + place.chip_at(o)) * block, block)
        part_of = random_ref.at[pl.ds(top, block)]
        return remote(part_of, part_of, random_sems.at[way, 0, 2 + spot_of[o]], random_sems.at[way, 1, 2 + spot_of[o]], device)

    events = [(i, way, step) for step in range(reach) for i in (0, 1) for way in (0, 1) if spread(i, way, step)]

    @pl.when(jnp.logical_not(is_dense))
    def _():
        for i in (0, 1):
            for way in (0, 1):
                if spread(i, way, 0):
                    turn_copy(i, way, 0).start()
            pass_copy(i, 0, -1).start()
            keep_copy(i).start()
        for i, way, step in events:
            turn_copy(i, way, step).wait_recv()
            if step + 1 < reach and spread(i, way, step + 1):
                turn_copy(i, way, step + 1).start()
            pass_copy(i, way, step).start()
        for i in (0, 1):
            keep_copy(i).wait()
        pl.semaphore_wait(pltpu.get_barrier_semaphore(), 1)
        for o in away:
            across_strip(o, place.across(), 0).start()

    def cross(o):
        @pl.when(is_dense)
        def _():
            for i in crossing:
                load(i, o, 1).wait()
                lend(i, o, 1).wait_recv()
                store_sum(held(own, i, o, 1), [held(own, i, o, 1), held(sib, i, o, 1)], piece_rows[PIECES[i][0]])
                across_copy(i, o).start()

    for step in range(reach):
        for i in plain + crossing:
            for way in (0, 1):
                if carried(i, way, step):
                    o = (reach - step) * (1 if way == 0 else -1)
                    total(held(own, i, o, 0), i, o, arrivals(i, o))
                    ring_copy(i, way, step).start()
            if i == plain[-1]:
                for o in away[(0 if step == 0 else 2 * step - 1) : 2 * step + 1]:
                    cross(o)
    cross(0)

    @pl.when(is_dense)
    def _():
        for o in away:
            across_strip(o, place.across(), 0).wait_recv()
            across_strip(o, place.sibling(), 1).start()

    outs = dict(value=value_ref, out=out_ref, up=up_ref, down=down_ref, small=small_ref)
    for i in plain + (small,):
        total(outs[PIECES[i][0]], i, 0, arrivals(i, 0))
    wides = dict(first=first_wide, second_a=second_wide.at[:, pl.ds(0, half)], second_b=second_wide.at[:, pl.ds(half, half)])
    for i in dense:
        total(wides[PIECES[i][0]], i, 0, arrivals(i, 0))
    mine = pl.multiple_of(place.core * quarter, 8)
    theirs = pl.multiple_of((1 - place.core) * quarter, 8)
    last = [
        remote(wide.at[pl.ds(theirs, quarter)], got, wide_sems.at[0, n], wide_sems.at[1, n], place.sibling())
        for n, (wide, got) in enumerate(((first_wide, first_part), (second_wide, second_part)))
    ]
    for copy in last:
        copy.start()
    for copy in last:
        copy.wait()
    for ref, wide, got, cols in ((first_ref, first_wide, first_part, dense_cols), (second_ref, second_wide, second_part, second_cols)):
        ref[:, pl.ds(pl.multiple_of(place.core * cols, cols), cols)] = wide[pl.ds(mine, quarter), :]
        ref[:, pl.ds(pl.multiple_of((1 - place.core) * cols, cols), cols)] = got[...]

    for o in away:
        for i in plain + (small,):
            lend(i, o, 0).wait_send()

        @pl.when(is_dense)
        def _():
            for i in dense:
                lend(i, o, 0).wait_send()
            for i in crossing:
                lend(i, o, 1).wait_send()
                across_copy(i, o).wait_send()

    @pl.when(is_dense)
    def _():
        for o in away:
            across_strip(o, place.sibling(), 1).wait()

    @pl.when(jnp.logical_not(is_dense))
    def _():
        for o in away:
            across_strip(o, place.across(), 0).wait_send()
        for i in (0, 1):
            pass_copy(i, 0, -1).wait()
            for way in (0, 1):
                for step in range(reach):
                    if spread(i, way, step):
                        turn_copy(i, way, step).wait_send()
        for e in events:
            pass_copy(*e).wait()

    for step in range(reach):
        for i in order:
            for way in (0, 1):
                if carried(i, way, step):
                    ring_copy(i, way, step).wait_send()


def reduce_grads(dp, value, out, up, down, first, second, random, dense_tables, random_tables, shares):
    chips = dp // 2
    rows, width = value.shape[0] // dp, value.shape[1]
    ff_rows = down.shape[0] // dp
    ff = up.shape[1]
    dense_rows = first.shape[0] // dp
    dense_cols = first.shape[1] // 2
    second_cols = second.shape[1] // 2
    sizes = (rows, ff_rows, dense_rows, dense_cols, second_cols, chips)
    reach = chips // 2
    count = len(PIECES)
    bf, f32 = jnp.bfloat16, jnp.float32
    anywhere = pl.BlockSpec(memory_space=pl.ANY)
    inside = pl.BlockSpec(memory_space=pltpu.VMEM)
    dma = pltpu.SemaphoreType.DMA
    blocks = ((rows, width), (rows, width), (rows, ff), (ff_rows, width))
    wide = ((dense_rows, dense_cols), (dense_rows, second_cols))
    scratch = [pltpu.VMEM((2, dp) + small_block, f32)]
    for _ in range(2):
        scratch += [pltpu.VMEM((chips,) + b, bf) for b in blocks]
        scratch += [pltpu.VMEM((2, chips) + small_block, f32)]
        scratch += [pltpu.VMEM((2, chips) + w, bf) for w in wide]
    scratch += [pltpu.VMEM((2, reach) + b, bf) for b in blocks]
    scratch += [pltpu.VMEM((2, reach) + small_block, f32)]
    scratch += [pltpu.VMEM((2, reach) + w, bf) for w in wide]
    scratch += [pltpu.VMEM((chips,) + small_block, f32)]
    scratch += [pltpu.VMEM((chips,) + w, bf) for w in wide]
    scratch += [pltpu.VMEM(w, f32) for w in wide]
    scratch += [pltpu.VMEM((dense_rows // 2, w[1]), f32) for w in wide]
    scratch += [
        dma((2, chips, count)),
        dma((2, chips, count)),
        dma((2, chips, count)),
        dma((2, reach, count)),
        dma((2, reach, count)),
        dma((chips, count)),
        dma((chips, count)),
        dma((2, 2)),
        dma((2, 2, 2 + chips)),
        dma((2, reach, 2)),
        dma((2, reach, 2)),
        dma((1 + 2 * reach, 2)),
        dma((1 + 2 * reach, 2)),
    ]
    tables = len(dense_tables)
    return pl.pallas_call(
        functools.partial(reduce_kernel, dp, sizes, shares, tables),
        out_shape=tuple(jax.ShapeDtypeStruct(b, f32) for b in blocks + (small_block,))
        + (
            jax.ShapeDtypeStruct((dense_rows // 2, first.shape[1]), f32),
            jax.ShapeDtypeStruct((dense_rows // 2, second.shape[1]), f32),
            jax.ShapeDtypeStruct((dp * random.shape[0], random.shape[1]), bf),
        ),
        in_specs=[anywhere] * 7 + [inside] * (2 * tables),
        out_specs=[inside] * 7 + [anywhere],
        scratch_shapes=scratch,
        compiler_params=pltpu.CompilerParams(
            collective_id=1, has_side_effects=True, vmem_limit_bytes=63 << 20
        ),
        name="reduce_grads",
    )(value, out, up, down, first, second, random, *dense_tables, *random_tables)


norm_eps = 1e-05
masked_score = -1e30
gelu_scale = 0.7978845608028654
gelu_cube = 0.044715
bf16, f32 = jnp.bfloat16, jnp.float32


def dot_rows(a, b):
    return lax.dot_general(a, b, (((1,), (0,)), ((), ())), preferred_element_type=f32)


def dot_back(a, b):
    return lax.dot_general(a, b, (((1,), (1,)), ((), ())), preferred_element_type=f32)


def dot_down(a, b):
    return lax.dot_general(a, b, (((0,), (0,)), ((), ())), preferred_element_type=f32)


def gelu_tanh(v):
    return jnp.tanh(gelu_scale * (v + gelu_cube * (v * v * v)))


def gelu(v):
    return 0.5 * v * (1.0 + gelu_tanh(v))


def gelu_both(v):
    t = gelu_tanh(v)
    value = 0.5 * v * (1.0 + t)
    slope = 0.5 * (1.0 + t) + 0.5 * v * (1.0 - t * t) * (gelu_scale * (1.0 + 3.0 * gelu_cube * (v * v)))
    return value, slope


def standard(v):
    centre = v - jnp.mean(v, axis=-1, keepdims=True)
    inverse = lax.rsqrt(jnp.mean(centre * centre, axis=-1, keepdims=True) + norm_eps)
    return centre * inverse, inverse


def standard_back(unit, inverse, grad):
    middle = jnp.mean(grad, axis=-1, keepdims=True)
    slant = jnp.mean(grad * unit, axis=-1, keepdims=True)
    return inverse * (grad - middle - unit * slant)


def column_sum(v):
    return jnp.sum(v.astype(f32), axis=0, keepdims=True)


class Bench:
    def __init__(self, **refs):
        self.__dict__.update(refs)
        self.waiting = {}
        self.used = 0
        self.sent = []
        self.last_tiles = []

    def vector(self, name, at):
        row = name
        return self.vectors[row : row + 1, at]

    def put_vector(self, name, at, value):
        row = name
        self.vector_grads[row : row + 1, at] = value

    def fetch(self, name, source, target):
        copy = pltpu.make_async_copy(source, target, self.sems.at[self.used])
        self.used += 1
        copy.start()
        self.waiting[name] = copy

    def need(self, *names):
        for name in names:
            copy = self.waiting.pop(name, None)
            if copy is not None:
                copy.wait()

    def send(self, source, target):
        copy = pltpu.make_async_copy(source, target, self.sems.at[self.used])
        self.used += 1
        copy.start()
        self.sent.append(copy)

    def settle(self):
        for copy in self.last_tiles:
            copy.wait()
        self.last_tiles = []

    def finish(self):
        self.settle()
        for copy in self.sent:
            copy.wait()

    def plan(self, added, *grads):
        self.added = added
        self.planned = list(grads)
        self.ahead()

    def tile_copies(self, grad, cols):
        across = grad.shape[1] // cols
        count = grad.shape[0] // unit_cols * across

        def place(t):
            top = pl.multiple_of(t // across * unit_cols, unit_cols)
            left = pl.multiple_of(lax.rem(t, across) * cols, cols)
            return grad.at[pl.ds(top, unit_cols), pl.ds(left, cols)]

        def result(t):
            slot = lax.rem(t, tile_slots)
            return pltpu.make_async_copy(self.stage.at[slot, :, pl.ds(0, cols)], place(t), self.stage_sems.at[slot])

        def prior(t):
            slot = lax.rem(t, tile_slots)
            return pltpu.make_async_copy(place(t), self.prior_stage.at[slot, :, pl.ds(0, cols)], self.prior_sems.at[slot])

        return count, across, result, prior

    def ahead(self):
        if self.added and self.planned:
            count, _, _, prior = self.tile_copies(*self.planned[0])
            for t in range(min(count, tile_slots - 1)):
                prior(t).start()

    def emit(self, tile):
        grad, cols = self.planned.pop(0)
        added = self.added
        count, across, result, prior = self.tile_copies(grad, cols)
        reach = tile_slots - 1
        self.settle()

        def turn(t, carry):
            slot = lax.rem(t, tile_slots)
            if added:

                @pl.when(t + reach < count)
                def _():
                    prior(t + reach).start()

                prior(t).wait()

            @pl.when(t >= tile_slots)
            def _():
                result(t - tile_slots).wait()

            def write(value, lanes=None):
                at = (slot, slice(None), pl.ds(0, cols) if lanes is None else lanes)
                if value is None:
                    self.stage[at] = self.prior_stage[at] if added else jnp.zeros((unit_cols, lanes.size), bf16)
                else:
                    if added:
                        value = value + self.prior_stage[at].astype(f32)
                    self.stage[at] = value.astype(bf16)

            tile(t // across, lax.rem(t, across), write)
            result(t).start()
            return carry

        lax.fori_loop(0, count, turn, 0)
        self.last_tiles = [result(t) for t in range(max(0, count - tile_slots), count)]
        self.ahead()


tile_slots = 6
unit_cols = 256
unit_rows = 128


def cols_at(t):
    return pl.ds(pl.multiple_of(t * unit_cols, unit_cols), unit_cols)


def by_cols(loose, n, extent, body):
    def turn(t, carry):
        body(pl.ds(0, n), cols_at(t), t)
        return carry

    count = extent // unit_cols
    lax.fori_loop(0, count, turn, 0, unroll=(3 if count == 3 else 2) if loose and count % 6 in (0, 3) else 1)


def by_rows(n, body, start=0):
    def turn(t, carry):
        return body(pl.ds(pl.multiple_of(t * unit_rows, unit_rows), unit_rows), carry)

    return lax.fori_loop(0, n // unit_rows, turn, start, unroll=2)


def lanes_of_first(n, size):
    return lax.broadcasted_iota(jnp.int32, (n, 2 * size), 1) < size


def send_padded(b, n, **targets):
    for name, target in targets.items():
        ref = getattr(b, name)
        if n < b.slots:
            ref[n:] = jnp.zeros((b.slots - n, ref.shape[1]), bf16)
        b.send(ref, target)


def softmax(b, n, scores):
    if n < b.slots:
        scores = jnp.where(in_item(b, (n, n), 1), scores, masked_score)
    e = jnp.exp(scores - jnp.max(scores, axis=-1, keepdims=True))
    return (e * (1.0 / jnp.sum(e, axis=-1, keepdims=True))).astype(bf16)


def forward_part(b, n, dense):
    width, ff, heads, slots = b.width, b.ff, b.heads, b.slots
    size = width // heads
    whole = slice(0, width)
    rows = pl.ds(0, n)
    loose = n < slots

    def first_norm(at, carry):
        unit, _ = standard(b.x[at, :].astype(f32))
        b.a[at, :] = (unit * b.vector(FIRST_GAIN, whole) + b.vector(FIRST_SHIFT, whole)).astype(bf16)
        return carry

    b.need("x")
    by_rows(n, first_norm)
    if dense:
        b.need("first")

        def hidden(rows, at, t):
            p = dot_rows(b.a[rows], b.first[:, at]) + b.vector(SYNTH_BIAS, at)
            b.p[rows, at] = p
            b.s[rows, at] = gelu(p).astype(bf16)

        by_cols(loose, n, width, hidden)
        b.send(b.p.at[rows], b.p_out.at[rows])
    b.need("value")

    def project(rows, at, t):
        b.v[rows, at] = dot_rows(b.a[rows], b.value[:, at]).astype(bf16)

    by_cols(loose, n, width, project)
    b.need("second" if dense else "att")

    def pair(i, carry):
        here = pl.ds(pl.multiple_of(i * 2 * size, 2 * size), 2 * size)
        values = b.v[:n, here]
        got = []
        for j in range(2):
            h = 2 * i + j
            if dense:
                scores = dot_rows(b.s[:n], b.second[:, pl.ds(pl.multiple_of(h * slots, slots), n)])
                b.att[h, :n, :n] = softmax(b, n, scores)
            got.append(dot_rows(b.att[h, :n, :n], values))
        b.o[:n, here] = jnp.where(lanes_of_first(n, size), got[0], got[1]).astype(bf16)
        return carry

    lax.fori_loop(0, heads // 2, pair, 0, unroll=2 if loose and heads % 4 == 0 else 1)
    if dense:
        b.send(b.att.at[:, rows, rows], b.att_out.at[:, rows, rows])
        b.send(b.v.at[rows], b.v_out.at[rows])
        b.send(b.o.at[rows], b.o_out.at[rows])
    b.need("out")

    def branch(rows, at, t):
        b.y[rows, at] = b.x[rows, at].astype(f32) + (dot_rows(b.o[rows], b.out[:, at]) + b.vector(OUT_BIAS, at))

    by_cols(loose, n, width, branch)
    if dense:
        b.send(b.y.at[rows], b.y_out.at[rows])

    def second_norm(at, carry):
        unit, _ = standard(b.y[at, :])
        b.u[at, :] = (unit * b.vector(SECOND_GAIN, whole) + b.vector(SECOND_SHIFT, whole)).astype(bf16)
        return carry

    by_rows(n, second_norm)
    b.need("up")

    def up(rows, at, t):
        m = dot_rows(b.u[rows], b.up[:, at]) + b.vector(UP_BIAS, at)
        b.m[rows, at] = m.astype(b.m.dtype)
        b.r[rows, at] = gelu(m).astype(bf16)

    by_cols(loose, n, ff, up)
    if dense:
        b.send(b.m.at[rows], b.m_out.at[rows])
    b.need("down")

    def down(rows, at, t):
        z = b.y[rows, at] + (dot_rows(b.r[rows], b.down[:, at]) + b.vector(DOWN_BIAS, at))
        if n < slots:
            z = jnp.where(in_item(b, (n, unit_cols), 0), z, 0.0)
        b.z[rows, at] = z.astype(bf16)

    by_cols(loose, n, width, down)
    if n < slots:
        b.z[n:] = jnp.zeros((slots - n, width), bf16)
    b.send(b.z, b.states.at[b.item])
    if dense:
        b.send(b.z, b.z_out)
    else:
        send_padded(b, n, r=b.r_out, o=b.o_out, a=b.a_out)


def plan_grads(b, added):
    wide = 2 * b.width
    b.plan(
        added, (b.down_grad, b.width), (b.up_grad, wide), (b.out_grad, b.width), (b.value_grad, b.width),
        (b.second_grad, wide), (b.first_grad, b.width),
    )


def random_copies(b, n):
    part = pl.ds(0, n)

    def prior(i):
        slot = lax.rem(i, 2)
        return pltpu.make_async_copy(
            b.random_grad.at[pl.ds(2 * i, 2), part, part], b.random_old.at[slot, :, part, part], b.random_sems.at[0, slot]
        )

    def result(i):
        slot = lax.rem(i, 2)
        return pltpu.make_async_copy(
            b.random_stage.at[slot, :, part, part], b.random_grad.at[pl.ds(2 * i, 2), part, part], b.random_sems.at[1, slot]
        )

    return prior, result


def backward_part(b, n, dense, added):
    width, ff, heads, slots = b.width, b.ff, b.heads, b.slots
    size = width // heads
    wide = 2 * width
    whole = slice(0, width)
    loose = not dense and n < slots
    b.need("c", "m", "down")
    if not dense and n < slots:
        b.c[:n] = jnp.where(in_item(b, (n, width), 0), b.c[:n], jnp.zeros((), bf16))

    def down_rows(rows, at, t):
        dr = dot_back(b.c[rows], b.down_rows(t))
        value, slope = gelu_both(b.m[rows, at].astype(f32))
        gm = (slope * dr).astype(bf16)
        b.gm[rows, at] = gm
        b.put_vector(UP_BIAS, at, column_sum(gm))
        return value

    def down_tile(t, _, write):
        value = down_rows(pl.ds(0, n), cols_at(t), t)
        write(dot_down(value.astype(bf16), b.c[:n]))

    if dense:
        b.emit(down_tile)
    else:
        by_cols(loose, n, ff, down_rows)
        send_padded(b, n, gm=b.gm_out, c=b.c_out)
    b.need("up", "y")

    def up_back(rows, at, t):
        b.wide[rows, at] = dot_back(b.gm[rows], b.up[at, :ff])

    by_cols(loose, n, width, up_back)
    if dense:
        b.fetch("second", b.second_in, b.up)
    none = jnp.zeros((1, width), f32)

    def second_back(at, carry):
        unit, inverse = standard(b.y[at, :])
        gain = b.vector(SECOND_GAIN, whole)
        b.u[at, :] = (unit * gain + b.vector(SECOND_SHIFT, whole)).astype(bf16)
        du = b.wide[at, :]
        gf = b.c[at, :].astype(f32)
        gy = gf + standard_back(unit, inverse, du * gain)
        b.gy[at, :] = gy
        gb = gy.astype(bf16)
        b.gb[at, :] = gb
        found = (column_sum(du * unit), column_sum(du), column_sum(gb), column_sum(gf))
        return tuple(a + f for a, f in zip(carry, found))

    sums = by_rows(n, second_back, (none,) * 4)
    for name, total in zip((SECOND_GAIN, SECOND_SHIFT, OUT_BIAS, DOWN_BIAS), sums):
        b.put_vector(name, whole, total)
    if dense:
        b.emit(
            lambda t, s, write: write(dot_down(b.u[:n, cols_at(t)], b.gm[:n, pl.ds(pl.multiple_of(s * wide, wide), wide)])),
        )
    else:
        send_padded(b, n, u=b.u_out, gb=b.gb_out)
    b.need("o", "out")
    if dense:
        b.emit(lambda t, s, write: write(dot_down(b.o[:n, cols_at(t)], b.gb[:n])))

    def out_back(rows, at, t):
        b.go[rows, at] = dot_back(b.gb[rows], b.out[at, :]).astype(bf16)

    by_cols(loose, n, width, out_back)
    b.need("v", "att")

    def pair_back(i, keep):
        here = pl.ds(pl.multiple_of(i * 2 * size, 2 * size), 2 * size)
        values, grads = b.v[:n, here], b.go[:n, here]
        first = lanes_of_first(n, size)
        got = []
        for j in range(2):
            own = jnp.where(first if j == 0 else jnp.logical_not(first), grads, jnp.zeros_like(grads))
            weight = b.att[2 * i + j, :n, :n]
            mixed = weight.astype(f32) * dot_back(own, values)
            keep(2 * i + j, j, mixed - weight.astype(f32) * jnp.sum(mixed, axis=-1, keepdims=True))
            got.append(dot_down(weight, grads))
        b.gv[:n, here] = jnp.where(first, got[0], got[1]).astype(bf16)

    if dense:

        def keep_dense(h, j, ds):
            b.gs[:n, pl.ds(pl.multiple_of(h * slots, slots), n)] = ds.astype(bf16)

        def loop(i, carry):
            pair_back(i, keep_dense)
            return carry

        lax.fori_loop(0, heads // 2, loop, 0)
    else:

        prior, result = random_copies(b, n if added else slots)

        def loop(i, carry):
            slot = lax.rem(i, 2)
            if added:

                @pl.when(i + 1 < heads // 2)
                def _():
                    prior(i + 1).start()

                prior(i).wait()

            @pl.when(i >= 2)
            def _():
                result(i - 2).wait()

            def keep_random(h, j, ds):
                if added:
                    ds = ds + b.random_old[slot, j, :n, :n].astype(f32)
                elif n < slots:
                    b.random_stage[slot, j] = jnp.zeros((slots, slots), bf16)
                b.random_stage[slot, j, :n, :n] = ds.astype(bf16)

            pair_back(i, keep_random)
            result(i).start()
            return carry

        lax.fori_loop(0, heads // 2, loop, 0)
        for i in (heads // 2 - 2, heads // 2 - 1):
            result(i).wait()
    b.need("x")
    if dense:

        def first_norm(at, carry):
            unit, _ = standard(b.x[at, :].astype(f32))
            b.a[at, :] = (unit * b.vector(FIRST_GAIN, whole) + b.vector(FIRST_SHIFT, whole)).astype(bf16)
            return carry

        by_rows(n, first_norm)
        b.emit(lambda t, s, write: write(dot_down(b.a[:n, cols_at(t)], b.gv[:n])))
    else:
        send_padded(b, n, gv=b.gv_out)
    if dense:
        b.need("p")

        def slopes(rows, at, t):
            value, slope = gelu_both(b.p[rows, at])
            b.s[rows, at] = value.astype(bf16)
            b.wide[rows, at] = slope

        by_cols(loose, n, width, slopes)
        group = wide // slots

        def second_tile(t, s, write):
            tile = b.s[:n, cols_at(t)]
            if n == slots:
                write(dot_down(tile, b.gs[:n, pl.ds(pl.multiple_of(s * wide, wide), wide)]))
                return
            for q in range(group):
                left = pl.multiple_of(s * wide + q * slots, slots)
                write(dot_down(tile, b.gs[:n, pl.ds(left, n)]), pl.ds(q * slots, n))
                write(None, pl.ds(q * slots + n, slots - n))

        b.emit(second_tile)
        b.need("second")

        def hidden_back(rows, at, t):
            if n == slots:
                hidden = dot_back(b.gs[rows], b.up[at, :])
            else:
                hidden = jnp.zeros((rows.size, unit_cols), f32)
                for h in range(heads):
                    part = slice(h * slots, h * slots + n)
                    hidden = hidden + dot_back(b.gs[rows, part], b.up[at, part])
            gp = (b.wide[rows, at] * hidden).astype(bf16)
            b.gp[rows, at] = gp
            b.put_vector(SYNTH_BIAS, at, column_sum(gp))

        by_cols(loose, n, width, hidden_back)
        b.emit(lambda t, s, write: write(dot_down(b.a[:n, cols_at(t)], b.gp[:n])))
    b.need("value", "first")

    def normed_back(rows, at, t):
        ga = dot_back(b.gv[rows], b.value[at, :])
        if dense:
            ga = ga + dot_back(b.gp[rows], b.first[at, :])
        b.wide[rows, at] = ga

    by_cols(loose, n, width, normed_back)

    def first_back(at, carry):
        unit, inverse = standard(b.x[at, :].astype(f32))
        ga = b.wide[at, :]
        dx = b.gy[at, :] + standard_back(unit, inverse, ga * b.vector(FIRST_GAIN, whole))
        b.dx[at, :] = dx.astype(bf16)
        return carry[0] + column_sum(ga * unit), carry[1] + column_sum(ga)

    sums = by_rows(n, first_back, (none,) * 2)
    b.put_vector(FIRST_GAIN, whole, sums[0])
    b.put_vector(FIRST_SHIFT, whole, sums[1])
    if n < slots:
        b.dx[n:] = jnp.zeros((slots - n, width), bf16)
    if not dense:
        b.send(b.dx, b.dx_out)
    b.send(b.dx, b.grads_in.at[b.item])
    b.send(b.vector_grads, b.table_out)


def item_of(lengths, turn):
    if lengths.shape[0] == 2:
        return jnp.where(lengths[1] < lengths[0], 1 - turn, turn)
    return jnp.int32(turn)


def by_length(section, lengths, turn, slots, call):
    long = lengths[item_of(lengths, turn)] > slots // 2
    if turn == 0:
        branches, which = (slots, slots // 2, 0), jnp.where(long, 0, 1)
    else:
        branches, which = (slots // 2, slots, 0), jnp.where(long, 1, 0)
    which = jnp.where(lax.axis_index(section_axis) == section, which, 2)
    return lax.switch(which, [functools.partial(call, n) for n in branches])


def in_item(b, shape, axis):
    return lax.broadcasted_iota(jnp.int32, shape, axis) < b.length


def shape_of(table):
    slots, width = table.x.shape
    return dict(width=width, ff=table.m.shape[1], heads=table.att.shape[0], slots=slots)


class ForwardRefs(NamedTuple):
    lengths: Any
    vectors: Any
    x_in: Any
    first_in: Any
    second_in: Any
    value_in: Any
    out_in: Any
    up_in: Any
    down_in: Any
    states: Any
    z_out: Any
    p_out: Any
    att_out: Any
    v_out: Any
    o_out: Any
    y_out: Any
    m_out: Any
    x: Any
    first: Any
    second: Any
    value: Any
    out: Any
    up: Any
    down: Any
    z: Any
    p: Any
    att: Any
    v: Any
    o: Any
    y: Any
    m: Any
    a: Any
    s: Any
    u: Any
    r: Any
    sems: Any


def dense_forward_kernel(n, turn, *refs):
    if n == 0:
        return
    refs = refs[:9] + refs[9 + (turn > 0) :]
    table = ForwardRefs(*refs)
    shape = shape_of(table)

    item = item_of(table.lengths, turn)
    b = Bench(item=item, length=table.lengths[item], **table._asdict(), **shape)
    rows = pl.ds(0, n)
    b.fetch("x", b.x_in.at[item, rows], b.x.at[rows])
    b.fetch("first", b.first_in, b.first)
    b.fetch("value", b.value_in, b.value)
    b.fetch("second", b.second_in, b.second)
    b.fetch("out", b.out_in, b.out)
    b.fetch("up", b.up_in, b.up)
    b.fetch("down", b.down_in, b.down)
    forward_part(b, n, True)
    b.finish()


class BackwardRefs(NamedTuple):
    lengths: Any
    vectors: Any
    x_in: Any
    c_in: Any
    p_in: Any
    att_in: Any
    v_in: Any
    o_in: Any
    y_in: Any
    m_in: Any
    first_in: Any
    second_in: Any
    value_in: Any
    out_in: Any
    up_in: Any
    down_in: Any
    grads_in: Any
    table_out: Any
    down_grad: Any
    up_grad: Any
    out_grad: Any
    value_grad: Any
    first_grad: Any
    second_grad: Any
    x: Any
    c: Any
    p: Any
    att: Any
    v: Any
    o: Any
    y: Any
    m: Any
    first: Any
    value: Any
    out: Any
    up: Any
    a: Any
    u: Any
    s: Any
    go: Any
    gv: Any
    gp: Any
    gb: Any
    gy: Any
    wide: Any
    dx: Any
    feed: Any
    stage: Any
    prior_stage: Any
    vector_grads: Any
    sems: Any
    stage_sems: Any
    prior_sems: Any


def dense_backward_kernel(n, turn, *refs):
    if n == 0:
        return
    refs = refs[:16] + refs[16 + (7 if turn > 0 else 5) :]
    table = BackwardRefs(*refs)
    shape = shape_of(table)
    ff, width = table.m.shape[1], table.x.shape[1]

    item = item_of(table.lengths, turn)
    b = Bench(item=item, length=table.lengths[item], **table._asdict(), **shape)
    b.gm, b.gs = b.feed.at[:, pl.ds(0, ff)], b.feed
    parts = width // unit_cols
    b.down_rows = lambda t: b.up[
        cols_at(lax.rem(t, parts)), pl.ds(pl.multiple_of(ff + t // parts * width, width), width)
    ]
    rows = pl.ds(0, n)
    b.fetch("c", b.c_in.at[rows], b.c.at[rows])
    b.fetch("m", b.m_in.at[rows], b.m.at[rows])
    for part in range(ff // width):
        b.fetch(f"down{part}", b.down_in.at[pl.ds(part * width, width)], b.up.at[:, pl.ds(ff + part * width, width)])
    b.fetch("up", b.up_in, b.up.at[:, pl.ds(0, ff)])
    b.fetch("y", b.y_in.at[rows], b.y.at[rows])
    b.fetch("o", b.o_in.at[rows], b.o.at[rows])
    b.fetch("out", b.out_in, b.out)
    b.fetch("v", b.v_in.at[rows], b.v.at[rows])
    b.fetch("att", b.att_in.at[:, rows, rows], b.att.at[:, rows, rows])
    b.fetch("x", b.x_in.at[item, rows], b.x.at[rows])
    b.fetch("p", b.p_in.at[rows], b.p.at[rows])
    b.fetch("value", b.value_in, b.value)
    b.fetch("first", b.first_in, b.first)
    plan_grads(b, turn > 0)
    b.need(*[f"down{part}" for part in range(ff // width)])
    backward_part(b, n, True, turn > 0)
    b.finish()


class RandomRefs(NamedTuple):
    lengths: Any
    vectors: Any
    x_in: Any
    c_in: Any
    att_in: Any
    value_in: Any
    out_in: Any
    up_in: Any
    down_in: Any
    states: Any
    grads_in: Any
    dx_out: Any
    table_out: Any
    random_grad: Any
    r_out: Any
    o_out: Any
    a_out: Any
    gm_out: Any
    u_out: Any
    gb_out: Any
    gv_out: Any
    c_out: Any
    x: Any
    c: Any
    att: Any
    v: Any
    o: Any
    y: Any
    m: Any
    value: Any
    out: Any
    up: Any
    down: Any
    a: Any
    u: Any
    go: Any
    gv: Any
    gb: Any
    gy: Any
    wide: Any
    z: Any
    dx: Any
    r: Any
    gm: Any
    random_stage: Any
    random_old: Any
    vector_grads: Any
    sems: Any
    random_sems: Any


def random_kernel(n, turn, *refs):
    if n == 0:
        return
    refs = refs[:9] + refs[9 + (3 if turn > 0 else 1) :]
    table = RandomRefs(*refs)
    shape = shape_of(table)

    item = item_of(table.lengths, turn)
    b = Bench(item=item, length=table.lengths[item], **table._asdict(), **shape)
    rows = pl.ds(0, n)
    b.fetch("x", b.x_in.at[rows], b.x.at[rows])
    b.fetch("value", b.value_in, b.value)
    b.fetch("att", b.att_in.at[:, rows, rows], b.att.at[:, rows, rows])
    b.fetch("out", b.out_in, b.out)
    b.fetch("up", b.up_in, b.up)
    b.fetch("down", b.down_in, b.down)
    b.down_rows = lambda t: b.down[cols_at(t), :]
    b.fetch("c", b.c_in.at[item, rows], b.c.at[rows])
    if turn > 0:
        random_copies(b, n)[0](0).start()
    forward_part(b, n, False)
    backward_part(b, n, False, turn > 0)
    b.finish()


class AttentionRefs(NamedTuple):
    lengths: Any
    logits_in: Any
    att_out: Any
    att: Any
    sems: Any


def random_attention_kernel(n, turn, *refs):
    if n == 0:
        return
    table = AttentionRefs(*refs)
    heads, slots, _ = table.att.shape
    b = Bench(length=table.lengths[item_of(table.lengths, turn)], slots=slots, **table._asdict())
    rows = pl.ds(0, n)
    half = heads // 2
    for k in (0, 1):
        part = pl.ds(k * half, half)
        b.fetch(k, b.logits_in.at[part, rows, rows], b.att.at[part, rows, rows])
    for k in (0, 1):
        b.need(k)

        def head(h, carry):
            b.att[h, :n, :n] = softmax(b, n, b.att[h, :n, :n].astype(f32))
            return carry

        lax.fori_loop(k * half, (k + 1) * half, head, 0)
        part = pl.ds(k * half, half)
        b.send(b.att.at[part, rows, rows], b.att_out.at[part, rows, rows])
    b.finish()


def random_attention(n, turn, lengths, logits):
    return pl.pallas_call(
        functools.partial(random_attention_kernel, n, turn),
        out_shape=S(logits.shape, bf16),
        in_specs=[scalars, anywhere],
        out_specs=anywhere,
        scratch_shapes=[] if n == 0 else [vmem(*logits.shape), pltpu.SemaphoreType.DMA((4,))],
        compiler_params=own_params(),
        name=f"random_attention_{n}",
    )(lengths, logits)


def weight_steps(kept, grads, c, r, o, a, gm, u, gb, gv, stage, sems, stage_sems):
    count = len(kept)
    slots = c.shape[0] // count
    b = Bench(stage=stage, sems=sems, stage_sems=stage_sems, width=c.shape[1])
    wide = 2 * b.width
    def need(*names):
        b.need(*[f"{name}{k}" for name in names for k in range(count)])

    def begin():
        for name, ref, at in (
            ("o", o, 1), ("gb", gb, 5), ("a", a, 2), ("gv", gv, 6), ("c", c, 7), ("r", r, 0), ("gm", gm, 3), ("u", u, 4),
        ):
            for k in range(count):
                b.fetch(f"{name}{k}", kept[k][at], ref.at[pl.ds(k * slots, slots)])
        out_grad, value_grad, down_grad, up_grad = grads
        b.plan(False, (out_grad, b.width), (value_grad, b.width), (down_grad, b.width), (up_grad, wide))

    def narrow():
        need("o", "gb")
        b.emit(lambda t, s, write: write(dot_down(o[:, cols_at(t)], gb[...])))
        need("a", "gv")
        b.emit(lambda t, s, write: write(dot_down(a[:, cols_at(t)], gv[...])))

    def down():
        need("c", "r")
        b.emit(lambda t, s, write: write(dot_down(r[:, cols_at(t)], c[...])))

    def up():
        need("gm", "u")
        b.emit(lambda t, s, write: write(dot_down(u[:, cols_at(t)], gm[:, pl.ds(pl.multiple_of(s * wide, wide), wide)])))
        b.finish()

    return begin, narrow, down, up


anywhere = pl.BlockSpec(memory_space=pl.ANY)
inside = pl.BlockSpec(memory_space=pltpu.VMEM)
scalars = pl.BlockSpec(memory_space=pltpu.SMEM)
S = jax.ShapeDtypeStruct


def vmem(*shape, dtype=bf16):
    return pltpu.VMEM(shape, dtype)


def own_params():
    return pltpu.CompilerParams(vmem_limit_bytes=63 << 20, has_side_effects=True)


def dense_forward(n, turn, lengths, vectors, inputs, weights, heads, states):
    _, slots, width = inputs.shape
    ff = weights["up"].shape[1]
    outs = (
        S(inputs.shape, bf16), S((slots, width), bf16), S((slots, width), f32), S((heads, slots, slots), bf16),
        S((slots, width), bf16), S((slots, width), bf16), S((slots, width), f32), S((slots, ff), bf16),
    )
    rows = vmem(slots, width)
    old = [] if states is None else [states]
    return pl.pallas_call(
        functools.partial(dense_forward_kernel, n, turn),
        out_shape=outs,
        in_specs=[scalars, inside if n else anywhere] + [anywhere] * (7 + len(old)),
        out_specs=[anywhere] * 8,
        input_output_aliases={9: 0} if old else {},
        scratch_shapes=[] if n == 0 else [
            rows, vmem(width, width), vmem(width, heads * slots), vmem(width, width), vmem(width, width), vmem(width, ff),
            vmem(ff, width), rows, vmem(slots, width, dtype=f32), vmem(heads, slots, slots), rows, rows,
            vmem(slots, width, dtype=f32), vmem(slots, ff), rows, rows, rows, vmem(slots, ff), pltpu.SemaphoreType.DMA((20,)),
        ],
        compiler_params=own_params(),
        name=f"dense_forward_{n}",
    )(lengths, vectors, inputs, *[weights[k] for k in ("first", "second", "value", "out", "up", "down")], *old)


def dense_backward(n, turn, lengths, vectors, inputs, c, kept, weights, grads_in, old):
    p, att, v, o, y, m = kept
    heads = att.shape[0]
    _, slots, width = inputs.shape
    ff = weights["up"].shape[1]
    names = ("down", "up", "out", "value", "first", "second")
    outs = (S(inputs.shape, bf16), S(vectors.shape, f32)) + tuple(S(weights[name].shape, bf16) for name in names)
    rows = vmem(slots, width)
    square = vmem(width, width)
    aliases = {16: 0}
    aliases.update({17 + n: 2 + n for n in range(len(old))})
    return pl.pallas_call(
        functools.partial(dense_backward_kernel, n, turn),
        out_shape=outs,
        in_specs=[scalars, inside if n else anywhere] + [anywhere] * (15 + len(old)),
        out_specs=[anywhere] * 8,
        input_output_aliases=aliases,
        scratch_shapes=[] if n == 0 else [
            rows, rows, vmem(slots, width, dtype=f32), vmem(heads, slots, slots), rows, rows,
            vmem(slots, width, dtype=f32), vmem(slots, ff), square, square, square, vmem(width, 2 * ff),
            rows, rows, rows, rows, rows, rows, rows, vmem(slots, width, dtype=f32), vmem(slots, width, dtype=f32), rows,
            vmem(slots, 2 * ff), vmem(tile_slots, unit_cols, 2 * width), vmem(tile_slots, unit_cols, 2 * width),
            pltpu.VMEM(vectors.shape, f32),
            pltpu.SemaphoreType.DMA((24,)), pltpu.SemaphoreType.DMA((tile_slots,)), pltpu.SemaphoreType.DMA((tile_slots,)),
        ],
        compiler_params=own_params(),
        name=f"dense_backward_{n}",
    )(
        lengths, vectors, inputs, c, p, att, v, o, y, m,
        *[weights[k] for k in ("first", "second", "value", "out", "up", "down")], grads_in, *old,
    )


def random_step(n, turn, lengths, vectors, x, cotangent, att, weights, states, old):
    heads, slots, _ = att.shape
    width = x.shape[1]
    ff = weights["up"].shape[1]
    narrow = S((slots, width), bf16)
    broad = S((slots, ff), bf16)
    outs = (
        S(cotangent.shape, bf16), S(cotangent.shape, bf16), narrow, S(vectors.shape, f32), S(att.shape, bf16),
        broad, narrow, narrow, broad, narrow, narrow, narrow, narrow,
    )
    rows = vmem(slots, width)
    square = vmem(width, width)
    deep = vmem(slots, width, dtype=f32)
    pair = vmem(2, 2, slots, slots)
    return pl.pallas_call(
        functools.partial(random_kernel, n, turn),
        out_shape=outs,
        in_specs=[scalars, inside if n else anywhere] + [anywhere] * (8 + len(old)),
        out_specs=[anywhere] * 13,
        input_output_aliases={9: 0, 10: 1, 11: 4} if old else {9: 0},
        scratch_shapes=[] if n == 0 else [
            rows, rows, vmem(heads, slots, slots), rows, rows, deep, vmem(slots, ff), square, square,
            vmem(width, ff), vmem(ff, width), rows, rows, rows, rows, rows, deep, deep, rows, rows,
            vmem(slots, ff), vmem(slots, ff), pair, pair, pltpu.VMEM(vectors.shape, f32),
            pltpu.SemaphoreType.DMA((28,)), pltpu.SemaphoreType.DMA((2, 2)),
        ],
        compiler_params=own_params(),
        name=f"random_step_{n}",
    )(lengths, vectors, x, cotangent, att, *[weights[k] for k in ("value", "out", "up", "down")], states, *old)


def weight_scratch(count, slots, width, ff):
    tall = vmem(count * slots, width)
    broad = vmem(count * slots, ff)
    return [
        tall, broad, tall, tall, broad, tall, tall, tall, vmem(tile_slots, unit_cols, 2 * width),
        pltpu.SemaphoreType.DMA((8 * count,)), pltpu.SemaphoreType.DMA((tile_slots,)),
    ]


def weights_kernel(count, *refs):
    kept = [refs[8 * k : 8 * k + 8] for k in range(count)]

    @pl.when(lax.axis_index(section_axis) == 1)
    def _():
        down, up, out, value, *scratch = refs[8 * count :]
        for step in weight_steps(kept, (out, value, down, up), *scratch):
            step()


def random_weights(kept, weights):
    slots, width = kept[0][1].shape
    ff = kept[0][0].shape[1]
    names = ("down", "up", "out", "value")
    return pl.pallas_call(
        functools.partial(weights_kernel, len(kept)),
        out_shape=tuple(S(weights[name].shape, bf16) for name in names),
        in_specs=[anywhere] * (8 * len(kept)),
        out_specs=[anywhere] * 4,
        scratch_shapes=weight_scratch(len(kept), slots, width, ff),
        compiler_params=own_params(),
        name="random_weights",
    )(*[a for item in kept for a in item])


def deliver_kernel(arrays, random_in, small, *refs):
    ins, outs = refs[:arrays], refs[arrays + 1 : 2 * arrays + 1]
    random_ref = refs[arrays]
    vectors = refs[2 * arrays + 1 : 2 * arrays + 1 + vector_count]
    narrow, wide, sems, random_sems = refs[2 * arrays + 1 + vector_count :]
    slots, rows, _ = narrow.shape
    count = random_in.shape[0] // rows

    def part(n):
        return pl.ds(pl.multiple_of(n * rows, rows), rows)

    def load(n):
        slot = lax.rem(n, slots)
        return pltpu.make_async_copy(random_in.at[part(n)], narrow.at[slot], random_sems.at[0, slot])

    def store(n):
        slot = lax.rem(n, slots)
        return pltpu.make_async_copy(wide.at[slot], random_ref.at[part(n)], random_sems.at[1, slot])

    for n in range(slots - 1):
        load(n).start()
    copies = [pltpu.make_async_copy(a, b, sems.at[n]) for n, (a, b) in enumerate(zip(ins, outs))]
    for copy in copies:
        copy.start()
    for row, ref in enumerate(vectors):
        ref[...] = small[row : row + 1, : ref.shape[1]]

    def turn(n, carry):
        @pl.when(n + slots - 1 < count)
        def _():
            load(n + slots - 1).start()

        load(n).wait()

        @pl.when(n >= slots)
        def _():
            store(n - slots).wait()

        wide[lax.rem(n, slots)] = narrow[lax.rem(n, slots)].astype(f32)
        store(n).start()
        return carry

    lax.fori_loop(0, count, turn, 0)
    for n in range(count - slots, count):
        store(n).wait()
    for copy in copies:
        copy.wait()


def deliver(random, small, extents, arrays):
    rows, cols = random.shape
    slots = 4
    inside = pl.BlockSpec(memory_space=pltpu.VMEM)
    return pl.pallas_call(
        functools.partial(deliver_kernel, len(arrays)),
        out_shape=(S(random.shape, f32),)
        + tuple(S(a.shape, f32) for a in arrays)
        + tuple(S((1, extent), f32) for extent in extents),
        in_specs=[anywhere, inside] + [inside] * len(arrays),
        out_specs=[anywhere] * (1 + len(arrays)) + [inside] * len(extents),
        scratch_shapes=[
            vmem(slots, rows // 12, cols), vmem(slots, rows // 12, cols, dtype=f32),
            pltpu.SemaphoreType.DMA((len(arrays),)), pltpu.SemaphoreType.DMA((2, slots)),
        ],
        compiler_params=own_params(),
        name="deliver",
    )(random, small, *arrays)


def run_layers(inputs, cotangent, lengths, weights, vectors, logits, finish_random):
    count, slots, _ = inputs.shape
    heads = logits.shape[0]
    states = None
    firsts, seconds = [], []
    for turn in range(count):

        def forward(n):
            return dense_forward(n, turn, lengths, vectors, inputs, weights, heads, states)

        states, z, *kept = by_length(0, lengths, turn, slots, forward)
        firsts.append(kept)
        seconds.append(passed_along(z, section_axis, 1))
    atts = [
        by_length(1, lengths, turn, slots, lambda n: random_attention(n, turn, lengths, logits)) for turn in range(count)
    ]
    seconds[0], *atts = lax.optimization_barrier((seconds[0], *atts))
    old, backs, random_tables, random_kept = [], [], [], []
    for turn in range(count):

        def step(n):
            return random_step(n, turn, lengths, vectors, seconds[turn], cotangent, atts[turn], weights, states, old)

        states, grads_in, dx, table, random_grad, *kept = by_length(1, lengths, turn, slots, step)
        old = [grads_in, random_grad]
        backs.append(passed_along(dx, section_axis, -1))
        random_tables.append(table)
        random_kept.append(kept)
    random_grad, *grads = finish_random(random_grad, random_kept, weights)
    dense_tables = []
    for turn in range(count):

        def backward(n):
            return dense_backward(
                n, turn, lengths, vectors, inputs, backs[turn], firsts[turn], weights, grads_in, grads
            )

        grads_in, table, *grads = by_length(0, lengths, turn, slots, backward)
        dense_tables.append(table)
    grads = dict(zip(("down", "up", "out", "value", "first", "second"), grads))
    return states, grads_in, grads, random_grad, dense_tables, random_tables


def random_finish_kernel(dp, count, random_in, *refs):
    kept = [refs[8 * k : 8 * k + 8] for k in range(count)]
    refs = refs[8 * count :]
    random_ref, down, up, out, value = refs[:5]
    grads = (out, value, down, up)
    (
        own, sib, ring, own_sems, sib_send, sib_recv, ring_send, ring_recv,
    ) = refs[5:13]
    begin, *meanwhile = weight_steps(kept, grads, *refs[13:])
    place = Place(dp)
    reach, chips = place.reach, place.chips
    block = random_in.shape[0] // (2 * chips)
    strip = block // 2
    away = (reach,) + tuple(o for t in range(reach - 1, 0, -1) for o in (t, -t)) + (0,)
    spot_of = {o: n for n, o in enumerate(away)}
    spot_of[-reach] = 0

    def part(ref, o, core):
        return ref.at[pl.ds(pl.multiple_of((core * chips + place.chip_at(o)) * block, block), block)]

    def load(o):
        return pltpu.make_async_copy(part(random_in, o, place.core), own.at[spot_of[o]], own_sems.at[spot_of[o]])

    def lend(o):
        at = spot_of[o]
        return remote(part(random_in, o, 1 - place.core), sib.at[at], sib_send.at[at], sib_recv.at[at], place.sibling())

    def carried(i, way, step):
        return step > 0 or i == way

    def ring_copy(i, way, step):
        turn = 1 if way == 0 else -1
        rows = pl.ds(i * strip, strip)
        return remote(
            own.at[spot_of[turn * (reach - step)], rows], ring.at[way, step, rows],
            ring_send.at[way, step, i], ring_recv.at[way, step, i], place.along(turn),
        )

    @pl.when(place.section == 1)
    def _():
        place.greet()
        for o in away:
            lend(o).start()
            load(o).start()
        begin()
        for step in range(reach + 1):
            for i in (0, 1):
                for way in (0, 1):
                    o = (reach - step) * (1 if way == 0 else -1)
                    if step < reach and not carried(i, way, step) or step == reach and way == 1:
                        continue
                    if i == 0:
                        load(o).wait()
                        lend(o).wait_recv()
                    rows = pl.ds(i * strip, strip)
                    terms = [own.at[spot_of[o], rows], sib.at[spot_of[o], rows]]
                    for back in (0, 1) if step == reach else (way,):
                        if step > 0 and carried(i, back, step - 1):
                            ring_copy(i, back, step - 1).wait_recv()
                            terms.append(ring.at[back, step - 1, rows])
                    store_sum(own.at[spot_of[o], rows], terms, strip)
                    if step < reach:
                        ring_copy(i, way, step).start()
            if meanwhile and step < reach:
                meanwhile.pop(0)()
        keep = pltpu.make_async_copy(own.at[spot_of[0]], random_ref, own_sems.at[chips])
        keep.start()
        for work in meanwhile:
            work()
        for o in away:
            lend(o).wait_send()
        keep.wait()
        for i in (0, 1):
            for way in (0, 1):
                for step in range(reach):
                    if carried(i, way, step):
                        ring_copy(i, way, step).wait_send()


def random_finish(dp, random, kept, weights):
    chips = dp // 2
    reach = chips // 2
    block = (random.shape[0] // dp, random.shape[1])
    slots, width = kept[0][1].shape
    ff = kept[0][0].shape[1]
    count = len(kept)
    dma = pltpu.SemaphoreType.DMA
    names = ("down", "up", "out", "value")
    return pl.pallas_call(
        functools.partial(random_finish_kernel, dp, count),
        out_shape=(S(block, random.dtype),) + tuple(S(weights[name].shape, bf16) for name in names),
        in_specs=[anywhere] * (1 + 8 * count),
        out_specs=[anywhere] * 5,
        scratch_shapes=[
            pltpu.VMEM((chips,) + block, random.dtype),
            pltpu.VMEM((chips,) + block, random.dtype),
            pltpu.VMEM((2, reach) + block, random.dtype),
            dma((chips + 1,)),
            dma((chips,)),
            dma((chips,)),
            dma((2, reach, 2)),
            dma((2, reach, 2)),
        ] + weight_scratch(count, slots, width, ff),
        compiler_params=pltpu.CompilerParams(
            collective_id=2, has_side_effects=True, vmem_limit_bytes=63 << 20
        ),
        name="random_finish",
    )(random, *[a for item in kept for a in item])


def passed_along(x, axis, by):
    size = lax.axis_size(axis)
    pairs = [(i, i + by) for i in range(size) if 0 <= i + by < size]
    return lax.ppermute(x, axis, pairs)


def table_of(vectors, ff):
    return jnp.stack([jnp.pad(v.astype(f32), (0, ff - v.shape[0])) for v in vectors])


def per_device(
    inputs,
    cotangent,
    lengths,
    first_gain,
    first_shift,
    value_weight,
    out_weight,
    out_bias,
    second_gain,
    second_shift,
    up_weight,
    up_bias,
    down_weight,
    down_bias,
    synth_first,
    synth_bias,
    synth_second,
    random_logits,
):
    dp = lax.axis_size(dp_axis)
    is_dense = lax.axis_index(section_axis) == 0
    value_share, out_share, up_share, down_share = value_weight[0], out_weight[0], up_weight[0], down_weight[0]
    ff = up_share.shape[1]
    shares = [
        a.reshape(1, -1)
        for a in (first_gain, first_shift, out_bias, second_gain, second_shift, down_bias, up_bias, synth_bias)
    ]
    extents = tuple(a.shape[1] for a in shares)
    ringed = (
        dp % 4 == 0 and dp > 4 and value_share.shape[0] % 16 == 0 and synth_first.shape[0] % 8 == 0
        and max(extents) <= small_block[1]
    )
    if ringed:
        value, out, up, down, first, second, table = gather_weights(
            dp, value_share, out_share, up_share, down_share, synth_first, synth_second, shares
        )
    else:
        value, out, up, down = (
            lax.all_gather(a, dp_axis, axis=0, tiled=True) for a in (value_share, out_share, up_share, down_share)
        )
        first, second = (lax.all_gather(a, (section_axis, dp_axis), axis=0, tiled=True) for a in (synth_first, synth_second))
        axes = [dp_axis] * synth_row + [(section_axis, dp_axis)]
        table = table_of([lax.all_gather(a[0], axis, axis=0, tiled=True) for a, axis in zip(shares, axes)], ff)
    weights = dict(value=value, out=out, up=up, down=down, first=first, second=second)

    def finish_random(grad, kept, of):
        flat = grad.reshape(-1, grad.shape[-1])
        return random_finish(dp, flat, kept, of) if ringed else (flat, *random_weights(kept, of))

    states, grads_in, grads, random_grad, dense_tables, random_tables = run_layers(
        inputs, cotangent, lengths, weights, table, random_logits, finish_random
    )
    arrays = [grads[name] for name in ("value", "out", "up", "down", "first", "second")]
    if ringed:
        g_value, g_out, g_up, g_down, small, g_first, g_second, random_grad = reduce_grads(
            dp, *arrays, random_grad, dense_tables, random_tables, extents
        )
        random_total, g_value, g_out, g_up, g_down, g_first, g_second, *g_vectors = deliver(
            random_grad, small, extents, (g_value, g_out, g_up, g_down, g_first, g_second)
        )
        g_vectors = [v.reshape(-1) for v in g_vectors]
    else:
        g_value, g_out, g_up, g_down = (
            lax.psum_scatter(a, dp_axis, scatter_dimension=0, tiled=True).astype(f32) for a in arrays[:4]
        )
        g_first, g_second = (
            lax.psum_scatter(jnp.where(is_dense, a, jnp.zeros_like(a)), (section_axis, dp_axis), scatter_dimension=0, tiled=True).astype(f32)
            for a in arrays[4:]
        )
        grad_table = jnp.where(is_dense, sum(dense_tables), sum(random_tables))
        g_vectors = [
            lax.psum_scatter(grad_table[row, : dp * extents[row]], dp_axis, scatter_dimension=0, tiled=True)
            for row in range(synth_row)
        ]
        synth_grad = jnp.where(is_dense, grad_table[synth_row, : 2 * dp * extents[synth_row]], 0.0)
        g_vectors.append(lax.psum_scatter(synth_grad, (section_axis, dp_axis), scatter_dimension=0, tiled=True))
        random_total = lax.psum(jnp.where(is_dense, jnp.zeros_like(random_grad), random_grad), (section_axis, dp_axis)).astype(f32)
    random_total = random_total.reshape(random_logits.shape)
    return (
        states[None],
        grads_in[None],
        g_vectors[FIRST_GAIN][None],
        g_vectors[FIRST_SHIFT][None],
        g_value[None],
        g_out[None],
        g_vectors[OUT_BIAS][None],
        g_vectors[SECOND_GAIN][None],
        g_vectors[SECOND_SHIFT][None],
        g_up[None],
        g_vectors[UP_BIAS][None],
        g_down[None],
        g_vectors[DOWN_BIAS][None],
        g_first,
        g_vectors[SYNTH_BIAS],
        g_second,
        random_total,
    )


def solution(mesh):
    in_specs = (
        P(dp_axis, None, None),
        P(dp_axis, None, None),
        P(dp_axis),
        P(section_axis, dp_axis),
        P(section_axis, dp_axis),
        P(section_axis, dp_axis, None),
        P(section_axis, dp_axis, None),
        P(section_axis, dp_axis),
        P(section_axis, dp_axis),
        P(section_axis, dp_axis),
        P(section_axis, dp_axis, None),
        P(section_axis, dp_axis),
        P(section_axis, dp_axis, None),
        P(section_axis, dp_axis),
        P((section_axis, dp_axis), None),
        P((section_axis, dp_axis)),
        P((section_axis, dp_axis), None),
        P(),
    )
    out_specs = (
        P(section_axis, dp_axis, None, None),
        P(section_axis, dp_axis, None, None),
        P(section_axis, dp_axis),
        P(section_axis, dp_axis),
        P(section_axis, dp_axis, None),
        P(section_axis, dp_axis, None),
        P(section_axis, dp_axis),
        P(section_axis, dp_axis),
        P(section_axis, dp_axis),
        P(section_axis, dp_axis, None),
        P(section_axis, dp_axis),
        P(section_axis, dp_axis, None),
        P(section_axis, dp_axis),
        P((section_axis, dp_axis), None),
        P((section_axis, dp_axis)),
        P((section_axis, dp_axis), None),
        P(),
    )
    return jax.shard_map(
        per_device, mesh=mesh, in_specs=in_specs, out_specs=out_specs, check_vma=False
    )
```

```python
import functools
from typing import Any, NamedTuple

import jax
import jax.numpy as jnp
from jax import lax
from jax.experimental import pallas as pl
from jax.experimental.pallas import tpu as pltpu
from jax.sharding import PartitionSpec as P

MESH = pl.DeviceIdType.MESH


class Place:
    def __init__(self, dp):
        self.chips = dp // 2
        self.reach = self.chips // 2
        self.section = lax.axis_index(section_axis)
        index = lax.axis_index(dp_axis)
        self.core = lax.rem(index, 2)
        self.chip = index // 2
        column = lax.rem(self.chip, 2)
        row = self.chip // 2
        self.position = row + column * (self.chips - 1 - 2 * row)

    def chip_at(self, steps):
        spot = lax.rem(self.position + steps + 2 * self.chips, self.chips)
        column = spot // self.reach
        row = spot + column * (self.chips - 1 - 2 * spot)
        return 2 * row + column

    def along(self, steps):
        return (self.section, 2 * self.chip_at(steps) + self.core)

    def sibling(self):
        return (self.section, 2 * self.chip + 1 - self.core)

    def across(self):
        return (1 - self.section, 2 * self.chip + self.core)

    def greet_late(self, early):
        barrier = pltpu.get_barrier_semaphore()
        near = (self.along(1), self.along(-1), self.sibling())
        for other in near:
            pl.semaphore_signal(barrier, inc=1, device_id=other, device_id_type=MESH)

        @pl.when(early)
        def _():
            pl.semaphore_wait(barrier, len(near))
            pl.semaphore_signal(barrier, inc=1, device_id=self.across(), device_id_type=MESH)

        @pl.when(jnp.logical_not(early))
        def _():
            pl.semaphore_wait(barrier, len(near) + 1)
            pl.semaphore_signal(barrier, inc=1, device_id=self.across(), device_id_type=MESH)

    def greet(self, *others):
        barrier = pltpu.get_barrier_semaphore()
        others = (self.along(1), self.along(-1), self.sibling()) + others
        for other in others:
            pl.semaphore_signal(barrier, inc=1, device_id=other, device_id_type=MESH)
        pl.semaphore_wait(barrier, len(others))


def remote(src, dst, send_sem, recv_sem, device):
    return pltpu.make_async_remote_copy(
        src_ref=src, dst_ref=dst, send_sem=send_sem, recv_sem=recv_sem,
        device_id=device, device_id_type=MESH,
    )


def hint(value, unit):
    return pl.multiple_of(value, unit)


PIECES = (
    ("second_a", 0, True),
    ("second_b", 1, True),
    ("first", 0, True),
    ("value", 0, False),
    ("out", 1, False),
    ("up", 0, False),
    ("down", 1, False),
    ("small", 0, True),
)
(FIRST_GAIN, FIRST_SHIFT, OUT_BIAS, SECOND_GAIN, SECOND_SHIFT, DOWN_BIAS, UP_BIAS, SYNTH_BIAS) = range(8)
vector_count = 8
up_row, synth_row = UP_BIAS, SYNTH_BIAS
section_axis, dp_axis = "section", "dp"
small_block = (8, 256)


def piece_view(refs, name, chip, core, section, sizes):
    rows, ff_rows, dense_rows, dense_cols, second_cols, chips = sizes
    who = 2 * chip + core
    if name in ("value", "out", "up"):
        return refs[name].at[pl.ds(hint(who * rows, rows), rows)]
    if name == "down":
        return refs[name].at[pl.ds(hint(who * ff_rows, ff_rows), ff_rows)]
    if name == "small":
        return refs[name].at[section, who]
    top = hint((section * chips + chip) * dense_rows, dense_rows)
    if name == "first":
        return refs[name].at[pl.ds(top, dense_rows), pl.ds(hint(core * dense_cols, dense_cols), dense_cols)]
    half = second_cols // 2
    left = core * second_cols + (half if name == "second_b" else 0)
    return refs["second"].at[pl.ds(top, dense_rows), pl.ds(hint(left, half), half)]


def gather_kernel(
    dp, sizes,
    value_in, out_in, up_in, down_in, first_in, second_in, *rest,
):
    vectors = rest[: vector_count]
    (
        value_ref, out_ref, up_ref, down_ref, first_ref, second_ref, table_ref,
        small_in, small_ref, first_wide, second_wide, first_stage, second_stage, wide_sems,         own_sems, ring_send, ring_recv, sib_send, sib_recv, across_send, across_recv, pass_send, pass_recv,
    ) = rest[vector_count :]
    rows, ff_rows, dense_rows, dense_cols, second_cols, chips = sizes
    place = Place(dp)
    reach = place.reach
    quarter = dense_rows // 2
    refs = dict(value=value_ref, out=out_ref, up=up_ref, down=down_ref, small=small_ref, first=first_ref, second=second_ref)
    half = second_cols // 2
    sources = dict(
        value=value_in, out=out_in, up=up_in, down=down_in, small=small_in, first=first_stage,
        second_a=second_stage.at[:, pl.ds(0, half)], second_b=second_stage.at[:, pl.ds(half, half)],
    )
    order = tuple(range(len(PIECES)))
    dense = tuple(i for i in order if PIECES[i][2])
    plain = tuple(i for i in order if not PIECES[i][2])

    def view(i, steps, section):
        return piece_view(refs, PIECES[i][0], place.chip_at(steps), place.core, section, sizes)

    def carried(i, way, step):
        return step < reach - 1 or (step == reach - 1 and PIECES[i][1] == way)

    def ring_copy(i, way, step):
        turn = 1 if way == 0 else -1
        target = view(i, -turn * step, place.section)
        source = sources[PIECES[i][0]] if step == 0 else target
        return remote(source, target, ring_send.at[way, step, i], ring_recv.at[way, step, i], place.along(turn))

    def slot(way, step):
        return 0 if step < 0 else 1 + 2 * step + way

    def sibling_copy(i, way, step):
        turn = 1 if way == 0 else -1
        target = view(i, -turn * (step + 1) if step >= 0 else 0, place.section)
        source = sources[PIECES[i][0]] if step < 0 else target
        at = slot(way, step)
        return remote(source, target, sib_send.at[at, i], sib_recv.at[at, i], place.sibling())

    def across_copy(i, way, step):
        turn = 1 if way == 0 else -1
        target = view(i, -turn * (step + 1) if step >= 0 else 0, place.section)
        source = sources[PIECES[i][0]] if step < 0 else target
        at = slot(way, step)
        return remote(source, target, across_send.at[at, i], across_recv.at[at, i], place.across())

    def pass_copy(i, way, step):
        turn = 1 if way == 0 else -1
        target = view(i, -turn * (step + 1) if step >= 0 else 0, 1 - place.section)
        at = slot(way, step)
        return remote(target, target, pass_send.at[at, i], pass_recv.at[at, i], place.sibling())

    def own_copy(i):
        return pltpu.make_async_copy(sources[PIECES[i][0]], view(i, 0, place.section), own_sems.at[i])

    def begin(i):
        for way in (0, 1):
            if carried(i, way, 0):
                ring_copy(i, way, 0).start()
        sibling_copy(i, 0, -1).start()
        if PIECES[i][2]:
            across_copy(i, 0, -1).start()
        own_copy(i).start()

    small_in[...] = jnp.zeros(small_block, jnp.float32)
    for row, ref in enumerate(vectors):
        small_in[row : row + 1, : ref.shape[1]] = ref[...].astype(jnp.float32)
    mine = hint(place.core * quarter, 8)
    first_wide[pl.ds(mine, quarter)] = first_in[...].astype(jnp.float32)
    second_wide[pl.ds(mine, quarter)] = second_in[...].astype(jnp.float32)
    place.greet(place.across())
    wide = [
        remote(ref.at[pl.ds(mine, quarter)], ref.at[pl.ds(mine, quarter)], wide_sems.at[0, n], wide_sems.at[1, n], place.sibling())
        for n, ref in enumerate((first_wide, second_wide))
    ]
    for copy in wide:
        copy.start()
    early = plain[:2]
    for i in early:
        begin(i)
    for copy in wide:
        copy.wait()
    first_stage[...] = first_wide[:, pl.ds(hint(place.core * dense_cols, dense_cols), dense_cols)].astype(jnp.bfloat16)
    second_stage[...] = second_wide[:, pl.ds(hint(place.core * second_cols, second_cols), second_cols)].astype(jnp.bfloat16)
    for i in dense + plain[len(early) :]:
        begin(i)

    events = [(i, way, step) for step in range(reach) for i in order for way in (0, 1) if carried(i, way, step)]
    crossing = [(i, 0, -1) for i in dense] + [e for e in events if e[0] in dense]
    passed = 0

    def pass_on(count):
        nonlocal passed
        while passed < min(count, len(crossing)):
            e = crossing[passed]
            across_copy(*e).wait_recv()
            pass_copy(*e).start()
            passed += 1

    for i, way, step in events:
        ring_copy(i, way, step).wait_recv()
        if carried(i, way, step + 1):
            ring_copy(i, way, step + 1).start()
        sibling_copy(i, way, step).start()
        if i in dense:
            across_copy(i, way, step).start()
        if i == order[-1] and way == 0:
            pass_on(len(dense) + 2 * len(dense) * step)
    pass_on(len(crossing))
    for i in order:
        own_copy(i).wait()
        sibling_copy(i, 0, -1).wait()
        for way in (0, 1):
            if carried(i, way, 0):
                ring_copy(i, way, 0).wait_send()
    for i, way, step in events:
        sibling_copy(i, way, step).wait()
        if step > 0:
            ring_copy(i, way, step).wait_send()
    for e in crossing:
        across_copy(*e).wait_send()
        pass_copy(*e).wait()
    shares = [ref.shape[1] for ref in vectors]
    share = shares[0]

    def side_by_side(blocks):
        return jnp.concatenate(blocks, axis=1)

    table_ref[:up_row, : dp * share] = side_by_side([small_ref[place.section, d, :up_row, :share] for d in range(dp)])
    up_share = shares[up_row]
    table_ref[up_row : up_row + 1, :] = side_by_side(
        [small_ref[place.section, d, up_row : up_row + 1, :up_share] for d in range(dp)]
    )
    synth_share = shares[synth_row]
    table_ref[synth_row : synth_row + 1, : 2 * dp * synth_share] = side_by_side(
        [small_ref[s, d, synth_row : synth_row + 1, :synth_share] for s in range(2) for d in range(dp)]
    )


def gather_weights(dp, value, out, up, down, first, second, vectors):
    rows, width = value.shape
    ff_rows = down.shape[0]
    ff = up.shape[1]
    chips = dp // 2
    dense_rows = 2 * first.shape[0]
    dense_cols = first.shape[1] // 2
    second_cols = second.shape[1] // 2
    sizes = (rows, ff_rows, dense_rows, dense_cols, second_cols, chips)
    reach = chips // 2
    count = len(PIECES)
    bf = jnp.bfloat16
    anywhere = pl.BlockSpec(memory_space=pl.ANY)
    inside = pl.BlockSpec(memory_space=pltpu.VMEM)
    dma = pltpu.SemaphoreType.DMA
    return pl.pallas_call(
        functools.partial(gather_kernel, dp, sizes),
        out_shape=(
            jax.ShapeDtypeStruct((rows * dp, width), bf),
            jax.ShapeDtypeStruct((rows * dp, width), bf),
            jax.ShapeDtypeStruct((rows * dp, ff), bf),
            jax.ShapeDtypeStruct((ff_rows * dp, width), bf),
            jax.ShapeDtypeStruct((2 * dp * first.shape[0], first.shape[1]), bf),
            jax.ShapeDtypeStruct((2 * dp * second.shape[0], second.shape[1]), bf),
            jax.ShapeDtypeStruct((vector_count, ff), jnp.float32),
        ),
        in_specs=[anywhere] * 4 + [inside] * (2 + len(vectors)),
        out_specs=[anywhere] * 6 + [inside],
        scratch_shapes=[
            pltpu.VMEM(small_block, jnp.float32),
            pltpu.VMEM((2, dp) + small_block, jnp.float32),
            pltpu.VMEM((dense_rows, 2 * dense_cols), jnp.float32),
            pltpu.VMEM((dense_rows, 2 * second_cols), jnp.float32),
            pltpu.VMEM((dense_rows, dense_cols), bf),
            pltpu.VMEM((dense_rows, second_cols), bf),
            dma((2, 2)),
            dma((count,)),
            dma((2, reach, count)),
            dma((2, reach, count)),
            dma((1 + 2 * reach, count)),
            dma((1 + 2 * reach, count)),
            dma((1 + 2 * reach, count)),
            dma((1 + 2 * reach, count)),
            dma((1 + 2 * reach, count)),
            dma((1 + 2 * reach, count)),
        ],
        compiler_params=pltpu.CompilerParams(
            collective_id=0, has_side_effects=True, vmem_limit_bytes=63 << 20
        ),
        name="gather_weights",
    )(value, out, up, down, first, second, *vectors)


def store_sum(target, terms, rows):
    if rows == 0:
        total = terms[0][...]
        for term in terms[1:]:
            total = total + term[...]
        target[...] = total
        return

    def some(n, carry):
        at = pl.ds(pl.multiple_of(n * 16, 16), 16)
        total = terms[0][at, :].astype(jnp.float32)
        for term in terms[1:]:
            total = total + term[at, :].astype(jnp.float32)
        target[at, :] = total.astype(target.dtype)
        return carry

    lax.fori_loop(0, rows // 16, some, 0)


def reduce_kernel(dp, sizes, shares, tables, value_in, out_in, up_in, down_in, first_in, second_in, random_in, *rest):
    dense_tables, random_tables = rest[:tables], rest[tables : 2 * tables]
    (
    value_ref, out_ref, up_ref, down_ref, small_ref, first_ref, second_ref, random_ref,
    small_in, own_value, own_out, own_up, own_down, own_small, own_first, own_second,
    sib_value, sib_out, sib_up, sib_down, sib_small, sib_first, sib_second,
    ring_value, ring_out, ring_up, ring_down, ring_small, ring_first, ring_second,
    across_small, across_first, across_second, first_wide, second_wide, first_part, second_part,
    own_sems, sib_send, sib_recv, ring_send, ring_recv, across_send, across_recv, wide_sems,
    random_sems, turn_send, turn_recv, pass_send, pass_recv,
    ) = rest[2 * tables :]
    rows, ff_rows, dense_rows, dense_cols, second_cols, chips = sizes
    place = Place(dp)
    reach = place.reach
    half = second_cols // 2
    quarter = dense_rows // 2
    is_dense = place.section == 0
    full = dict(value=value_in, out=out_in, up=up_in, down=down_in, small=small_in, first=first_in, second=second_in)
    own = dict(value=own_value, out=own_out, up=own_up, down=own_down, small=own_small, first=own_first, second=own_second)
    sib = dict(value=sib_value, out=sib_out, up=sib_up, down=sib_down, small=sib_small, first=sib_first, second=sib_second)
    ring = dict(value=ring_value, out=ring_out, up=ring_up, down=ring_down, small=ring_small, first=ring_first, second=ring_second)
    crossed = dict(first=across_first, second=across_second, small=across_small)
    order = tuple(range(len(PIECES)))
    small = len(PIECES) - 1
    crossing = tuple(i for i in order if PIECES[i][2])
    dense = crossing[:-1]
    plain = tuple(i for i in order if not PIECES[i][2])
    piece_rows = dict(value=rows, out=rows, up=rows, down=ff_rows, small=0, first=dense_rows, second_a=dense_rows, second_b=dense_rows)
    away = (reach,) + tuple(o for t in range(reach - 1, 0, -1) for o in (t, -t)) + (0,)
    spot_of = {o: n for n, o in enumerate(away)}
    spot_of[-reach] = 0

    def part(table, i, *at):
        name = PIECES[i][0]
        if name == "second_a":
            return table["second"].at[(*at, slice(None), pl.ds(0, half))]
        if name == "second_b":
            return table["second"].at[(*at, slice(None), pl.ds(half, half))]
        return table[name].at[at]

    def held(table, i, o, plane):
        spot = spot_of[o]
        return part(table, i, plane, spot) if PIECES[i][2] else part(table, i, spot)

    def source(i, o, core, plane):
        section = place.section if plane == 0 else 1 - place.section
        return piece_view(full, PIECES[i][0], place.chip_at(o), core, section, sizes)

    def load(i, o, plane):
        return pltpu.make_async_copy(
            source(i, o, place.core, plane), held(own, i, o, plane), own_sems.at[plane, spot_of[o], i]
        )

    def lend(i, o, plane):
        at = (plane, spot_of[o], i)
        return remote(source(i, o, 1 - place.core, plane), held(sib, i, o, plane), sib_send.at[at], sib_recv.at[at], place.sibling())

    def ring_copy(i, way, step):
        turn = 1 if way == 0 else -1
        o = turn * (reach - step)
        return remote(held(own, i, o, 0), part(ring, i, way, step), ring_send.at[way, step, i], ring_recv.at[way, step, i], place.along(turn))

    def across_copy(i, o):
        at = (spot_of[o], i)
        return remote(held(own, i, o, 1), part(crossed, i, spot_of[o]), across_send.at[at], across_recv.at[at], place.across())

    def carried(i, way, step):
        return step > 0 or PIECES[i][1] == way

    def local_terms(i, o):
        load(i, o, 0).wait()
        lend(i, o, 0).wait_recv()
        return [held(own, i, o, 0), held(sib, i, o, 0)]

    def total(target, i, o, arrived):
        if i == small:
            terms = local_terms(i, o) + arrived

            @pl.when(is_dense)
            def _():
                store_sum(target, terms, 0)

            @pl.when(jnp.logical_not(is_dense))
            def _():
                across_copy(i, o).wait_recv()
                store_sum(target, terms + [part(crossed, i, spot_of[o])], 0)
        elif PIECES[i][2]:

            @pl.when(is_dense)
            def _():
                store_sum(target, local_terms(i, o) + arrived, piece_rows[PIECES[i][0]])

            @pl.when(jnp.logical_not(is_dense))
            def _():
                across_copy(i, o).wait_recv()
                store_sum(target, [part(crossed, i, spot_of[o])] + arrived, piece_rows[PIECES[i][0]])
        else:
            store_sum(target, local_terms(i, o) + arrived, piece_rows[PIECES[i][0]])

    def arrivals(i, o):
        ways = (0, 1) if o == 0 else ((0,) if o > 0 else (1,))
        found = []
        for way in ways:
            step = reach - abs(o) - 1
            if step >= 0 and carried(i, way, step):
                ring_copy(i, way, step).wait_recv()
                found.append(part(ring, i, way, step))
        return found

    small_in[...] = jnp.zeros(small_in.shape, jnp.float32)

    def blocks_of(got, section, names):
        whole = got[0][...]
        for more in got[1:]:
            whole = whole + more[...]
        for d in range(dp):
            if names:
                share = shares[0]
                small_in[section, d, :up_row, :share] = whole[:up_row, d * share : (d + 1) * share]
                share = shares[up_row]
                small_in[section, d, up_row : up_row + 1, :share] = whole[up_row : up_row + 1, d * share : (d + 1) * share]
            if got is dense_tables:
                share = shares[synth_row]
                left = (section * dp + d) * share
                small_in[section, d, synth_row : synth_row + 1, :share] = whole[synth_row : synth_row + 1, left : left + share]

    @pl.when(is_dense)
    def _():
        blocks_of(dense_tables, 0, True)
        blocks_of(dense_tables, 1, False)

    @pl.when(jnp.logical_not(is_dense))
    def _():
        blocks_of(random_tables, 1, True)

    place.greet_late(jnp.logical_not(is_dense))
    for o in away:
        for i in plain + (small,):
            lend(i, o, 0).start()
            load(i, o, 0).start()

        @pl.when(is_dense)
        def _():
            for plane in (1, 0):
                for i in dense + ((small,) if plane == 1 else ()):
                    lend(i, o, plane).start()
                    load(i, o, plane).start()

    block = random_ref.shape[0] // (2 * chips)
    strip = block // 2

    def view(i, o, core):
        top = (core * chips + place.chip_at(o)) * block + i * strip
        return random_ref.at[pl.ds(pl.multiple_of(top, strip), strip)]

    def spread(i, way, step):
        return step < reach - 1 or i == way

    def turn_copy(i, way, step):
        turn = 1 if way == 0 else -1
        target = view(i, -turn * step, place.core)
        source = random_in.at[pl.ds(i * strip, strip)] if step == 0 else target
        return remote(source, target, turn_send.at[way, step, i], turn_recv.at[way, step, i], place.along(turn))

    def pass_copy(i, way, step):
        turn = 1 if way == 0 else -1
        target = view(i, -turn * (step + 1) if step >= 0 else 0, place.core)
        source = random_in.at[pl.ds(i * strip, strip)] if step < 0 else target
        at = 0 if step < 0 else 1 + 2 * step + way
        return remote(source, target, pass_send.at[at, i], pass_recv.at[at, i], place.sibling())

    def keep_copy(i):
        return pltpu.make_async_copy(random_in.at[pl.ds(i * strip, strip)], view(i, 0, place.core), random_sems.at[1, 1, i])

    def across_strip(o, device, way):
        top = pl.multiple_of((place.core * chips + place.chip_at(o)) * block, block)
        part_of = random_ref.at[pl.ds(top, block)]
        return remote(part_of, part_of, random_sems.at[way, 0, 2 + spot_of[o]], random_sems.at[way, 1, 2 + spot_of[o]], device)

    events = [(i, way, step) for step in range(reach) for i in (0, 1) for way in (0, 1) if spread(i, way, step)]

    @pl.when(jnp.logical_not(is_dense))
    def _():
        for i in (0, 1):
            for way in (0, 1):
                if spread(i, way, 0):
                    turn_copy(i, way, 0).start()
            pass_copy(i, 0, -1).start()
            keep_copy(i).start()
        for i, way, step in events:
            turn_copy(i, way, step).wait_recv()
            if step + 1 < reach and spread(i, way, step + 1):
                turn_copy(i, way, step + 1).start()
            pass_copy(i, way, step).start()
        for i in (0, 1):
            keep_copy(i).wait()
        pl.semaphore_wait(pltpu.get_barrier_semaphore(), 1)
        for o in away:
            across_strip(o, place.across(), 0).start()

    def cross(o):
        @pl.when(is_dense)
        def _():
            for i in crossing:
                load(i, o, 1).wait()
                lend(i, o, 1).wait_recv()
                store_sum(held(own, i, o, 1), [held(own, i, o, 1), held(sib, i, o, 1)], piece_rows[PIECES[i][0]])
                across_copy(i, o).start()

    for step in range(reach):
        for i in plain + crossing:
            for way in (0, 1):
                if carried(i, way, step):
                    o = (reach - step) * (1 if way == 0 else -1)
                    total(held(own, i, o, 0), i, o, arrivals(i, o))
                    ring_copy(i, way, step).start()
            if i == plain[-1]:
                for o in away[(0 if step == 0 else 2 * step - 1) : 2 * step + 1]:
                    cross(o)
    cross(0)

    @pl.when(is_dense)
    def _():
        for o in away:
            across_strip(o, place.across(), 0).wait_recv()
            across_strip(o, place.sibling(), 1).start()

    outs = dict(value=value_ref, out=out_ref, up=up_ref, down=down_ref, small=small_ref)
    for i in plain + (small,):
        total(outs[PIECES[i][0]], i, 0, arrivals(i, 0))
    wides = dict(first=first_wide, second_a=second_wide.at[:, pl.ds(0, half)], second_b=second_wide.at[:, pl.ds(half, half)])
    for i in dense:
        total(wides[PIECES[i][0]], i, 0, arrivals(i, 0))
    mine = pl.multiple_of(place.core * quarter, 8)
    theirs = pl.multiple_of((1 - place.core) * quarter, 8)
    last = [
        remote(wide.at[pl.ds(theirs, quarter)], got, wide_sems.at[0, n], wide_sems.at[1, n], place.sibling())
        for n, (wide, got) in enumerate(((first_wide, first_part), (second_wide, second_part)))
    ]
    for copy in last:
        copy.start()
    for copy in last:
        copy.wait()
    for ref, wide, got, cols in ((first_ref, first_wide, first_part, dense_cols), (second_ref, second_wide, second_part, second_cols)):
        ref[:, pl.ds(pl.multiple_of(place.core * cols, cols), cols)] = wide[pl.ds(mine, quarter), :]
        ref[:, pl.ds(pl.multiple_of((1 - place.core) * cols, cols), cols)] = got[...]

    for o in away:
        for i in plain + (small,):
            lend(i, o, 0).wait_send()

        @pl.when(is_dense)
        def _():
            for i in dense:
                lend(i, o, 0).wait_send()
            for i in crossing:
                lend(i, o, 1).wait_send()
                across_copy(i, o).wait_send()

    @pl.when(is_dense)
    def _():
        for o in away:
            across_strip(o, place.sibling(), 1).wait()

    @pl.when(jnp.logical_not(is_dense))
    def _():
        for o in away:
            across_strip(o, place.across(), 0).wait_send()
        for i in (0, 1):
            pass_copy(i, 0, -1).wait()
            for way in (0, 1):
                for step in range(reach):
                    if spread(i, way, step):
                        turn_copy(i, way, step).wait_send()
        for e in events:
            pass_copy(*e).wait()

    for step in range(reach):
        for i in order:
            for way in (0, 1):
                if carried(i, way, step):
                    ring_copy(i, way, step).wait_send()


def reduce_grads(dp, value, out, up, down, first, second, random, dense_tables, random_tables, shares):
    chips = dp // 2
    rows, width = value.shape[0] // dp, value.shape[1]
    ff_rows = down.shape[0] // dp
    ff = up.shape[1]
    dense_rows = first.shape[0] // dp
    dense_cols = first.shape[1] // 2
    second_cols = second.shape[1] // 2
    sizes = (rows, ff_rows, dense_rows, dense_cols, second_cols, chips)
    reach = chips // 2
    count = len(PIECES)
    bf, f32 = jnp.bfloat16, jnp.float32
    anywhere = pl.BlockSpec(memory_space=pl.ANY)
    inside = pl.BlockSpec(memory_space=pltpu.VMEM)
    dma = pltpu.SemaphoreType.DMA
    blocks = ((rows, width), (rows, width), (rows, ff), (ff_rows, width))
    wide = ((dense_rows, dense_cols), (dense_rows, second_cols))
    scratch = [pltpu.VMEM((2, dp) + small_block, f32)]
    for _ in range(2):
        scratch += [pltpu.VMEM((chips,) + b, bf) for b in blocks]
        scratch += [pltpu.VMEM((2, chips) + small_block, f32)]
        scratch += [pltpu.VMEM((2, chips) + w, bf) for w in wide]
    scratch += [pltpu.VMEM((2, reach) + b, bf) for b in blocks]
    scratch += [pltpu.VMEM((2, reach) + small_block, f32)]
    scratch += [pltpu.VMEM((2, reach) + w, bf) for w in wide]
    scratch += [pltpu.VMEM((chips,) + small_block, f32)]
    scratch += [pltpu.VMEM((chips,) + w, bf) for w in wide]
    scratch += [pltpu.VMEM(w, f32) for w in wide]
    scratch += [pltpu.VMEM((dense_rows // 2, w[1]), f32) for w in wide]
    scratch += [
        dma((2, chips, count)),
        dma((2, chips, count)),
        dma((2, chips, count)),
        dma((2, reach, count)),
        dma((2, reach, count)),
        dma((chips, count)),
        dma((chips, count)),
        dma((2, 2)),
        dma((2, 2, 2 + chips)),
        dma((2, reach, 2)),
        dma((2, reach, 2)),
        dma((1 + 2 * reach, 2)),
        dma((1 + 2 * reach, 2)),
    ]
    tables = len(dense_tables)
    return pl.pallas_call(
        functools.partial(reduce_kernel, dp, sizes, shares, tables),
        out_shape=tuple(jax.ShapeDtypeStruct(b, f32) for b in blocks + (small_block,))
        + (
            jax.ShapeDtypeStruct((dense_rows // 2, first.shape[1]), f32),
            jax.ShapeDtypeStruct((dense_rows // 2, second.shape[1]), f32),
            jax.ShapeDtypeStruct((dp * random.shape[0], random.shape[1]), bf),
        ),
        in_specs=[anywhere] * 7 + [inside] * (2 * tables),
        out_specs=[inside] * 7 + [anywhere],
        scratch_shapes=scratch,
        compiler_params=pltpu.CompilerParams(
            collective_id=1, has_side_effects=True, vmem_limit_bytes=63 << 20
        ),
        name="reduce_grads",
    )(value, out, up, down, first, second, random, *dense_tables, *random_tables)


norm_eps = 1e-05
masked_score = -1e30
gelu_scale = 0.7978845608028654
gelu_cube = 0.044715
bf16, f32 = jnp.bfloat16, jnp.float32


def dot_rows(a, b):
    return lax.dot_general(a, b, (((1,), (0,)), ((), ())), preferred_element_type=f32)


def dot_back(a, b):
    return lax.dot_general(a, b, (((1,), (1,)), ((), ())), preferred_element_type=f32)


def dot_down(a, b):
    return lax.dot_general(a, b, (((0,), (0,)), ((), ())), preferred_element_type=f32)


def gelu_tanh(v):
    return jnp.tanh(gelu_scale * (v + gelu_cube * (v * v * v)))


def gelu(v):
    return 0.5 * v * (1.0 + gelu_tanh(v))


def gelu_both(v):
    t = gelu_tanh(v)
    value = 0.5 * v * (1.0 + t)
    slope = 0.5 * (1.0 + t) + 0.5 * v * (1.0 - t * t) * (gelu_scale * (1.0 + 3.0 * gelu_cube * (v * v)))
    return value, slope


def standard(v):
    centre = v - jnp.mean(v, axis=-1, keepdims=True)
    inverse = lax.rsqrt(jnp.mean(centre * centre, axis=-1, keepdims=True) + norm_eps)
    return centre * inverse, inverse


def standard_back(unit, inverse, grad):
    middle = jnp.mean(grad, axis=-1, keepdims=True)
    slant = jnp.mean(grad * unit, axis=-1, keepdims=True)
    return inverse * (grad - middle - unit * slant)


def column_sum(v):
    return jnp.sum(v.astype(f32), axis=0, keepdims=True)


class Bench:
    def __init__(self, **refs):
        self.__dict__.update(refs)
        self.waiting = {}
        self.used = 0
        self.sent = []
        self.last_tiles = []

    def vector(self, name, at):
        row = name
        return self.vectors[row : row + 1, at]

    def put_vector(self, name, at, value):
        row = name
        self.vector_grads[row : row + 1, at] = value

    def fetch(self, name, source, target):
        copy = pltpu.make_async_copy(source, target, self.sems.at[self.used])
        self.used += 1
        copy.start()
        self.waiting[name] = copy

    def need(self, *names):
        for name in names:
            copy = self.waiting.pop(name, None)
            if copy is not None:
                copy.wait()

    def send(self, source, target):
        copy = pltpu.make_async_copy(source, target, self.sems.at[self.used])
        self.used += 1
        copy.start()
        self.sent.append(copy)

    def settle(self):
        for copy in self.last_tiles:
            copy.wait()
        self.last_tiles = []

    def finish(self):
        self.settle()
        for copy in self.sent:
            copy.wait()

    def plan(self, added, *grads):
        self.added = added
        self.planned = list(grads)
        self.ahead()

    def tile_copies(self, grad, cols):
        across = grad.shape[1] // cols
        count = grad.shape[0] // unit_cols * across

        def place(t):
            top = pl.multiple_of(t // across * unit_cols, unit_cols)
            left = pl.multiple_of(lax.rem(t, across) * cols, cols)
            return grad.at[pl.ds(top, unit_cols), pl.ds(left, cols)]

        def result(t):
            slot = lax.rem(t, tile_slots)
            return pltpu.make_async_copy(self.stage.at[slot, :, pl.ds(0, cols)], place(t), self.stage_sems.at[slot])

        def prior(t):
            slot = lax.rem(t, tile_slots)
            return pltpu.make_async_copy(place(t), self.prior_stage.at[slot, :, pl.ds(0, cols)], self.prior_sems.at[slot])

        return count, across, result, prior

    def ahead(self):
        if self.added and self.planned:
            count, _, _, prior = self.tile_copies(*self.planned[0])
            for t in range(min(count, tile_slots - 1)):
                prior(t).start()

    def emit(self, tile):
        grad, cols = self.planned.pop(0)
        added = self.added
        count, across, result, prior = self.tile_copies(grad, cols)
        reach = tile_slots - 1
        self.settle()

        def turn(t, carry):
            slot = lax.rem(t, tile_slots)
            if added:

                @pl.when(t + reach < count)
                def _():
                    prior(t + reach).start()

                prior(t).wait()

            @pl.when(t >= tile_slots)
            def _():
                result(t - tile_slots).wait()

            def write(value, lanes=None):
                at = (slot, slice(None), pl.ds(0, cols) if lanes is None else lanes)
                if value is None:
                    self.stage[at] = self.prior_stage[at] if added else jnp.zeros((unit_cols, lanes.size), bf16)
                else:
                    if added:
                        value = value + self.prior_stage[at].astype(f32)
                    self.stage[at] = value.astype(bf16)

            tile(t // across, lax.rem(t, across), write)
            result(t).start()
            return carry

        lax.fori_loop(0, count, turn, 0)
        self.last_tiles = [result(t) for t in range(max(0, count - tile_slots), count)]
        self.ahead()


tile_slots = 6
unit_cols = 256
unit_rows = 128


def cols_at(t):
    return pl.ds(pl.multiple_of(t * unit_cols, unit_cols), unit_cols)


def by_cols(loose, n, extent, body):
    def turn(t, carry):
        body(pl.ds(0, n), cols_at(t), t)
        return carry

    count = extent // unit_cols
    lax.fori_loop(0, count, turn, 0, unroll=(3 if count == 3 else 2) if loose and count % 6 in (0, 3) else 1)


def by_rows(n, body, start=0):
    def turn(t, carry):
        return body(pl.ds(pl.multiple_of(t * unit_rows, unit_rows), unit_rows), carry)

    return lax.fori_loop(0, n // unit_rows, turn, start, unroll=2)


def lanes_of_first(n, size):
    return lax.broadcasted_iota(jnp.int32, (n, 2 * size), 1) < size


def send_padded(b, n, **targets):
    for name, target in targets.items():
        ref = getattr(b, name)
        if n < b.slots:
            ref[n:] = jnp.zeros((b.slots - n, ref.shape[1]), bf16)
        b.send(ref, target)


def softmax(b, n, scores):
    if n < b.slots:
        scores = jnp.where(in_item(b, (n, n), 1), scores, masked_score)
    e = jnp.exp(scores - jnp.max(scores, axis=-1, keepdims=True))
    return (e * (1.0 / jnp.sum(e, axis=-1, keepdims=True))).astype(bf16)


def forward_part(b, n, dense):
    width, ff, heads, slots = b.width, b.ff, b.heads, b.slots
    size = width // heads
    whole = slice(0, width)
    rows = pl.ds(0, n)
    loose = not dense and n < slots

    def first_norm(at, carry):
        unit, _ = standard(b.x[at, :].astype(f32))
        b.a[at, :] = (unit * b.vector(FIRST_GAIN, whole) + b.vector(FIRST_SHIFT, whole)).astype(bf16)
        return carry

    b.need("x")
    by_rows(n, first_norm)
    if dense:
        b.need("first")

        def hidden(rows, at, t):
            p = dot_rows(b.a[rows], b.first[:, at]) + b.vector(SYNTH_BIAS, at)
            b.p[rows, at] = p
            b.s[rows, at] = gelu(p).astype(bf16)

        by_cols(loose, n, width, hidden)
        b.send(b.p.at[rows], b.p_out.at[rows])
    b.need("value")

    def project(rows, at, t):
        b.v[rows, at] = dot_rows(b.a[rows], b.value[:, at]).astype(bf16)

    by_cols(loose, n, width, project)
    b.need("second" if dense else "att")

    def pair(i, carry):
        here = pl.ds(pl.multiple_of(i * 2 * size, 2 * size), 2 * size)
        values = b.v[:n, here]
        got = []
        for j in range(2):
            h = 2 * i + j
            if dense:
                scores = dot_rows(b.s[:n], b.second[:, pl.ds(pl.multiple_of(h * slots, slots), n)])
                b.att[h, :n, :n] = softmax(b, n, scores)
            got.append(dot_rows(b.att[h, :n, :n], values))
        b.o[:n, here] = jnp.where(lanes_of_first(n, size), got[0], got[1]).astype(bf16)
        return carry

    lax.fori_loop(0, heads // 2, pair, 0, unroll=1)
    if dense:
        b.send(b.att.at[:, rows, rows], b.att_out.at[:, rows, rows])
        b.send(b.v.at[rows], b.v_out.at[rows])
        b.send(b.o.at[rows], b.o_out.at[rows])
    b.need("out")

    def branch(rows, at, t):
        b.y[rows, at] = b.x[rows, at].astype(f32) + (dot_rows(b.o[rows], b.out[:, at]) + b.vector(OUT_BIAS, at))

    by_cols(loose, n, width, branch)
    if dense:
        b.send(b.y.at[rows], b.y_out.at[rows])

    def second_norm(at, carry):
        unit, _ = standard(b.y[at, :])
        b.u[at, :] = (unit * b.vector(SECOND_GAIN, whole) + b.vector(SECOND_SHIFT, whole)).astype(bf16)
        return carry

    by_rows(n, second_norm)
    b.need("up")

    def up(rows, at, t):
        m = dot_rows(b.u[rows], b.up[:, at]) + b.vector(UP_BIAS, at)
        b.m[rows, at] = m.astype(b.m.dtype)
        b.r[rows, at] = gelu(m).astype(bf16)

    by_cols(loose, n, ff, up)
    if dense:
        b.send(b.m.at[rows], b.m_out.at[rows])
    b.need("down")

    def down(rows, at, t):
        z = b.y[rows, at] + (dot_rows(b.r[rows], b.down[:, at]) + b.vector(DOWN_BIAS, at))
        if n < slots:
            z = jnp.where(in_item(b, (n, unit_cols), 0), z, 0.0)
        b.z[rows, at] = z.astype(bf16)

    by_cols(loose, n, width, down)
    if n < slots:
        b.z[n:] = jnp.zeros((slots - n, width), bf16)
    b.send(b.z, b.states.at[b.item])
    if dense:
        b.send(b.z, b.z_out)
    else:
        send_padded(b, n, r=b.r_out, o=b.o_out, a=b.a_out)


def plan_grads(b, added):
    wide = 2 * b.width
    b.plan(
        added, (b.down_grad, b.width), (b.up_grad, wide), (b.out_grad, b.width), (b.value_grad, b.width),
        (b.second_grad, wide), (b.first_grad, b.width),
    )


def random_copies(b, n):
    part = pl.ds(0, n)

    def prior(i):
        slot = lax.rem(i, 2)
        return pltpu.make_async_copy(
            b.random_grad.at[pl.ds(2 * i, 2), part, part], b.random_old.at[slot, :, part, part], b.random_sems.at[0, slot]
        )

    def result(i):
        slot = lax.rem(i, 2)
        return pltpu.make_async_copy(
            b.random_stage.at[slot, :, part, part], b.random_grad.at[pl.ds(2 * i, 2), part, part], b.random_sems.at[1, slot]
        )

    return prior, result


def backward_part(b, n, dense, added):
    width, ff, heads, slots = b.width, b.ff, b.heads, b.slots
    size = width // heads
    wide = 2 * width
    whole = slice(0, width)
    loose = not dense and n < slots
    b.need("c", "m", "down")
    if not dense and n < slots:
        b.c[:n] = jnp.where(in_item(b, (n, width), 0), b.c[:n], jnp.zeros((), bf16))

    def down_rows(rows, at, t):
        dr = dot_back(b.c[rows], b.down_rows(t))
        value, slope = gelu_both(b.m[rows, at].astype(f32))
        gm = (slope * dr).astype(bf16)
        b.gm[rows, at] = gm
        b.put_vector(UP_BIAS, at, column_sum(gm))
        return value

    def down_tile(t, _, write):
        value = down_rows(pl.ds(0, n), cols_at(t), t)
        write(dot_down(value.astype(bf16), b.c[:n]))

    if dense:
        b.emit(down_tile)
    else:
        by_cols(loose, n, ff, down_rows)
        send_padded(b, n, gm=b.gm_out, c=b.c_out)
    b.need("up", "y")

    def up_back(rows, at, t):
        b.wide[rows, at] = dot_back(b.gm[rows], b.up[at, :ff])

    by_cols(loose, n, width, up_back)
    if dense:
        b.fetch("second", b.second_in, b.up)
    none = jnp.zeros((1, width), f32)

    def second_back(at, carry):
        unit, inverse = standard(b.y[at, :])
        gain = b.vector(SECOND_GAIN, whole)
        b.u[at, :] = (unit * gain + b.vector(SECOND_SHIFT, whole)).astype(bf16)
        du = b.wide[at, :]
        gf = b.c[at, :].astype(f32)
        gy = gf + standard_back(unit, inverse, du * gain)
        b.gy[at, :] = gy
        gb = gy.astype(bf16)
        b.gb[at, :] = gb
        found = (column_sum(du * unit), column_sum(du), column_sum(gb), column_sum(gf))
        return tuple(a + f for a, f in zip(carry, found))

    sums = by_rows(n, second_back, (none,) * 4)
    for name, total in zip((SECOND_GAIN, SECOND_SHIFT, OUT_BIAS, DOWN_BIAS), sums):
        b.put_vector(name, whole, total)
    if dense:
        b.emit(
            lambda t, s, write: write(dot_down(b.u[:n, cols_at(t)], b.gm[:n, pl.ds(pl.multiple_of(s * wide, wide), wide)])),
        )
    else:
        send_padded(b, n, u=b.u_out, gb=b.gb_out)
    b.need("o", "out")
    if dense:
        b.emit(lambda t, s, write: write(dot_down(b.o[:n, cols_at(t)], b.gb[:n])))

    def out_back(rows, at, t):
        b.go[rows, at] = dot_back(b.gb[rows], b.out[at, :]).astype(bf16)

    by_cols(loose, n, width, out_back)
    b.need("v", "att")

    def pair_back(i, keep):
        here = pl.ds(pl.multiple_of(i * 2 * size, 2 * size), 2 * size)
        values, grads = b.v[:n, here], b.go[:n, here]
        first = lanes_of_first(n, size)
        got = []
        for j in range(2):
            own = jnp.where(first if j == 0 else jnp.logical_not(first), grads, jnp.zeros_like(grads))
            weight = b.att[2 * i + j, :n, :n]
            mixed = weight.astype(f32) * dot_back(own, values)
            keep(2 * i + j, j, mixed - weight.astype(f32) * jnp.sum(mixed, axis=-1, keepdims=True))
            got.append(dot_down(weight, grads))
        b.gv[:n, here] = jnp.where(first, got[0], got[1]).astype(bf16)

    if dense:

        def keep_dense(h, j, ds):
            b.gs[:n, pl.ds(pl.multiple_of(h * slots, slots), n)] = ds.astype(bf16)

        def loop(i, carry):
            pair_back(i, keep_dense)
            return carry

        lax.fori_loop(0, heads // 2, loop, 0)
    else:

        prior, result = random_copies(b, n if added else slots)

        def loop(i, carry):
            slot = lax.rem(i, 2)
            if added:

                @pl.when(i + 1 < heads // 2)
                def _():
                    prior(i + 1).start()

                prior(i).wait()

            @pl.when(i >= 2)
            def _():
                result(i - 2).wait()

            def keep_random(h, j, ds):
                if added:
                    ds = ds + b.random_old[slot, j, :n, :n].astype(f32)
                elif n < slots:
                    b.random_stage[slot, j] = jnp.zeros((slots, slots), bf16)
                b.random_stage[slot, j, :n, :n] = ds.astype(bf16)

            pair_back(i, keep_random)
            result(i).start()
            return carry

        lax.fori_loop(0, heads // 2, loop, 0)
        for i in (heads // 2 - 2, heads // 2 - 1):
            result(i).wait()
    b.need("x")
    if dense:

        def first_norm(at, carry):
            unit, _ = standard(b.x[at, :].astype(f32))
            b.a[at, :] = (unit * b.vector(FIRST_GAIN, whole) + b.vector(FIRST_SHIFT, whole)).astype(bf16)
            return carry

        by_rows(n, first_norm)
        b.emit(lambda t, s, write: write(dot_down(b.a[:n, cols_at(t)], b.gv[:n])))
    else:
        send_padded(b, n, gv=b.gv_out)
    if dense:
        b.need("p")

        def slopes(rows, at, t):
            value, slope = gelu_both(b.p[rows, at])
            b.s[rows, at] = value.astype(bf16)
            b.wide[rows, at] = slope

        by_cols(loose, n, width, slopes)
        group = wide // slots

        def second_tile(t, s, write):
            tile = b.s[:n, cols_at(t)]
            if n == slots:
                write(dot_down(tile, b.gs[:n, pl.ds(pl.multiple_of(s * wide, wide), wide)]))
                return
            for q in range(group):
                left = pl.multiple_of(s * wide + q * slots, slots)
                write(dot_down(tile, b.gs[:n, pl.ds(left, n)]), pl.ds(q * slots, n))
                write(None, pl.ds(q * slots + n, slots - n))

        b.emit(second_tile)
        b.need("second")

        def hidden_back(rows, at, t):
            if n == slots:
                hidden = dot_back(b.gs[rows], b.up[at, :])
            else:
                hidden = jnp.zeros((rows.size, unit_cols), f32)
                for h in range(heads):
                    part = slice(h * slots, h * slots + n)
                    hidden = hidden + dot_back(b.gs[rows, part], b.up[at, part])
            gp = (b.wide[rows, at] * hidden).astype(bf16)
            b.gp[rows, at] = gp
            b.put_vector(SYNTH_BIAS, at, column_sum(gp))

        by_cols(loose, n, width, hidden_back)
        b.emit(lambda t, s, write: write(dot_down(b.a[:n, cols_at(t)], b.gp[:n])))
    b.need("value", "first")

    def normed_back(rows, at, t):
        ga = dot_back(b.gv[rows], b.value[at, :])
        if dense:
            ga = ga + dot_back(b.gp[rows], b.first[at, :])
        b.wide[rows, at] = ga

    by_cols(loose, n, width, normed_back)

    def first_back(at, carry):
        unit, inverse = standard(b.x[at, :].astype(f32))
        ga = b.wide[at, :]
        dx = b.gy[at, :] + standard_back(unit, inverse, ga * b.vector(FIRST_GAIN, whole))
        b.dx[at, :] = dx.astype(bf16)
        return carry[0] + column_sum(ga * unit), carry[1] + column_sum(ga)

    sums = by_rows(n, first_back, (none,) * 2)
    b.put_vector(FIRST_GAIN, whole, sums[0])
    b.put_vector(FIRST_SHIFT, whole, sums[1])
    if n < slots:
        b.dx[n:] = jnp.zeros((slots - n, width), bf16)
    if not dense:
        b.send(b.dx, b.dx_out)
    b.send(b.dx, b.grads_in.at[b.item])
    b.send(b.vector_grads, b.table_out)


def item_of(lengths, turn):
    if lengths.shape[0] == 2:
        return jnp.where(lengths[1] < lengths[0], 1 - turn, turn)
    return jnp.int32(turn)


def by_length(section, lengths, turn, slots, call, long_late=False):
    long = lengths[item_of(lengths, turn)] > slots // 2
    if turn == 0 and not long_late:
        branches, which = (slots, slots // 2, 0), jnp.where(long, 0, 1)
    else:
        branches, which = (slots // 2, slots, 0), jnp.where(long, 1, 0)
    which = jnp.where(lax.axis_index(section_axis) == section, which, 2)
    return lax.switch(which, [functools.partial(call, n) for n in branches])


def in_item(b, shape, axis):
    return lax.broadcasted_iota(jnp.int32, shape, axis) < b.length


def shape_of(table):
    slots, width = table.x.shape
    return dict(width=width, ff=table.m.shape[1], heads=table.att.shape[0], slots=slots)


class ForwardRefs(NamedTuple):
    lengths: Any
    vectors: Any
    x_in: Any
    first_in: Any
    second_in: Any
    value_in: Any
    out_in: Any
    up_in: Any
    down_in: Any
    states: Any
    z_out: Any
    p_out: Any
    att_out: Any
    v_out: Any
    o_out: Any
    y_out: Any
    m_out: Any
    x: Any
    first: Any
    second: Any
    value: Any
    out: Any
    up: Any
    down: Any
    z: Any
    p: Any
    att: Any
    v: Any
    o: Any
    y: Any
    m: Any
    a: Any
    s: Any
    u: Any
    r: Any
    sems: Any


def dense_forward_kernel(n, turn, *refs):
    if n == 0:
        return
    refs = refs[:9] + refs[9 + (turn > 0) :]
    table = ForwardRefs(*refs)
    shape = shape_of(table)

    item = item_of(table.lengths, turn)
    b = Bench(item=item, length=table.lengths[item], **table._asdict(), **shape)
    rows = pl.ds(0, n)
    b.fetch("x", b.x_in.at[item, rows], b.x.at[rows])
    b.fetch("first", b.first_in, b.first)
    b.fetch("value", b.value_in, b.value)
    b.fetch("second", b.second_in, b.second)
    b.fetch("out", b.out_in, b.out)
    b.fetch("up", b.up_in, b.up)
    b.fetch("down", b.down_in, b.down)
    forward_part(b, n, True)
    b.finish()


class BackwardRefs(NamedTuple):
    lengths: Any
    vectors: Any
    x_in: Any
    c_in: Any
    p_in: Any
    att_in: Any
    v_in: Any
    o_in: Any
    y_in: Any
    m_in: Any
    first_in: Any
    second_in: Any
    value_in: Any
    out_in: Any
    up_in: Any
    down_in: Any
    grads_in: Any
    table_out: Any
    down_grad: Any
    up_grad: Any
    out_grad: Any
    value_grad: Any
    first_grad: Any
    second_grad: Any
    x: Any
    c: Any
    p: Any
    att: Any
    v: Any
    o: Any
    y: Any
    m: Any
    first: Any
    value: Any
    out: Any
    up: Any
    a: Any
    u: Any
    s: Any
    go: Any
    gv: Any
    gp: Any
    gb: Any
    gy: Any
    wide: Any
    dx: Any
    feed: Any
    stage: Any
    prior_stage: Any
    vector_grads: Any
    sems: Any
    stage_sems: Any
    prior_sems: Any


def dense_backward_kernel(n, turn, *refs):
    if n == 0:
        return
    refs = refs[:16] + refs[16 + (7 if turn > 0 else 5) :]
    table = BackwardRefs(*refs)
    shape = shape_of(table)
    ff, width = table.m.shape[1], table.x.shape[1]

    item = item_of(table.lengths, turn)
    b = Bench(item=item, length=table.lengths[item], **table._asdict(), **shape)
    b.gm, b.gs = b.feed.at[:, pl.ds(0, ff)], b.feed
    parts = width // unit_cols
    b.down_rows = lambda t: b.up[
        cols_at(lax.rem(t, parts)), pl.ds(pl.multiple_of(ff + t // parts * width, width), width)
    ]
    rows = pl.ds(0, n)
    b.fetch("c", b.c_in.at[rows], b.c.at[rows])
    b.fetch("m", b.m_in.at[rows], b.m.at[rows])
    for part in range(ff // width):
        b.fetch(f"down{part}", b.down_in.at[pl.ds(part * width, width)], b.up.at[:, pl.ds(ff + part * width, width)])
    b.fetch("up", b.up_in, b.up.at[:, pl.ds(0, ff)])
    b.fetch("y", b.y_in.at[rows], b.y.at[rows])
    b.fetch("o", b.o_in.at[rows], b.o.at[rows])
    b.fetch("out", b.out_in, b.out)
    b.fetch("v", b.v_in.at[rows], b.v.at[rows])
    b.fetch("att", b.att_in.at[:, rows, rows], b.att.at[:, rows, rows])
    b.fetch("x", b.x_in.at[item, rows], b.x.at[rows])
    b.fetch("p", b.p_in.at[rows], b.p.at[rows])
    b.fetch("value", b.value_in, b.value)
    b.fetch("first", b.first_in, b.first)
    plan_grads(b, turn > 0)
    b.need(*[f"down{part}" for part in range(ff // width)])
    backward_part(b, n, True, turn > 0)
    b.finish()


class RandomRefs(NamedTuple):
    lengths: Any
    vectors: Any
    x_in: Any
    c_in: Any
    att_in: Any
    value_in: Any
    out_in: Any
    up_in: Any
    down_in: Any
    states: Any
    grads_in: Any
    dx_out: Any
    table_out: Any
    random_grad: Any
    r_out: Any
    o_out: Any
    a_out: Any
    gm_out: Any
    u_out: Any
    gb_out: Any
    gv_out: Any
    c_out: Any
    x: Any
    c: Any
    att: Any
    v: Any
    o: Any
    y: Any
    m: Any
    value: Any
    out: Any
    up: Any
    down: Any
    a: Any
    u: Any
    go: Any
    gv: Any
    gb: Any
    gy: Any
    wide: Any
    z: Any
    dx: Any
    r: Any
    gm: Any
    random_stage: Any
    random_old: Any
    vector_grads: Any
    sems: Any
    random_sems: Any


def random_kernel(n, turn, *refs):
    if n == 0:
        return
    refs = refs[:9] + refs[9 + (3 if turn > 0 else 1) :]
    table = RandomRefs(*refs)
    shape = shape_of(table)

    item = item_of(table.lengths, turn)
    b = Bench(item=item, length=table.lengths[item], **table._asdict(), **shape)
    rows = pl.ds(0, n)
    b.fetch("x", b.x_in.at[rows], b.x.at[rows])
    b.fetch("value", b.value_in, b.value)
    b.fetch("att", b.att_in.at[:, rows, rows], b.att.at[:, rows, rows])
    b.fetch("out", b.out_in, b.out)
    b.fetch("up", b.up_in, b.up)
    b.fetch("down", b.down_in, b.down)
    b.down_rows = lambda t: b.down[cols_at(t), :]
    b.fetch("c", b.c_in.at[item, rows], b.c.at[rows])
    if turn > 0:
        random_copies(b, n)[0](0).start()
    forward_part(b, n, False)
    backward_part(b, n, False, turn > 0)
    b.finish()


class AttentionRefs(NamedTuple):
    lengths: Any
    logits_in: Any
    att_out: Any
    att: Any
    sems: Any


def random_attention_kernel(n, turn, *refs):
    if n == 0:
        return
    table = AttentionRefs(*refs)
    heads, slots, _ = table.att.shape
    b = Bench(length=table.lengths[item_of(table.lengths, turn)], slots=slots, **table._asdict())
    rows = pl.ds(0, n)
    half = heads // 2
    for k in (0, 1):
        part = pl.ds(k * half, half)
        b.fetch(k, b.logits_in.at[part, rows, rows], b.att.at[part, rows, rows])
    for k in (0, 1):
        b.need(k)

        def head(h, carry):
            b.att[h, :n, :n] = softmax(b, n, b.att[h, :n, :n].astype(f32))
            return carry

        lax.fori_loop(k * half, (k + 1) * half, head, 0)
        part = pl.ds(k * half, half)
        b.send(b.att.at[part, rows, rows], b.att_out.at[part, rows, rows])
    b.finish()


def random_attention(n, turn, lengths, logits):
    return pl.pallas_call(
        functools.partial(random_attention_kernel, n, turn),
        out_shape=S(logits.shape, bf16),
        in_specs=[scalars, anywhere],
        out_specs=anywhere,
        scratch_shapes=[] if n == 0 else [vmem(*logits.shape), pltpu.SemaphoreType.DMA((4,))],
        compiler_params=own_params(),
        name=f"random_attention_{n}",
    )(lengths, logits)


def weight_steps(kept, grads, c, r, o, a, gm, u, gb, gv, stage, sems, stage_sems):
    count = len(kept)
    slots = c.shape[0] // count
    b = Bench(stage=stage, sems=sems, stage_sems=stage_sems, width=c.shape[1])
    wide = 2 * b.width
    def need(*names):
        b.need(*[f"{name}{k}" for name in names for k in range(count)])

    def begin():
        for name, ref, at in (
            ("o", o, 1), ("gb", gb, 5), ("a", a, 2), ("gv", gv, 6), ("c", c, 7), ("r", r, 0), ("gm", gm, 3), ("u", u, 4),
        ):
            for k in range(count):
                b.fetch(f"{name}{k}", kept[k][at], ref.at[pl.ds(k * slots, slots)])
        out_grad, value_grad, down_grad, up_grad = grads
        b.plan(False, (out_grad, b.width), (value_grad, b.width), (down_grad, b.width), (up_grad, wide))

    def narrow():
        need("o", "gb")
        b.emit(lambda t, s, write: write(dot_down(o[:, cols_at(t)], gb[...])))
        need("a", "gv")
        b.emit(lambda t, s, write: write(dot_down(a[:, cols_at(t)], gv[...])))

    def down():
        need("c", "r")
        b.emit(lambda t, s, write: write(dot_down(r[:, cols_at(t)], c[...])))

    def up():
        need("gm", "u")
        b.emit(lambda t, s, write: write(dot_down(u[:, cols_at(t)], gm[:, pl.ds(pl.multiple_of(s * wide, wide), wide)])))
        b.finish()

    return begin, narrow, down, up


anywhere = pl.BlockSpec(memory_space=pl.ANY)
inside = pl.BlockSpec(memory_space=pltpu.VMEM)
scalars = pl.BlockSpec(memory_space=pltpu.SMEM)
S = jax.ShapeDtypeStruct


def vmem(*shape, dtype=bf16):
    return pltpu.VMEM(shape, dtype)


def own_params():
    return pltpu.CompilerParams(vmem_limit_bytes=63 << 20, has_side_effects=True)


def dense_forward(n, turn, lengths, vectors, inputs, weights, heads, states):
    _, slots, width = inputs.shape
    ff = weights["up"].shape[1]
    outs = (
        S(inputs.shape, bf16), S((slots, width), bf16), S((slots, width), f32), S((heads, slots, slots), bf16),
        S((slots, width), bf16), S((slots, width), bf16), S((slots, width), f32), S((slots, ff), bf16),
    )
    rows = vmem(slots, width)
    old = [] if states is None else [states]
    return pl.pallas_call(
        functools.partial(dense_forward_kernel, n, turn),
        out_shape=outs,
        in_specs=[scalars, inside if n else anywhere] + [anywhere] * (7 + len(old)),
        out_specs=[anywhere] * 8,
        input_output_aliases={9: 0} if old else {},
        scratch_shapes=[] if n == 0 else [
            rows, vmem(width, width), vmem(width, heads * slots), vmem(width, width), vmem(width, width), vmem(width, ff),
            vmem(ff, width), rows, vmem(slots, width, dtype=f32), vmem(heads, slots, slots), rows, rows,
            vmem(slots, width, dtype=f32), vmem(slots, ff), rows, rows, rows, vmem(slots, ff), pltpu.SemaphoreType.DMA((20,)),
        ],
        compiler_params=own_params(),
        name=f"dense_forward_{n}",
    )(lengths, vectors, inputs, *[weights[k] for k in ("first", "second", "value", "out", "up", "down")], *old)


def dense_backward(n, turn, lengths, vectors, inputs, c, kept, weights, grads_in, old):
    p, att, v, o, y, m = kept
    heads = att.shape[0]
    _, slots, width = inputs.shape
    ff = weights["up"].shape[1]
    names = ("down", "up", "out", "value", "first", "second")
    outs = (S(inputs.shape, bf16), S(vectors.shape, f32)) + tuple(S(weights[name].shape, bf16) for name in names)
    rows = vmem(slots, width)
    square = vmem(width, width)
    aliases = {16: 0}
    aliases.update({17 + n: 2 + n for n in range(len(old))})
    return pl.pallas_call(
        functools.partial(dense_backward_kernel, n, turn),
        out_shape=outs,
        in_specs=[scalars, inside if n else anywhere] + [anywhere] * (15 + len(old)),
        out_specs=[anywhere] * 8,
        input_output_aliases=aliases,
        scratch_shapes=[] if n == 0 else [
            rows, rows, vmem(slots, width, dtype=f32), vmem(heads, slots, slots), rows, rows,
            vmem(slots, width, dtype=f32), vmem(slots, ff), square, square, square, vmem(width, 2 * ff),
            rows, rows, rows, rows, rows, rows, rows, vmem(slots, width, dtype=f32), vmem(slots, width, dtype=f32), rows,
            vmem(slots, 2 * ff), vmem(tile_slots, unit_cols, 2 * width), vmem(tile_slots, unit_cols, 2 * width),
            pltpu.VMEM(vectors.shape, f32),
            pltpu.SemaphoreType.DMA((24,)), pltpu.SemaphoreType.DMA((tile_slots,)), pltpu.SemaphoreType.DMA((tile_slots,)),
        ],
        compiler_params=own_params(),
        name=f"dense_backward_{n}",
    )(
        lengths, vectors, inputs, c, p, att, v, o, y, m,
        *[weights[k] for k in ("first", "second", "value", "out", "up", "down")], grads_in, *old,
    )


def random_step(n, turn, lengths, vectors, x, cotangent, att, weights, states, old):
    heads, slots, _ = att.shape
    width = x.shape[1]
    ff = weights["up"].shape[1]
    narrow = S((slots, width), bf16)
    broad = S((slots, ff), bf16)
    outs = (
        S(cotangent.shape, bf16), S(cotangent.shape, bf16), narrow, S(vectors.shape, f32), S(att.shape, bf16),
        broad, narrow, narrow, broad, narrow, narrow, narrow, narrow,
    )
    rows = vmem(slots, width)
    square = vmem(width, width)
    deep = vmem(slots, width, dtype=f32)
    pair = vmem(2, 2, slots, slots)
    return pl.pallas_call(
        functools.partial(random_kernel, n, turn),
        out_shape=outs,
        in_specs=[scalars, inside if n else anywhere] + [anywhere] * (8 + len(old)),
        out_specs=[anywhere] * 13,
        input_output_aliases={9: 0, 10: 1, 11: 4} if old else {9: 0},
        scratch_shapes=[] if n == 0 else [
            rows, rows, vmem(heads, slots, slots), rows, rows, deep, vmem(slots, ff), square, square,
            vmem(width, ff), vmem(ff, width), rows, rows, rows, rows, rows, deep, deep, rows, rows,
            vmem(slots, ff), vmem(slots, ff), pair, pair, pltpu.VMEM(vectors.shape, f32),
            pltpu.SemaphoreType.DMA((28,)), pltpu.SemaphoreType.DMA((2, 2)),
        ],
        compiler_params=own_params(),
        name=f"random_step_{n}",
    )(lengths, vectors, x, cotangent, att, *[weights[k] for k in ("value", "out", "up", "down")], states, *old)


def weight_scratch(count, slots, width, ff):
    tall = vmem(count * slots, width)
    broad = vmem(count * slots, ff)
    return [
        tall, broad, tall, tall, broad, tall, tall, tall, vmem(tile_slots, unit_cols, 2 * width),
        pltpu.SemaphoreType.DMA((8 * count,)), pltpu.SemaphoreType.DMA((tile_slots,)),
    ]


def weights_kernel(count, *refs):
    kept = [refs[8 * k : 8 * k + 8] for k in range(count)]

    @pl.when(lax.axis_index(section_axis) == 1)
    def _():
        down, up, out, value, *scratch = refs[8 * count :]
        for step in weight_steps(kept, (out, value, down, up), *scratch):
            step()


def random_weights(kept, weights):
    slots, width = kept[0][1].shape
    ff = kept[0][0].shape[1]
    names = ("down", "up", "out", "value")
    return pl.pallas_call(
        functools.partial(weights_kernel, len(kept)),
        out_shape=tuple(S(weights[name].shape, bf16) for name in names),
        in_specs=[anywhere] * (8 * len(kept)),
        out_specs=[anywhere] * 4,
        scratch_shapes=weight_scratch(len(kept), slots, width, ff),
        compiler_params=own_params(),
        name="random_weights",
    )(*[a for item in kept for a in item])


def deliver_kernel(arrays, random_in, small, *refs):
    ins, outs = refs[:arrays], refs[arrays + 1 : 2 * arrays + 1]
    random_ref = refs[arrays]
    vectors = refs[2 * arrays + 1 : 2 * arrays + 1 + vector_count]
    narrow, wide, sems, random_sems = refs[2 * arrays + 1 + vector_count :]
    slots, rows, _ = narrow.shape
    count = random_in.shape[0] // rows

    def part(n):
        return pl.ds(pl.multiple_of(n * rows, rows), rows)

    def load(n):
        slot = lax.rem(n, slots)
        return pltpu.make_async_copy(random_in.at[part(n)], narrow.at[slot], random_sems.at[0, slot])

    def store(n):
        slot = lax.rem(n, slots)
        return pltpu.make_async_copy(wide.at[slot], random_ref.at[part(n)], random_sems.at[1, slot])

    for n in range(slots - 1):
        load(n).start()
    copies = [pltpu.make_async_copy(a, b, sems.at[n]) for n, (a, b) in enumerate(zip(ins, outs))]
    for copy in copies:
        copy.start()
    for row, ref in enumerate(vectors):
        ref[...] = small[row : row + 1, : ref.shape[1]]

    def turn(n, carry):
        @pl.when(n + slots - 1 < count)
        def _():
            load(n + slots - 1).start()

        load(n).wait()

        @pl.when(n >= slots)
        def _():
            store(n - slots).wait()

        wide[lax.rem(n, slots)] = narrow[lax.rem(n, slots)].astype(f32)
        store(n).start()
        return carry

    lax.fori_loop(0, count, turn, 0)
    for n in range(count - slots, count):
        store(n).wait()
    for copy in copies:
        copy.wait()


def deliver(random, small, extents, arrays):
    rows, cols = random.shape
    slots = 4
    inside = pl.BlockSpec(memory_space=pltpu.VMEM)
    return pl.pallas_call(
        functools.partial(deliver_kernel, len(arrays)),
        out_shape=(S(random.shape, f32),)
        + tuple(S(a.shape, f32) for a in arrays)
        + tuple(S((1, extent), f32) for extent in extents),
        in_specs=[anywhere, inside] + [inside] * len(arrays),
        out_specs=[anywhere] * (1 + len(arrays)) + [inside] * len(extents),
        scratch_shapes=[
            vmem(slots, rows // 12, cols), vmem(slots, rows // 12, cols, dtype=f32),
            pltpu.SemaphoreType.DMA((len(arrays),)), pltpu.SemaphoreType.DMA((2, slots)),
        ],
        compiler_params=own_params(),
        name="deliver",
    )(random, small, *arrays)


def run_layers(inputs, cotangent, lengths, weights, vectors, logits, finish_random):
    count, slots, _ = inputs.shape
    heads = logits.shape[0]
    states = None
    firsts, seconds = [], []
    for turn in range(count):

        def forward(n):
            return dense_forward(n, turn, lengths, vectors, inputs, weights, heads, states)

        states, z, *kept = by_length(0, lengths, turn, slots, forward)
        firsts.append(kept)
        seconds.append(passed_along(z, section_axis, 1))
    atts = [
        by_length(1, lengths, turn, slots, lambda n: random_attention(n, turn, lengths, logits)) for turn in range(count)
    ]
    seconds[0], *atts = lax.optimization_barrier((seconds[0], *atts))
    old, backs, random_tables, random_kept = [], [], [], []
    for turn in range(count):

        def step(n):
            return random_step(n, turn, lengths, vectors, seconds[turn], cotangent, atts[turn], weights, states, old)

        states, grads_in, dx, table, random_grad, *kept = by_length(1, lengths, turn, slots, step)
        old = [grads_in, random_grad]
        backs.append(passed_along(dx, section_axis, -1))
        random_tables.append(table)
        random_kept.append(kept)
    random_grad, *grads = finish_random(random_grad, random_kept, weights)
    dense_tables = []
    for turn in range(count):

        def backward(n):
            return dense_backward(
                n, turn, lengths, vectors, inputs, backs[turn], firsts[turn], weights, grads_in, grads
            )

        grads_in, table, *grads = by_length(0, lengths, turn, slots, backward, long_late=True)
        dense_tables.append(table)
    grads = dict(zip(("down", "up", "out", "value", "first", "second"), grads))
    return states, grads_in, grads, random_grad, dense_tables, random_tables


def random_finish_kernel(dp, count, random_in, *refs):
    kept = [refs[8 * k : 8 * k + 8] for k in range(count)]
    refs = refs[8 * count :]
    random_ref, down, up, out, value = refs[:5]
    grads = (out, value, down, up)
    (
        own, sib, ring, own_sems, sib_send, sib_recv, ring_send, ring_recv,
    ) = refs[5:13]
    begin, *meanwhile = weight_steps(kept, grads, *refs[13:])
    place = Place(dp)
    reach, chips = place.reach, place.chips
    block = random_in.shape[0] // (2 * chips)
    strip = block // 2
    away = (reach,) + tuple(o for t in range(reach - 1, 0, -1) for o in (t, -t)) + (0,)
    spot_of = {o: n for n, o in enumerate(away)}
    spot_of[-reach] = 0

    def part(ref, o, core):
        return ref.at[pl.ds(pl.multiple_of((core * chips + place.chip_at(o)) * block, block), block)]

    def load(o):
        return pltpu.make_async_copy(part(random_in, o, place.core), own.at[spot_of[o]], own_sems.at[spot_of[o]])

    def lend(o):
        at = spot_of[o]
        return remote(part(random_in, o, 1 - place.core), sib.at[at], sib_send.at[at], sib_recv.at[at], place.sibling())

    def carried(i, way, step):
        return step > 0 or i == way

    def ring_copy(i, way, step):
        turn = 1 if way == 0 else -1
        rows = pl.ds(i * strip, strip)
        return remote(
            own.at[spot_of[turn * (reach - step)], rows], ring.at[way, step, rows],
            ring_send.at[way, step, i], ring_recv.at[way, step, i], place.along(turn),
        )

    @pl.when(place.section == 1)
    def _():
        place.greet()
        for o in away:
            lend(o).start()
            load(o).start()
        begin()
        for step in range(reach + 1):
            for i in (0, 1):
                for way in (0, 1):
                    o = (reach - step) * (1 if way == 0 else -1)
                    if step < reach and not carried(i, way, step) or step == reach and way == 1:
                        continue
                    if i == 0:
                        load(o).wait()
                        lend(o).wait_recv()
                    rows = pl.ds(i * strip, strip)
                    terms = [own.at[spot_of[o], rows], sib.at[spot_of[o], rows]]
                    for back in (0, 1) if step == reach else (way,):
                        if step > 0 and carried(i, back, step - 1):
                            ring_copy(i, back, step - 1).wait_recv()
                            terms.append(ring.at[back, step - 1, rows])
                    store_sum(own.at[spot_of[o], rows], terms, strip)
                    if step < reach:
                        ring_copy(i, way, step).start()
            if meanwhile and step < reach:
                meanwhile.pop(0)()
        keep = pltpu.make_async_copy(own.at[spot_of[0]], random_ref, own_sems.at[chips])
        keep.start()
        for work in meanwhile:
            work()
        for o in away:
            lend(o).wait_send()
        keep.wait()
        for i in (0, 1):
            for way in (0, 1):
                for step in range(reach):
                    if carried(i, way, step):
                        ring_copy(i, way, step).wait_send()


def random_finish(dp, random, kept, weights):
    chips = dp // 2
    reach = chips // 2
    block = (random.shape[0] // dp, random.shape[1])
    slots, width = kept[0][1].shape
    ff = kept[0][0].shape[1]
    count = len(kept)
    dma = pltpu.SemaphoreType.DMA
    names = ("down", "up", "out", "value")
    return pl.pallas_call(
        functools.partial(random_finish_kernel, dp, count),
        out_shape=(S(block, random.dtype),) + tuple(S(weights[name].shape, bf16) for name in names),
        in_specs=[anywhere] * (1 + 8 * count),
        out_specs=[anywhere] * 5,
        scratch_shapes=[
            pltpu.VMEM((chips,) + block, random.dtype),
            pltpu.VMEM((chips,) + block, random.dtype),
            pltpu.VMEM((2, reach) + block, random.dtype),
            dma((chips + 1,)),
            dma((chips,)),
            dma((chips,)),
            dma((2, reach, 2)),
            dma((2, reach, 2)),
        ] + weight_scratch(count, slots, width, ff),
        compiler_params=pltpu.CompilerParams(
            collective_id=2, has_side_effects=True, vmem_limit_bytes=63 << 20
        ),
        name="random_finish",
    )(random, *[a for item in kept for a in item])


def passed_along(x, axis, by):
    size = lax.axis_size(axis)
    pairs = [(i, i + by) for i in range(size) if 0 <= i + by < size]
    return lax.ppermute(x, axis, pairs)


def table_of(vectors, ff):
    return jnp.stack([jnp.pad(v.astype(f32), (0, ff - v.shape[0])) for v in vectors])


def per_device(
    inputs,
    cotangent,
    lengths,
    first_gain,
    first_shift,
    value_weight,
    out_weight,
    out_bias,
    second_gain,
    second_shift,
    up_weight,
    up_bias,
    down_weight,
    down_bias,
    synth_first,
    synth_bias,
    synth_second,
    random_logits,
):
    dp = lax.axis_size(dp_axis)
    is_dense = lax.axis_index(section_axis) == 0
    value_share, out_share, up_share, down_share = value_weight[0], out_weight[0], up_weight[0], down_weight[0]
    ff = up_share.shape[1]
    shares = [
        a.reshape(1, -1)
        for a in (first_gain, first_shift, out_bias, second_gain, second_shift, down_bias, up_bias, synth_bias)
    ]
    extents = tuple(a.shape[1] for a in shares)
    ringed = (
        dp % 4 == 0 and dp > 4 and value_share.shape[0] % 16 == 0 and synth_first.shape[0] % 8 == 0
        and max(extents) <= small_block[1]
    )
    if ringed:
        value, out, up, down, first, second, table = gather_weights(
            dp, value_share, out_share, up_share, down_share, synth_first, synth_second, shares
        )
    else:
        value, out, up, down = (
            lax.all_gather(a, dp_axis, axis=0, tiled=True) for a in (value_share, out_share, up_share, down_share)
        )
        first, second = (lax.all_gather(a, (section_axis, dp_axis), axis=0, tiled=True) for a in (synth_first, synth_second))
        axes = [dp_axis] * synth_row + [(section_axis, dp_axis)]
        table = table_of([lax.all_gather(a[0], axis, axis=0, tiled=True) for a, axis in zip(shares, axes)], ff)
    weights = dict(value=value, out=out, up=up, down=down, first=first, second=second)

    def finish_random(grad, kept, of):
        flat = grad.reshape(-1, grad.shape[-1])
        return random_finish(dp, flat, kept, of) if ringed else (flat, *random_weights(kept, of))

    states, grads_in, grads, random_grad, dense_tables, random_tables = run_layers(
        inputs, cotangent, lengths, weights, table, random_logits, finish_random
    )
    arrays = [grads[name] for name in ("value", "out", "up", "down", "first", "second")]
    if ringed:
        g_value, g_out, g_up, g_down, small, g_first, g_second, random_grad = reduce_grads(
            dp, *arrays, random_grad, dense_tables, random_tables, extents
        )
        random_total, g_value, g_out, g_up, g_down, g_first, g_second, *g_vectors = deliver(
            random_grad, small, extents, (g_value, g_out, g_up, g_down, g_first, g_second)
        )
        g_vectors = [v.reshape(-1) for v in g_vectors]
    else:
        g_value, g_out, g_up, g_down = (
            lax.psum_scatter(a, dp_axis, scatter_dimension=0, tiled=True).astype(f32) for a in arrays[:4]
        )
        g_first, g_second = (
            lax.psum_scatter(jnp.where(is_dense, a, jnp.zeros_like(a)), (section_axis, dp_axis), scatter_dimension=0, tiled=True).astype(f32)
            for a in arrays[4:]
        )
        grad_table = jnp.where(is_dense, sum(dense_tables), sum(random_tables))
        g_vectors = [
            lax.psum_scatter(grad_table[row, : dp * extents[row]], dp_axis, scatter_dimension=0, tiled=True)
            for row in range(synth_row)
        ]
        synth_grad = jnp.where(is_dense, grad_table[synth_row, : 2 * dp * extents[synth_row]], 0.0)
        g_vectors.append(lax.psum_scatter(synth_grad, (section_axis, dp_axis), scatter_dimension=0, tiled=True))
        random_total = lax.psum(jnp.where(is_dense, jnp.zeros_like(random_grad), random_grad), (section_axis, dp_axis)).astype(f32)
    random_total = random_total.reshape(random_logits.shape)
    return (
        states[None],
        grads_in[None],
        g_vectors[FIRST_GAIN][None],
        g_vectors[FIRST_SHIFT][None],
        g_value[None],
        g_out[None],
        g_vectors[OUT_BIAS][None],
        g_vectors[SECOND_GAIN][None],
        g_vectors[SECOND_SHIFT][None],
        g_up[None],
        g_vectors[UP_BIAS][None],
        g_down[None],
        g_vectors[DOWN_BIAS][None],
        g_first,
        g_vectors[SYNTH_BIAS],
        g_second,
        random_total,
    )


def solution(mesh):
    in_specs = (
        P(dp_axis, None, None),
        P(dp_axis, None, None),
        P(dp_axis),
        P(section_axis, dp_axis),
        P(section_axis, dp_axis),
        P(section_axis, dp_axis, None),
        P(section_axis, dp_axis, None),
        P(section_axis, dp_axis),
        P(section_axis, dp_axis),
        P(section_axis, dp_axis),
        P(section_axis, dp_axis, None),
        P(section_axis, dp_axis),
        P(section_axis, dp_axis, None),
        P(section_axis, dp_axis),
        P((section_axis, dp_axis), None),
        P((section_axis, dp_axis)),
        P((section_axis, dp_axis), None),
        P(),
    )
    out_specs = (
        P(section_axis, dp_axis, None, None),
        P(section_axis, dp_axis, None, None),
        P(section_axis, dp_axis),
        P(section_axis, dp_axis),
        P(section_axis, dp_axis, None),
        P(section_axis, dp_axis, None),
        P(section_axis, dp_axis),
        P(section_axis, dp_axis),
        P(section_axis, dp_axis),
        P(section_axis, dp_axis, None),
        P(section_axis, dp_axis),
        P(section_axis, dp_axis, None),
        P(section_axis, dp_axis),
        P((section_axis, dp_axis), None),
        P((section_axis, dp_axis)),
        P((section_axis, dp_axis), None),
        P(),
    )
    return jax.shard_map(
        per_device, mesh=mesh, in_specs=in_specs, out_specs=out_specs, check_vma=False
    )
```

```python
import functools
from typing import Any, NamedTuple

import jax
import jax.numpy as jnp
from jax import lax
from jax.experimental import pallas as pl
from jax.experimental.pallas import tpu as pltpu
from jax.sharding import PartitionSpec as P

MESH = pl.DeviceIdType.MESH


class Place:
    def __init__(self, dp):
        self.chips = dp // 2
        self.reach = self.chips // 2
        self.section = lax.axis_index(section_axis)
        index = lax.axis_index(dp_axis)
        self.core = lax.rem(index, 2)
        self.chip = index // 2
        column = lax.rem(self.chip, 2)
        row = self.chip // 2
        self.position = row + column * (self.chips - 1 - 2 * row)

    def chip_at(self, steps):
        spot = lax.rem(self.position + steps + 2 * self.chips, self.chips)
        column = spot // self.reach
        row = spot + column * (self.chips - 1 - 2 * spot)
        return 2 * row + column

    def along(self, steps):
        return (self.section, 2 * self.chip_at(steps) + self.core)

    def sibling(self):
        return (self.section, 2 * self.chip + 1 - self.core)

    def across(self):
        return (1 - self.section, 2 * self.chip + self.core)

    def greet_late(self, early):
        barrier = pltpu.get_barrier_semaphore()
        near = (self.along(1), self.along(-1), self.sibling())
        for other in near:
            pl.semaphore_signal(barrier, inc=1, device_id=other, device_id_type=MESH)

        @pl.when(early)
        def _():
            pl.semaphore_wait(barrier, len(near))
            pl.semaphore_signal(barrier, inc=1, device_id=self.across(), device_id_type=MESH)

        @pl.when(jnp.logical_not(early))
        def _():
            pl.semaphore_wait(barrier, len(near) + 1)
            pl.semaphore_signal(barrier, inc=1, device_id=self.across(), device_id_type=MESH)

    def greet(self, *others):
        barrier = pltpu.get_barrier_semaphore()
        others = (self.along(1), self.along(-1), self.sibling()) + others
        for other in others:
            pl.semaphore_signal(barrier, inc=1, device_id=other, device_id_type=MESH)
        pl.semaphore_wait(barrier, len(others))


def remote(src, dst, send_sem, recv_sem, device):
    return pltpu.make_async_remote_copy(
        src_ref=src, dst_ref=dst, send_sem=send_sem, recv_sem=recv_sem,
        device_id=device, device_id_type=MESH,
    )


def hint(value, unit):
    return pl.multiple_of(value, unit)


PIECES = (
    ("second_a", 0, True),
    ("second_b", 1, True),
    ("first", 0, True),
    ("value", 0, False),
    ("out", 1, False),
    ("up", 0, False),
    ("down", 1, False),
    ("small", 0, True),
)
(FIRST_GAIN, FIRST_SHIFT, OUT_BIAS, SECOND_GAIN, SECOND_SHIFT, DOWN_BIAS, UP_BIAS, SYNTH_BIAS) = range(8)
vector_count = 8
up_row, synth_row = UP_BIAS, SYNTH_BIAS
section_axis, dp_axis = "section", "dp"
small_block = (8, 256)


def piece_view(refs, name, chip, core, section, sizes):
    rows, ff_rows, dense_rows, dense_cols, second_cols, chips = sizes
    who = 2 * chip + core
    if name in ("value", "out", "up"):
        return refs[name].at[pl.ds(hint(who * rows, rows), rows)]
    if name == "down":
        return refs[name].at[pl.ds(hint(who * ff_rows, ff_rows), ff_rows)]
    if name == "small":
        return refs[name].at[section, who]
    top = hint((section * chips + chip) * dense_rows, dense_rows)
    if name == "first":
        return refs[name].at[pl.ds(top, dense_rows), pl.ds(hint(core * dense_cols, dense_cols), dense_cols)]
    half = second_cols // 2
    left = core * second_cols + (half if name == "second_b" else 0)
    return refs["second"].at[pl.ds(top, dense_rows), pl.ds(hint(left, half), half)]


def gather_kernel(
    dp, sizes,
    value_in, out_in, up_in, down_in, first_in, second_in, *rest,
):
    vectors = rest[: vector_count]
    (
        value_ref, out_ref, up_ref, down_ref, first_ref, second_ref, table_ref,
        small_in, small_ref, first_wide, second_wide, first_stage, second_stage, wide_sems,         own_sems, ring_send, ring_recv, sib_send, sib_recv, across_send, across_recv, pass_send, pass_recv,
    ) = rest[vector_count :]
    rows, ff_rows, dense_rows, dense_cols, second_cols, chips = sizes
    place = Place(dp)
    reach = place.reach
    quarter = dense_rows // 2
    refs = dict(value=value_ref, out=out_ref, up=up_ref, down=down_ref, small=small_ref, first=first_ref, second=second_ref)
    half = second_cols // 2
    sources = dict(
        value=value_in, out=out_in, up=up_in, down=down_in, small=small_in, first=first_stage,
        second_a=second_stage.at[:, pl.ds(0, half)], second_b=second_stage.at[:, pl.ds(half, half)],
    )
    order = tuple(range(len(PIECES)))
    dense = tuple(i for i in order if PIECES[i][2])
    plain = tuple(i for i in order if not PIECES[i][2])

    def view(i, steps, section):
        return piece_view(refs, PIECES[i][0], place.chip_at(steps), place.core, section, sizes)

    def carried(i, way, step):
        return step < reach - 1 or (step == reach - 1 and PIECES[i][1] == way)

    def ring_copy(i, way, step):
        turn = 1 if way == 0 else -1
        target = view(i, -turn * step, place.section)
        source = sources[PIECES[i][0]] if step == 0 else target
        return remote(source, target, ring_send.at[way, step, i], ring_recv.at[way, step, i], place.along(turn))

    def slot(way, step):
        return 0 if step < 0 else 1 + 2 * step + way

    def sibling_copy(i, way, step):
        turn = 1 if way == 0 else -1
        target = view(i, -turn * (step + 1) if step >= 0 else 0, place.section)
        source = sources[PIECES[i][0]] if step < 0 else target
        at = slot(way, step)
        return remote(source, target, sib_send.at[at, i], sib_recv.at[at, i], place.sibling())

    def across_copy(i, way, step):
        turn = 1 if way == 0 else -1
        target = view(i, -turn * (step + 1) if step >= 0 else 0, place.section)
        source = sources[PIECES[i][0]] if step < 0 else target
        at = slot(way, step)
        return remote(source, target, across_send.at[at, i], across_recv.at[at, i], place.across())

    def pass_copy(i, way, step):
        turn = 1 if way == 0 else -1
        target = view(i, -turn * (step + 1) if step >= 0 else 0, 1 - place.section)
        at = slot(way, step)
        return remote(target, target, pass_send.at[at, i], pass_recv.at[at, i], place.sibling())

    def own_copy(i):
        return pltpu.make_async_copy(sources[PIECES[i][0]], view(i, 0, place.section), own_sems.at[i])

    def begin(i):
        for way in (0, 1):
            if carried(i, way, 0):
                ring_copy(i, way, 0).start()
        sibling_copy(i, 0, -1).start()
        if PIECES[i][2]:
            across_copy(i, 0, -1).start()
        own_copy(i).start()

    small_in[...] = jnp.zeros(small_block, jnp.float32)
    for row, ref in enumerate(vectors):
        small_in[row : row + 1, : ref.shape[1]] = ref[...].astype(jnp.float32)
    mine = hint(place.core * quarter, 8)
    first_wide[pl.ds(mine, quarter)] = first_in[...].astype(jnp.float32)
    second_wide[pl.ds(mine, quarter)] = second_in[...].astype(jnp.float32)
    place.greet(place.across())
    wide = [
        remote(ref.at[pl.ds(mine, quarter)], ref.at[pl.ds(mine, quarter)], wide_sems.at[0, n], wide_sems.at[1, n], place.sibling())
        for n, ref in enumerate((first_wide, second_wide))
    ]
    for copy in wide:
        copy.start()
    early = plain[:2]
    for i in early:
        begin(i)
    for copy in wide:
        copy.wait()
    first_stage[...] = first_wide[:, pl.ds(hint(place.core * dense_cols, dense_cols), dense_cols)].astype(jnp.bfloat16)
    second_stage[...] = second_wide[:, pl.ds(hint(place.core * second_cols, second_cols), second_cols)].astype(jnp.bfloat16)
    for i in dense + plain[len(early) :]:
        begin(i)

    events = [(i, way, step) for step in range(reach) for i in order for way in (0, 1) if carried(i, way, step)]
    crossing = [(i, 0, -1) for i in dense] + [e for e in events if e[0] in dense]
    passed = 0

    def pass_on(count):
        nonlocal passed
        while passed < min(count, len(crossing)):
            e = crossing[passed]
            across_copy(*e).wait_recv()
            pass_copy(*e).start()
            passed += 1

    for i, way, step in events:
        ring_copy(i, way, step).wait_recv()
        if carried(i, way, step + 1):
            ring_copy(i, way, step + 1).start()
        sibling_copy(i, way, step).start()
        if i in dense:
            across_copy(i, way, step).start()
        if i == order[-1] and way == 0:
            pass_on(len(dense) + 2 * len(dense) * step)
    pass_on(len(crossing))
    def drain(some):
        for i in some:
            own_copy(i).wait()
            sibling_copy(i, 0, -1).wait()
            for way in (0, 1):
                if carried(i, way, 0):
                    ring_copy(i, way, 0).wait_send()
        for i, way, step in events:
            if i in some:
                sibling_copy(i, way, step).wait()
                if step > 0:
                    ring_copy(i, way, step).wait_send()
        for e in crossing:
            if e[0] in some:
                across_copy(*e).wait_send()
                pass_copy(*e).wait()

    drain(order[-1:])
    shares = [ref.shape[1] for ref in vectors]
    share = shares[0]

    def side_by_side(blocks):
        return jnp.concatenate(blocks, axis=1)

    table_ref[:up_row, : dp * share] = side_by_side([small_ref[place.section, d, :up_row, :share] for d in range(dp)])
    up_share = shares[up_row]
    table_ref[up_row : up_row + 1, :] = side_by_side(
        [small_ref[place.section, d, up_row : up_row + 1, :up_share] for d in range(dp)]
    )
    synth_share = shares[synth_row]
    table_ref[synth_row : synth_row + 1, : 2 * dp * synth_share] = side_by_side(
        [small_ref[s, d, synth_row : synth_row + 1, :synth_share] for s in range(2) for d in range(dp)]
    )
    drain(order[:-1])


def gather_weights(dp, value, out, up, down, first, second, vectors):
    rows, width = value.shape
    ff_rows = down.shape[0]
    ff = up.shape[1]
    chips = dp // 2
    dense_rows = 2 * first.shape[0]
    dense_cols = first.shape[1] // 2
    second_cols = second.shape[1] // 2
    sizes = (rows, ff_rows, dense_rows, dense_cols, second_cols, chips)
    reach = chips // 2
    count = len(PIECES)
    bf = jnp.bfloat16
    anywhere = pl.BlockSpec(memory_space=pl.ANY)
    inside = pl.BlockSpec(memory_space=pltpu.VMEM)
    dma = pltpu.SemaphoreType.DMA
    return pl.pallas_call(
        functools.partial(gather_kernel, dp, sizes),
        out_shape=(
            jax.ShapeDtypeStruct((rows * dp, width), bf),
            jax.ShapeDtypeStruct((rows * dp, width), bf),
            jax.ShapeDtypeStruct((rows * dp, ff), bf),
            jax.ShapeDtypeStruct((ff_rows * dp, width), bf),
            jax.ShapeDtypeStruct((2 * dp * first.shape[0], first.shape[1]), bf),
            jax.ShapeDtypeStruct((2 * dp * second.shape[0], second.shape[1]), bf),
            jax.ShapeDtypeStruct((vector_count, ff), jnp.float32),
        ),
        in_specs=[anywhere] * 4 + [inside] * (2 + len(vectors)),
        out_specs=[anywhere] * 6 + [inside],
        scratch_shapes=[
            pltpu.VMEM(small_block, jnp.float32),
            pltpu.VMEM((2, dp) + small_block, jnp.float32),
            pltpu.VMEM((dense_rows, 2 * dense_cols), jnp.float32),
            pltpu.VMEM((dense_rows, 2 * second_cols), jnp.float32),
            pltpu.VMEM((dense_rows, dense_cols), bf),
            pltpu.VMEM((dense_rows, second_cols), bf),
            dma((2, 2)),
            dma((count,)),
            dma((2, reach, count)),
            dma((2, reach, count)),
            dma((1 + 2 * reach, count)),
            dma((1 + 2 * reach, count)),
            dma((1 + 2 * reach, count)),
            dma((1 + 2 * reach, count)),
            dma((1 + 2 * reach, count)),
            dma((1 + 2 * reach, count)),
        ],
        compiler_params=pltpu.CompilerParams(
            collective_id=0, has_side_effects=True, vmem_limit_bytes=63 << 20
        ),
        name="gather_weights",
    )(value, out, up, down, first, second, *vectors)


def store_sum(target, terms, rows):
    if rows == 0:
        total = terms[0][...]
        for term in terms[1:]:
            total = total + term[...]
        target[...] = total
        return

    def some(n, carry):
        at = pl.ds(pl.multiple_of(n * 16, 16), 16)
        total = terms[0][at, :].astype(jnp.float32)
        for term in terms[1:]:
            total = total + term[at, :].astype(jnp.float32)
        target[at, :] = total.astype(target.dtype)
        return carry

    lax.fori_loop(0, rows // 16, some, 0)


def reduce_kernel(dp, sizes, shares, tables, value_in, out_in, up_in, down_in, first_in, second_in, random_in, *rest):
    dense_tables, random_tables = rest[:tables], rest[tables : 2 * tables]
    (
    value_ref, out_ref, up_ref, down_ref, small_ref, first_ref, second_ref, random_ref,
    small_in, own_value, own_out, own_up, own_down, own_small, own_first, own_second,
    sib_value, sib_out, sib_up, sib_down, sib_small, sib_first, sib_second,
    ring_value, ring_out, ring_up, ring_down, ring_small, ring_first, ring_second,
    across_small, across_first, across_second, first_wide, second_wide, first_part, second_part,
    own_sems, sib_send, sib_recv, ring_send, ring_recv, across_send, across_recv, wide_sems,
    random_sems, turn_send, turn_recv, pass_send, pass_recv,
    ) = rest[2 * tables :]
    rows, ff_rows, dense_rows, dense_cols, second_cols, chips = sizes
    place = Place(dp)
    reach = place.reach
    half = second_cols // 2
    quarter = dense_rows // 2
    is_dense = place.section == 0
    full = dict(value=value_in, out=out_in, up=up_in, down=down_in, small=small_in, first=first_in, second=second_in)
    own = dict(value=own_value, out=own_out, up=own_up, down=own_down, small=own_small, first=own_first, second=own_second)
    sib = dict(value=sib_value, out=sib_out, up=sib_up, down=sib_down, small=sib_small, first=sib_first, second=sib_second)
    ring = dict(value=ring_value, out=ring_out, up=ring_up, down=ring_down, small=ring_small, first=ring_first, second=ring_second)
    crossed = dict(first=across_first, second=across_second, small=across_small)
    order = tuple(range(len(PIECES)))
    small = len(PIECES) - 1
    crossing = tuple(i for i in order if PIECES[i][2])
    dense = crossing[:-1]
    plain = tuple(i for i in order if not PIECES[i][2])
    piece_rows = dict(value=rows, out=rows, up=rows, down=ff_rows, small=0, first=dense_rows, second_a=dense_rows, second_b=dense_rows)
    away = (reach,) + tuple(o for t in range(reach - 1, 0, -1) for o in (t, -t)) + (0,)
    spot_of = {o: n for n, o in enumerate(away)}
    spot_of[-reach] = 0

    def part(table, i, *at):
        name = PIECES[i][0]
        if name == "second_a":
            return table["second"].at[(*at, slice(None), pl.ds(0, half))]
        if name == "second_b":
            return table["second"].at[(*at, slice(None), pl.ds(half, half))]
        return table[name].at[at]

    def held(table, i, o, plane):
        spot = spot_of[o]
        return part(table, i, plane, spot) if PIECES[i][2] else part(table, i, spot)

    def source(i, o, core, plane):
        section = place.section if plane == 0 else 1 - place.section
        return piece_view(full, PIECES[i][0], place.chip_at(o), core, section, sizes)

    def load(i, o, plane):
        return pltpu.make_async_copy(
            source(i, o, place.core, plane), held(own, i, o, plane), own_sems.at[plane, spot_of[o], i]
        )

    def lend(i, o, plane):
        at = (plane, spot_of[o], i)
        return remote(source(i, o, 1 - place.core, plane), held(sib, i, o, plane), sib_send.at[at], sib_recv.at[at], place.sibling())

    def ring_copy(i, way, step):
        turn = 1 if way == 0 else -1
        o = turn * (reach - step)
        return remote(held(own, i, o, 0), part(ring, i, way, step), ring_send.at[way, step, i], ring_recv.at[way, step, i], place.along(turn))

    def across_copy(i, o):
        at = (spot_of[o], i)
        return remote(held(own, i, o, 1), part(crossed, i, spot_of[o]), across_send.at[at], across_recv.at[at], place.across())

    def carried(i, way, step):
        return step > 0 or PIECES[i][1] == way

    def local_terms(i, o):
        load(i, o, 0).wait()
        lend(i, o, 0).wait_recv()
        return [held(own, i, o, 0), held(sib, i, o, 0)]

    def total(target, i, o, arrived):
        if i == small:
            terms = local_terms(i, o) + arrived

            @pl.when(is_dense)
            def _():
                store_sum(target, terms, 0)

            @pl.when(jnp.logical_not(is_dense))
            def _():
                across_copy(i, o).wait_recv()
                store_sum(target, terms + [part(crossed, i, spot_of[o])], 0)
        elif PIECES[i][2]:

            @pl.when(is_dense)
            def _():
                store_sum(target, local_terms(i, o) + arrived, piece_rows[PIECES[i][0]])

            @pl.when(jnp.logical_not(is_dense))
            def _():
                across_copy(i, o).wait_recv()
                store_sum(target, [part(crossed, i, spot_of[o])] + arrived, piece_rows[PIECES[i][0]])
        else:
            store_sum(target, local_terms(i, o) + arrived, piece_rows[PIECES[i][0]])

    def arrivals(i, o):
        ways = (0, 1) if o == 0 else ((0,) if o > 0 else (1,))
        found = []
        for way in ways:
            step = reach - abs(o) - 1
            if step >= 0 and carried(i, way, step):
                ring_copy(i, way, step).wait_recv()
                found.append(part(ring, i, way, step))
        return found

    place.greet_late(jnp.logical_not(is_dense))
    for o in away:
        for i in plain:
            lend(i, o, 0).start()
            load(i, o, 0).start()

        @pl.when(is_dense)
        def _():
            for plane in (1, 0):
                for i in dense:
                    lend(i, o, plane).start()
                    load(i, o, plane).start()

    small_in[...] = jnp.zeros(small_in.shape, jnp.float32)

    def blocks_of(got, section, names):
        whole = got[0][...]
        for more in got[1:]:
            whole = whole + more[...]
        for d in range(dp):
            if names:
                share = shares[0]
                small_in[section, d, :up_row, :share] = whole[:up_row, d * share : (d + 1) * share]
                share = shares[up_row]
                small_in[section, d, up_row : up_row + 1, :share] = whole[up_row : up_row + 1, d * share : (d + 1) * share]
            if got is dense_tables:
                share = shares[synth_row]
                left = (section * dp + d) * share
                small_in[section, d, synth_row : synth_row + 1, :share] = whole[synth_row : synth_row + 1, left : left + share]

    @pl.when(is_dense)
    def _():
        blocks_of(dense_tables, 0, True)
        blocks_of(dense_tables, 1, False)

    @pl.when(jnp.logical_not(is_dense))
    def _():
        blocks_of(random_tables, 1, True)

    for o in away:
        lend(small, o, 0).start()
        load(small, o, 0).start()

        @pl.when(is_dense)
        def _():
            lend(small, o, 1).start()
            load(small, o, 1).start()

    block = random_ref.shape[0] // (2 * chips)
    strip = block // 2

    def view(i, o, core):
        top = (core * chips + place.chip_at(o)) * block + i * strip
        return random_ref.at[pl.ds(pl.multiple_of(top, strip), strip)]

    def spread(i, way, step):
        return step < reach - 1 or i == way

    def turn_copy(i, way, step):
        turn = 1 if way == 0 else -1
        target = view(i, -turn * step, place.core)
        source = random_in.at[pl.ds(i * strip, strip)] if step == 0 else target
        return remote(source, target, turn_send.at[way, step, i], turn_recv.at[way, step, i], place.along(turn))

    def pass_copy(i, way, step):
        turn = 1 if way == 0 else -1
        target = view(i, -turn * (step + 1) if step >= 0 else 0, place.core)
        source = random_in.at[pl.ds(i * strip, strip)] if step < 0 else target
        at = 0 if step < 0 else 1 + 2 * step + way
        return remote(source, target, pass_send.at[at, i], pass_recv.at[at, i], place.sibling())

    def keep_copy(i):
        return pltpu.make_async_copy(random_in.at[pl.ds(i * strip, strip)], view(i, 0, place.core), random_sems.at[1, 1, i])

    def across_strip(o, device, way):
        top = pl.multiple_of((place.core * chips + place.chip_at(o)) * block, block)
        part_of = random_ref.at[pl.ds(top, block)]
        return remote(part_of, part_of, random_sems.at[way, 0, 2 + spot_of[o]], random_sems.at[way, 1, 2 + spot_of[o]], device)

    events = [(i, way, step) for step in range(reach) for i in (0, 1) for way in (0, 1) if spread(i, way, step)]

    @pl.when(jnp.logical_not(is_dense))
    def _():
        for i in (0, 1):
            for way in (0, 1):
                if spread(i, way, 0):
                    turn_copy(i, way, 0).start()
            pass_copy(i, 0, -1).start()
            keep_copy(i).start()
        for i, way, step in events:
            turn_copy(i, way, step).wait_recv()
            if step + 1 < reach and spread(i, way, step + 1):
                turn_copy(i, way, step + 1).start()
            pass_copy(i, way, step).start()
        for i in (0, 1):
            keep_copy(i).wait()
        pl.semaphore_wait(pltpu.get_barrier_semaphore(), 1)
        for o in away:
            across_strip(o, place.across(), 0).start()

    def cross(o):
        @pl.when(is_dense)
        def _():
            for i in crossing:
                load(i, o, 1).wait()
                lend(i, o, 1).wait_recv()
                store_sum(held(own, i, o, 1), [held(own, i, o, 1), held(sib, i, o, 1)], piece_rows[PIECES[i][0]])
                across_copy(i, o).start()

    for step in range(reach):
        for i in plain + crossing:
            for way in (0, 1):
                if carried(i, way, step):
                    o = (reach - step) * (1 if way == 0 else -1)
                    total(held(own, i, o, 0), i, o, arrivals(i, o))
                    ring_copy(i, way, step).start()
            if i == plain[-1]:
                for o in away[(0 if step == 0 else 2 * step - 1) : 2 * step + 1]:
                    cross(o)
    cross(0)

    @pl.when(is_dense)
    def _():
        for o in away:
            across_strip(o, place.across(), 0).wait_recv()
            across_strip(o, place.sibling(), 1).start()

    outs = dict(value=value_ref, out=out_ref, up=up_ref, down=down_ref, small=small_ref)
    for i in plain + (small,):
        total(outs[PIECES[i][0]], i, 0, arrivals(i, 0))
    wides = dict(first=first_wide, second_a=second_wide.at[:, pl.ds(0, half)], second_b=second_wide.at[:, pl.ds(half, half)])
    for i in dense:
        total(wides[PIECES[i][0]], i, 0, arrivals(i, 0))
    mine = pl.multiple_of(place.core * quarter, 8)
    theirs = pl.multiple_of((1 - place.core) * quarter, 8)
    last = [
        remote(wide.at[pl.ds(theirs, quarter)], got, wide_sems.at[0, n], wide_sems.at[1, n], place.sibling())
        for n, (wide, got) in enumerate(((first_wide, first_part), (second_wide, second_part)))
    ]
    for copy in last:
        copy.start()
    for copy in last:
        copy.wait()
    for ref, wide, got, cols in ((first_ref, first_wide, first_part, dense_cols), (second_ref, second_wide, second_part, second_cols)):
        ref[:, pl.ds(pl.multiple_of(place.core * cols, cols), cols)] = wide[pl.ds(mine, quarter), :]
        ref[:, pl.ds(pl.multiple_of((1 - place.core) * cols, cols), cols)] = got[...]

    for o in away:
        for i in plain + (small,):
            lend(i, o, 0).wait_send()

        @pl.when(is_dense)
        def _():
            for i in dense:
                lend(i, o, 0).wait_send()
            for i in crossing:
                lend(i, o, 1).wait_send()
                across_copy(i, o).wait_send()

    @pl.when(is_dense)
    def _():
        for o in away:
            across_strip(o, place.sibling(), 1).wait()

    @pl.when(jnp.logical_not(is_dense))
    def _():
        for o in away:
            across_strip(o, place.across(), 0).wait_send()
        for i in (0, 1):
            pass_copy(i, 0, -1).wait()
            for way in (0, 1):
                for step in range(reach):
                    if spread(i, way, step):
                        turn_copy(i, way, step).wait_send()
        for e in events:
            pass_copy(*e).wait()

    for step in range(reach):
        for i in order:
            for way in (0, 1):
                if carried(i, way, step):
                    ring_copy(i, way, step).wait_send()


def reduce_grads(dp, value, out, up, down, first, second, random, dense_tables, random_tables, shares):
    chips = dp // 2
    rows, width = value.shape[0] // dp, value.shape[1]
    ff_rows = down.shape[0] // dp
    ff = up.shape[1]
    dense_rows = first.shape[0] // dp
    dense_cols = first.shape[1] // 2
    second_cols = second.shape[1] // 2
    sizes = (rows, ff_rows, dense_rows, dense_cols, second_cols, chips)
    reach = chips // 2
    count = len(PIECES)
    bf, f32 = jnp.bfloat16, jnp.float32
    anywhere = pl.BlockSpec(memory_space=pl.ANY)
    inside = pl.BlockSpec(memory_space=pltpu.VMEM)
    dma = pltpu.SemaphoreType.DMA
    blocks = ((rows, width), (rows, width), (rows, ff), (ff_rows, width))
    wide = ((dense_rows, dense_cols), (dense_rows, second_cols))
    scratch = [pltpu.VMEM((2, dp) + small_block, f32)]
    for _ in range(2):
        scratch += [pltpu.VMEM((chips,) + b, bf) for b in blocks]
        scratch += [pltpu.VMEM((2, chips) + small_block, f32)]
        scratch += [pltpu.VMEM((2, chips) + w, bf) for w in wide]
    scratch += [pltpu.VMEM((2, reach) + b, bf) for b in blocks]
    scratch += [pltpu.VMEM((2, reach) + small_block, f32)]
    scratch += [pltpu.VMEM((2, reach) + w, bf) for w in wide]
    scratch += [pltpu.VMEM((chips,) + small_block, f32)]
    scratch += [pltpu.VMEM((chips,) + w, bf) for w in wide]
    scratch += [pltpu.VMEM(w, f32) for w in wide]
    scratch += [pltpu.VMEM((dense_rows // 2, w[1]), f32) for w in wide]
    scratch += [
        dma((2, chips, count)),
        dma((2, chips, count)),
        dma((2, chips, count)),
        dma((2, reach, count)),
        dma((2, reach, count)),
        dma((chips, count)),
        dma((chips, count)),
        dma((2, 2)),
        dma((2, 2, 2 + chips)),
        dma((2, reach, 2)),
        dma((2, reach, 2)),
        dma((1 + 2 * reach, 2)),
        dma((1 + 2 * reach, 2)),
    ]
    tables = len(dense_tables)
    return pl.pallas_call(
        functools.partial(reduce_kernel, dp, sizes, shares, tables),
        out_shape=tuple(jax.ShapeDtypeStruct(b, f32) for b in blocks + (small_block,))
        + (
            jax.ShapeDtypeStruct((dense_rows // 2, first.shape[1]), f32),
            jax.ShapeDtypeStruct((dense_rows // 2, second.shape[1]), f32),
            jax.ShapeDtypeStruct((dp * random.shape[0], random.shape[1]), bf),
        ),
        in_specs=[anywhere] * 7 + [inside] * (2 * tables),
        out_specs=[inside] * 7 + [anywhere],
        scratch_shapes=scratch,
        compiler_params=pltpu.CompilerParams(
            collective_id=1, has_side_effects=True, vmem_limit_bytes=63 << 20
        ),
        name="reduce_grads",
    )(value, out, up, down, first, second, random, *dense_tables, *random_tables)


norm_eps = 1e-05
masked_score = -1e30
gelu_scale = 0.7978845608028654
gelu_cube = 0.044715
bf16, f32 = jnp.bfloat16, jnp.float32


def dot_rows(a, b):
    return lax.dot_general(a, b, (((1,), (0,)), ((), ())), preferred_element_type=f32)


def dot_back(a, b):
    return lax.dot_general(a, b, (((1,), (1,)), ((), ())), preferred_element_type=f32)


def dot_down(a, b):
    return lax.dot_general(a, b, (((0,), (0,)), ((), ())), preferred_element_type=f32)


def gelu_tanh(v):
    return jnp.tanh(gelu_scale * (v + gelu_cube * (v * v * v)))


def gelu(v):
    return 0.5 * v * (1.0 + gelu_tanh(v))


def gelu_both(v):
    t = gelu_tanh(v)
    value = 0.5 * v * (1.0 + t)
    slope = 0.5 * (1.0 + t) + 0.5 * v * (1.0 - t * t) * (gelu_scale * (1.0 + 3.0 * gelu_cube * (v * v)))
    return value, slope


def standard(v):
    centre = v - jnp.mean(v, axis=-1, keepdims=True)
    inverse = lax.rsqrt(jnp.mean(centre * centre, axis=-1, keepdims=True) + norm_eps)
    return centre * inverse, inverse


def standard_back(unit, inverse, grad):
    middle = jnp.mean(grad, axis=-1, keepdims=True)
    slant = jnp.mean(grad * unit, axis=-1, keepdims=True)
    return inverse * (grad - middle - unit * slant)


def column_sum(v):
    return jnp.sum(v.astype(f32), axis=0, keepdims=True)


class Bench:
    def __init__(self, **refs):
        self.__dict__.update(refs)
        self.waiting = {}
        self.used = 0
        self.sent = []
        self.last_tiles = []

    def vector(self, name, at):
        row = name
        return self.vectors[row : row + 1, at]

    def put_vector(self, name, at, value):
        row = name
        self.vector_grads[row : row + 1, at] = value

    def fetch(self, name, source, target):
        copy = pltpu.make_async_copy(source, target, self.sems.at[self.used])
        self.used += 1
        copy.start()
        self.waiting[name] = copy

    def need(self, *names):
        for name in names:
            copy = self.waiting.pop(name, None)
            if copy is not None:
                copy.wait()

    def send(self, source, target):
        copy = pltpu.make_async_copy(source, target, self.sems.at[self.used])
        self.used += 1
        copy.start()
        self.sent.append(copy)

    def settle(self):
        for copy in self.last_tiles:
            copy.wait()
        self.last_tiles = []

    def finish(self):
        self.settle()
        for copy in self.sent:
            copy.wait()

    def plan(self, added, *grads):
        self.added = added
        self.planned = list(grads)
        self.ahead()

    def tile_copies(self, grad, cols):
        across = grad.shape[1] // cols
        count = grad.shape[0] // unit_cols * across

        def place(t):
            top = pl.multiple_of(t // across * unit_cols, unit_cols)
            left = pl.multiple_of(lax.rem(t, across) * cols, cols)
            return grad.at[pl.ds(top, unit_cols), pl.ds(left, cols)]

        def result(t):
            slot = lax.rem(t, tile_slots)
            return pltpu.make_async_copy(self.stage.at[slot, :, pl.ds(0, cols)], place(t), self.stage_sems.at[slot])

        def prior(t):
            slot = lax.rem(t, tile_slots)
            return pltpu.make_async_copy(place(t), self.prior_stage.at[slot, :, pl.ds(0, cols)], self.prior_sems.at[slot])

        return count, across, result, prior

    def ahead(self):
        if self.added and self.planned:
            count, _, _, prior = self.tile_copies(*self.planned[0])
            for t in range(min(count, tile_slots - 1)):
                prior(t).start()

    def emit(self, tile):
        grad, cols = self.planned.pop(0)
        added = self.added
        count, across, result, prior = self.tile_copies(grad, cols)
        reach = tile_slots - 1
        self.settle()

        def turn(t, carry):
            slot = lax.rem(t, tile_slots)
            if added:

                @pl.when(t + reach < count)
                def _():
                    prior(t + reach).start()

                prior(t).wait()

            @pl.when(t >= tile_slots)
            def _():
                result(t - tile_slots).wait()

            def write(value, lanes=None):
                at = (slot, slice(None), pl.ds(0, cols) if lanes is None else lanes)
                if value is None:
                    self.stage[at] = self.prior_stage[at] if added else jnp.zeros((unit_cols, lanes.size), bf16)
                else:
                    if added:
                        value = value + self.prior_stage[at].astype(f32)
                    self.stage[at] = value.astype(bf16)

            tile(t // across, lax.rem(t, across), write)
            result(t).start()
            return carry

        lax.fori_loop(0, count, turn, 0)
        self.last_tiles = [result(t) for t in range(max(0, count - tile_slots), count)]
        self.ahead()


tile_slots = 6
unit_cols = 256
unit_rows = 128


def cols_at(t):
    return pl.ds(pl.multiple_of(t * unit_cols, unit_cols), unit_cols)


def by_cols(loose, n, extent, body):
    def turn(t, carry):
        body(pl.ds(0, n), cols_at(t), t)
        return carry

    count = extent // unit_cols
    lax.fori_loop(0, count, turn, 0, unroll=(3 if count == 3 else 2) if loose and count % 6 in (0, 3) else 1)


def by_rows(n, body, start=0):
    def turn(t, carry):
        return body(pl.ds(pl.multiple_of(t * unit_rows, unit_rows), unit_rows), carry)

    return lax.fori_loop(0, n // unit_rows, turn, start, unroll=2)


def lanes_of_first(n, size):
    return lax.broadcasted_iota(jnp.int32, (n, 2 * size), 1) < size


def send_padded(b, n, **targets):
    for name, target in targets.items():
        ref = getattr(b, name)
        if n < b.slots:
            ref[n:] = jnp.zeros((b.slots - n, ref.shape[1]), bf16)
        b.send(ref, target)


def softmax(b, n, scores):
    if n < b.slots:
        scores = jnp.where(in_item(b, (n, n), 1), scores, masked_score)
    e = jnp.exp(scores - jnp.max(scores, axis=-1, keepdims=True))
    return (e * (1.0 / jnp.sum(e, axis=-1, keepdims=True))).astype(bf16)


def forward_part(b, n, dense):
    width, ff, heads, slots = b.width, b.ff, b.heads, b.slots
    size = width // heads
    whole = slice(0, width)
    rows = pl.ds(0, n)
    loose = not dense and n < slots

    def first_norm(at, carry):
        unit, _ = standard(b.x[at, :].astype(f32))
        b.a[at, :] = (unit * b.vector(FIRST_GAIN, whole) + b.vector(FIRST_SHIFT, whole)).astype(bf16)
        return carry

    b.need("x")
    by_rows(n, first_norm)
    if dense:
        b.need("first")

        def hidden(rows, at, t):
            p = dot_rows(b.a[rows], b.first[:, at]) + b.vector(SYNTH_BIAS, at)
            b.p[rows, at] = p
            b.s[rows, at] = gelu(p).astype(bf16)

        by_cols(loose, n, width, hidden)
        b.send(b.p.at[rows], b.p_out.at[rows])
    b.need("value")

    def project(rows, at, t):
        b.v[rows, at] = dot_rows(b.a[rows], b.value[:, at]).astype(bf16)

    by_cols(loose, n, width, project)
    b.need("second" if dense else "att")

    def pair(i, carry):
        here = pl.ds(pl.multiple_of(i * 2 * size, 2 * size), 2 * size)
        values = b.v[:n, here]
        got = []
        for j in range(2):
            h = 2 * i + j
            if dense:
                scores = dot_rows(b.s[:n], b.second[:, pl.ds(pl.multiple_of(h * slots, slots), n)])
                b.att[h, :n, :n] = softmax(b, n, scores)
            got.append(dot_rows(b.att[h, :n, :n], values))
        b.o[:n, here] = jnp.where(lanes_of_first(n, size), got[0], got[1]).astype(bf16)
        return carry

    lax.fori_loop(0, heads // 2, pair, 0, unroll=1)
    if dense:
        b.send(b.att.at[:, rows, rows], b.att_out.at[:, rows, rows])
        b.send(b.v.at[rows], b.v_out.at[rows])
        b.send(b.o.at[rows], b.o_out.at[rows])
    b.need("out")

    def branch(rows, at, t):
        b.y[rows, at] = b.x[rows, at].astype(f32) + (dot_rows(b.o[rows], b.out[:, at]) + b.vector(OUT_BIAS, at))

    by_cols(loose, n, width, branch)
    if dense:
        b.send(b.y.at[rows], b.y_out.at[rows])

    def second_norm(at, carry):
        unit, _ = standard(b.y[at, :])
        b.u[at, :] = (unit * b.vector(SECOND_GAIN, whole) + b.vector(SECOND_SHIFT, whole)).astype(bf16)
        return carry

    by_rows(n, second_norm)
    b.need("up")

    def up(rows, at, t):
        m = dot_rows(b.u[rows], b.up[:, at]) + b.vector(UP_BIAS, at)
        b.m[rows, at] = m.astype(b.m.dtype)
        b.r[rows, at] = gelu(m).astype(bf16)

    by_cols(loose, n, ff, up)
    if dense:
        b.send(b.m.at[rows], b.m_out.at[rows])
    b.need("down")

    def down(rows, at, t):
        z = b.y[rows, at] + (dot_rows(b.r[rows], b.down[:, at]) + b.vector(DOWN_BIAS, at))
        if n < slots:
            z = jnp.where(in_item(b, (n, unit_cols), 0), z, 0.0)
        b.z[rows, at] = z.astype(bf16)

    by_cols(loose, n, width, down)
    if n < slots:
        b.z[n:] = jnp.zeros((slots - n, width), bf16)
    b.send(b.z, b.states.at[b.item])
    if dense:
        b.send(b.z, b.z_out)
    else:
        send_padded(b, n, r=b.r_out, o=b.o_out, a=b.a_out)


def plan_grads(b, added):
    wide = 2 * b.width
    b.plan(
        added, (b.down_grad, b.width), (b.up_grad, wide), (b.out_grad, b.width), (b.value_grad, b.width),
        (b.second_grad, wide), (b.first_grad, b.width),
    )


def random_copies(b, n):
    part = pl.ds(0, n)

    def prior(i):
        slot = lax.rem(i, 2)
        return pltpu.make_async_copy(
            b.random_grad.at[pl.ds(2 * i, 2), part, part], b.random_old.at[slot, :, part, part], b.random_sems.at[0, slot]
        )

    def result(i):
        slot = lax.rem(i, 2)
        return pltpu.make_async_copy(
            b.random_stage.at[slot, :, part, part], b.random_grad.at[pl.ds(2 * i, 2), part, part], b.random_sems.at[1, slot]
        )

    return prior, result


def backward_part(b, n, dense, added):
    width, ff, heads, slots = b.width, b.ff, b.heads, b.slots
    size = width // heads
    wide = 2 * width
    whole = slice(0, width)
    loose = not dense and n < slots
    b.need("c", "m", "down")
    if not dense and n < slots:
        b.c[:n] = jnp.where(in_item(b, (n, width), 0), b.c[:n], jnp.zeros((), bf16))

    def down_rows(rows, at, t):
        dr = dot_back(b.c[rows], b.down_rows(t))
        value, slope = gelu_both(b.m[rows, at].astype(f32))
        gm = (slope * dr).astype(bf16)
        b.gm[rows, at] = gm
        b.put_vector(UP_BIAS, at, column_sum(gm))
        return value

    def down_tile(t, _, write):
        value = down_rows(pl.ds(0, n), cols_at(t), t)
        write(dot_down(value.astype(bf16), b.c[:n]))

    if dense:
        b.emit(down_tile)
    else:
        by_cols(loose, n, ff, down_rows)
        send_padded(b, n, gm=b.gm_out, c=b.c_out)
    b.need("up", "y")

    def up_back(rows, at, t):
        b.wide[rows, at] = dot_back(b.gm[rows], b.up[at, :ff])

    by_cols(loose, n, width, up_back)
    if dense:
        b.fetch("second", b.second_in, b.up)
    none = jnp.zeros((1, width), f32)

    def second_back(at, carry):
        unit, inverse = standard(b.y[at, :])
        gain = b.vector(SECOND_GAIN, whole)
        b.u[at, :] = (unit * gain + b.vector(SECOND_SHIFT, whole)).astype(bf16)
        du = b.wide[at, :]
        gf = b.c[at, :].astype(f32)
        gy = gf + standard_back(unit, inverse, du * gain)
        b.gy[at, :] = gy
        gb = gy.astype(bf16)
        b.gb[at, :] = gb
        found = (column_sum(du * unit), column_sum(du), column_sum(gb), column_sum(gf))
        return tuple(a + f for a, f in zip(carry, found))

    sums = by_rows(n, second_back, (none,) * 4)
    for name, total in zip((SECOND_GAIN, SECOND_SHIFT, OUT_BIAS, DOWN_BIAS), sums):
        b.put_vector(name, whole, total)
    if dense:
        b.emit(
            lambda t, s, write: write(dot_down(b.u[:n, cols_at(t)], b.gm[:n, pl.ds(pl.multiple_of(s * wide, wide), wide)])),
        )
    else:
        send_padded(b, n, u=b.u_out, gb=b.gb_out)
    b.need("o", "out")
    if dense:
        b.emit(lambda t, s, write: write(dot_down(b.o[:n, cols_at(t)], b.gb[:n])))

    def out_back(rows, at, t):
        b.go[rows, at] = dot_back(b.gb[rows], b.out[at, :]).astype(bf16)

    by_cols(loose, n, width, out_back)
    b.need("v", "att")

    def pair_back(i, keep):
        here = pl.ds(pl.multiple_of(i * 2 * size, 2 * size), 2 * size)
        values, grads = b.v[:n, here], b.go[:n, here]
        first = lanes_of_first(n, size)
        got = []
        for j in range(2):
            own = jnp.where(first if j == 0 else jnp.logical_not(first), grads, jnp.zeros_like(grads))
            weight = b.att[2 * i + j, :n, :n]
            mixed = weight.astype(f32) * dot_back(own, values)
            keep(2 * i + j, j, mixed - weight.astype(f32) * jnp.sum(mixed, axis=-1, keepdims=True))
            got.append(dot_down(weight, grads))
        b.gv[:n, here] = jnp.where(first, got[0], got[1]).astype(bf16)

    if dense:

        def keep_dense(h, j, ds):
            b.gs[:n, pl.ds(pl.multiple_of(h * slots, slots), n)] = ds.astype(bf16)

        def loop(i, carry):
            pair_back(i, keep_dense)
            return carry

        lax.fori_loop(0, heads // 2, loop, 0)
    else:

        prior, result = random_copies(b, n if added else slots)

        def loop(i, carry):
            slot = lax.rem(i, 2)
            if added:

                @pl.when(i + 1 < heads // 2)
                def _():
                    prior(i + 1).start()

                prior(i).wait()

            @pl.when(i >= 2)
            def _():
                result(i - 2).wait()

            def keep_random(h, j, ds):
                if added:
                    ds = ds + b.random_old[slot, j, :n, :n].astype(f32)
                elif n < slots:
                    b.random_stage[slot, j] = jnp.zeros((slots, slots), bf16)
                b.random_stage[slot, j, :n, :n] = ds.astype(bf16)

            pair_back(i, keep_random)
            result(i).start()
            return carry

        lax.fori_loop(0, heads // 2, loop, 0)
        for i in (heads // 2 - 2, heads // 2 - 1):
            result(i).wait()
    b.need("x")
    if dense:

        def first_norm(at, carry):
            unit, _ = standard(b.x[at, :].astype(f32))
            b.a[at, :] = (unit * b.vector(FIRST_GAIN, whole) + b.vector(FIRST_SHIFT, whole)).astype(bf16)
            return carry

        by_rows(n, first_norm)
        b.emit(lambda t, s, write: write(dot_down(b.a[:n, cols_at(t)], b.gv[:n])))
    else:
        send_padded(b, n, gv=b.gv_out)
    if dense:
        b.need("p")

        def slopes(rows, at, t):
            value, slope = gelu_both(b.p[rows, at])
            b.s[rows, at] = value.astype(bf16)
            b.wide[rows, at] = slope

        by_cols(loose, n, width, slopes)
        group = wide // slots

        def second_tile(t, s, write):
            tile = b.s[:n, cols_at(t)]
            if n == slots:
                write(dot_down(tile, b.gs[:n, pl.ds(pl.multiple_of(s * wide, wide), wide)]))
                return
            for q in range(group):
                left = pl.multiple_of(s * wide + q * slots, slots)
                write(dot_down(tile, b.gs[:n, pl.ds(left, n)]), pl.ds(q * slots, n))
                write(None, pl.ds(q * slots + n, slots - n))

        b.emit(second_tile)
        b.need("second")

        def hidden_back(rows, at, t):
            if n == slots:
                hidden = dot_back(b.gs[rows], b.up[at, :])
            else:
                hidden = jnp.zeros((rows.size, unit_cols), f32)
                for h in range(heads):
                    part = slice(h * slots, h * slots + n)
                    hidden = hidden + dot_back(b.gs[rows, part], b.up[at, part])
            gp = (b.wide[rows, at] * hidden).astype(bf16)
            b.gp[rows, at] = gp
            b.put_vector(SYNTH_BIAS, at, column_sum(gp))

        by_cols(loose, n, width, hidden_back)
        b.emit(lambda t, s, write: write(dot_down(b.a[:n, cols_at(t)], b.gp[:n])))
    b.need("value", "first")

    def normed_back(rows, at, t):
        ga = dot_back(b.gv[rows], b.value[at, :])
        if dense:
            ga = ga + dot_back(b.gp[rows], b.first[at, :])
        b.wide[rows, at] = ga

    by_cols(loose, n, width, normed_back)

    def first_back(at, carry):
        unit, inverse = standard(b.x[at, :].astype(f32))
        ga = b.wide[at, :]
        dx = b.gy[at, :] + standard_back(unit, inverse, ga * b.vector(FIRST_GAIN, whole))
        b.dx[at, :] = dx.astype(bf16)
        return carry[0] + column_sum(ga * unit), carry[1] + column_sum(ga)

    sums = by_rows(n, first_back, (none,) * 2)
    b.put_vector(FIRST_GAIN, whole, sums[0])
    b.put_vector(FIRST_SHIFT, whole, sums[1])
    if n < slots:
        b.dx[n:] = jnp.zeros((slots - n, width), bf16)
    if not dense:
        b.send(b.dx, b.dx_out)
    b.send(b.dx, b.grads_in.at[b.item])
    b.send(b.vector_grads, b.table_out)


def item_of(lengths, turn):
    if lengths.shape[0] == 2:
        return jnp.where(lengths[1] < lengths[0], 1 - turn, turn)
    return jnp.int32(turn)


def by_length(section, lengths, turn, slots, call, long_late=False):
    long = lengths[item_of(lengths, turn)] > slots // 2
    if turn == 0 and not long_late:
        branches, which = (slots, slots // 2, 0), jnp.where(long, 0, 1)
    else:
        branches, which = (slots // 2, slots, 0), jnp.where(long, 1, 0)
    which = jnp.where(lax.axis_index(section_axis) == section, which, 2)
    return lax.switch(which, [functools.partial(call, n) for n in branches])


def in_item(b, shape, axis):
    return lax.broadcasted_iota(jnp.int32, shape, axis) < b.length


def shape_of(table):
    slots, width = table.x.shape
    return dict(width=width, ff=table.m.shape[1], heads=table.att.shape[0], slots=slots)


class ForwardRefs(NamedTuple):
    lengths: Any
    vectors: Any
    x_in: Any
    first_in: Any
    second_in: Any
    value_in: Any
    out_in: Any
    up_in: Any
    down_in: Any
    states: Any
    z_out: Any
    p_out: Any
    att_out: Any
    v_out: Any
    o_out: Any
    y_out: Any
    m_out: Any
    x: Any
    first: Any
    second: Any
    value: Any
    out: Any
    up: Any
    down: Any
    z: Any
    p: Any
    att: Any
    v: Any
    o: Any
    y: Any
    m: Any
    a: Any
    s: Any
    u: Any
    r: Any
    sems: Any


def dense_forward_kernel(n, turn, *refs):
    if n == 0:
        return
    refs = refs[:9] + refs[9 + (turn > 0) :]
    table = ForwardRefs(*refs)
    shape = shape_of(table)

    item = item_of(table.lengths, turn)
    b = Bench(item=item, length=table.lengths[item], **table._asdict(), **shape)
    rows = pl.ds(0, n)
    b.fetch("x", b.x_in.at[item, rows], b.x.at[rows])
    b.fetch("first", b.first_in, b.first)
    b.fetch("value", b.value_in, b.value)
    b.fetch("second", b.second_in, b.second)
    b.fetch("out", b.out_in, b.out)
    b.fetch("up", b.up_in, b.up)
    b.fetch("down", b.down_in, b.down)
    forward_part(b, n, True)
    b.finish()


class BackwardRefs(NamedTuple):
    lengths: Any
    vectors: Any
    x_in: Any
    c_in: Any
    p_in: Any
    att_in: Any
    v_in: Any
    o_in: Any
    y_in: Any
    m_in: Any
    first_in: Any
    second_in: Any
    value_in: Any
    out_in: Any
    up_in: Any
    down_in: Any
    grads_in: Any
    table_out: Any
    down_grad: Any
    up_grad: Any
    out_grad: Any
    value_grad: Any
    first_grad: Any
    second_grad: Any
    x: Any
    c: Any
    p: Any
    att: Any
    v: Any
    o: Any
    y: Any
    m: Any
    first: Any
    value: Any
    out: Any
    up: Any
    a: Any
    u: Any
    s: Any
    go: Any
    gv: Any
    gp: Any
    gb: Any
    gy: Any
    wide: Any
    dx: Any
    feed: Any
    stage: Any
    prior_stage: Any
    vector_grads: Any
    sems: Any
    stage_sems: Any
    prior_sems: Any


def dense_backward_kernel(n, turn, *refs):
    if n == 0:
        return
    refs = refs[:16] + refs[16 + (7 if turn > 0 else 5) :]
    table = BackwardRefs(*refs)
    shape = shape_of(table)
    ff, width = table.m.shape[1], table.x.shape[1]

    item = item_of(table.lengths, turn)
    b = Bench(item=item, length=table.lengths[item], **table._asdict(), **shape)
    b.gm, b.gs = b.feed.at[:, pl.ds(0, ff)], b.feed
    parts = width // unit_cols
    b.down_rows = lambda t: b.up[
        cols_at(lax.rem(t, parts)), pl.ds(pl.multiple_of(ff + t // parts * width, width), width)
    ]
    rows = pl.ds(0, n)
    b.fetch("c", b.c_in.at[rows], b.c.at[rows])
    b.fetch("m", b.m_in.at[rows], b.m.at[rows])
    for part in range(ff // width):
        b.fetch(f"down{part}", b.down_in.at[pl.ds(part * width, width)], b.up.at[:, pl.ds(ff + part * width, width)])
    b.fetch("up", b.up_in, b.up.at[:, pl.ds(0, ff)])
    b.fetch("y", b.y_in.at[rows], b.y.at[rows])
    b.fetch("o", b.o_in.at[rows], b.o.at[rows])
    b.fetch("out", b.out_in, b.out)
    b.fetch("v", b.v_in.at[rows], b.v.at[rows])
    b.fetch("att", b.att_in.at[:, rows, rows], b.att.at[:, rows, rows])
    b.fetch("x", b.x_in.at[item, rows], b.x.at[rows])
    b.fetch("p", b.p_in.at[rows], b.p.at[rows])
    b.fetch("value", b.value_in, b.value)
    b.fetch("first", b.first_in, b.first)
    plan_grads(b, turn > 0)
    b.need(*[f"down{part}" for part in range(ff // width)])
    backward_part(b, n, True, turn > 0)
    b.finish()


class RandomRefs(NamedTuple):
    lengths: Any
    vectors: Any
    x_in: Any
    c_in: Any
    att_in: Any
    value_in: Any
    out_in: Any
    up_in: Any
    down_in: Any
    states: Any
    grads_in: Any
    dx_out: Any
    table_out: Any
    random_grad: Any
    r_out: Any
    o_out: Any
    a_out: Any
    gm_out: Any
    u_out: Any
    gb_out: Any
    gv_out: Any
    c_out: Any
    x: Any
    c: Any
    att: Any
    v: Any
    o: Any
    y: Any
    m: Any
    value: Any
    out: Any
    up: Any
    down: Any
    a: Any
    u: Any
    go: Any
    gv: Any
    gb: Any
    gy: Any
    wide: Any
    z: Any
    dx: Any
    r: Any
    gm: Any
    random_stage: Any
    random_old: Any
    vector_grads: Any
    sems: Any
    random_sems: Any


def random_kernel(n, turn, *refs):
    if n == 0:
        return
    refs = refs[:9] + refs[9 + (3 if turn > 0 else 1) :]
    table = RandomRefs(*refs)
    shape = shape_of(table)

    item = item_of(table.lengths, turn)
    b = Bench(item=item, length=table.lengths[item], **table._asdict(), **shape)
    rows = pl.ds(0, n)
    b.fetch("x", b.x_in.at[rows], b.x.at[rows])
    b.fetch("value", b.value_in, b.value)
    b.fetch("att", b.att_in.at[:, rows, rows], b.att.at[:, rows, rows])
    b.fetch("out", b.out_in, b.out)
    b.fetch("up", b.up_in, b.up)
    b.fetch("down", b.down_in, b.down)
    b.down_rows = lambda t: b.down[cols_at(t), :]
    b.fetch("c", b.c_in.at[item, rows], b.c.at[rows])
    if turn > 0:
        random_copies(b, n)[0](0).start()
    forward_part(b, n, False)
    backward_part(b, n, False, turn > 0)
    b.finish()


class AttentionRefs(NamedTuple):
    lengths: Any
    logits_in: Any
    att_out: Any
    att: Any
    sems: Any


def random_attention_kernel(n, turn, *refs):
    if n == 0:
        return
    table = AttentionRefs(*refs)
    heads, slots, _ = table.att.shape
    b = Bench(length=table.lengths[item_of(table.lengths, turn)], slots=slots, **table._asdict())
    rows = pl.ds(0, n)
    half = heads // 2
    for k in (0, 1):
        part = pl.ds(k * half, half)
        b.fetch(k, b.logits_in.at[part, rows, rows], b.att.at[part, rows, rows])
    for k in (0, 1):
        b.need(k)

        def head(h, carry):
            b.att[h, :n, :n] = softmax(b, n, b.att[h, :n, :n].astype(f32))
            return carry

        lax.fori_loop(k * half, (k + 1) * half, head, 0)
        part = pl.ds(k * half, half)
        b.send(b.att.at[part, rows, rows], b.att_out.at[part, rows, rows])
    b.finish()


def random_attention(n, turn, lengths, logits):
    return pl.pallas_call(
        functools.partial(random_attention_kernel, n, turn),
        out_shape=S(logits.shape, bf16),
        in_specs=[scalars, anywhere],
        out_specs=anywhere,
        scratch_shapes=[] if n == 0 else [vmem(*logits.shape), pltpu.SemaphoreType.DMA((4,))],
        compiler_params=own_params(),
        name=f"random_attention_{n}",
    )(lengths, logits)


def weight_steps(kept, grads, c, r, o, a, gm, u, gb, gv, stage, sems, stage_sems):
    count = len(kept)
    slots = c.shape[0] // count
    b = Bench(stage=stage, sems=sems, stage_sems=stage_sems, width=c.shape[1])
    wide = 2 * b.width
    def need(*names):
        b.need(*[f"{name}{k}" for name in names for k in range(count)])

    def begin():
        for name, ref, at in (
            ("o", o, 1), ("gb", gb, 5), ("a", a, 2), ("gv", gv, 6), ("c", c, 7), ("r", r, 0), ("gm", gm, 3), ("u", u, 4),
        ):
            for k in range(count):
                b.fetch(f"{name}{k}", kept[k][at], ref.at[pl.ds(k * slots, slots)])
        out_grad, value_grad, down_grad, up_grad = grads
        b.plan(False, (out_grad, b.width), (value_grad, b.width), (down_grad, b.width), (up_grad, wide))

    def narrow():
        need("o", "gb")
        b.emit(lambda t, s, write: write(dot_down(o[:, cols_at(t)], gb[...])))
        need("a", "gv")
        b.emit(lambda t, s, write: write(dot_down(a[:, cols_at(t)], gv[...])))

    def down():
        need("c", "r")
        b.emit(lambda t, s, write: write(dot_down(r[:, cols_at(t)], c[...])))

    def up():
        need("gm", "u")
        b.emit(lambda t, s, write: write(dot_down(u[:, cols_at(t)], gm[:, pl.ds(pl.multiple_of(s * wide, wide), wide)])))
        b.finish()

    return begin, narrow, down, up


anywhere = pl.BlockSpec(memory_space=pl.ANY)
inside = pl.BlockSpec(memory_space=pltpu.VMEM)
scalars = pl.BlockSpec(memory_space=pltpu.SMEM)
S = jax.ShapeDtypeStruct


def vmem(*shape, dtype=bf16):
    return pltpu.VMEM(shape, dtype)


def own_params():
    return pltpu.CompilerParams(vmem_limit_bytes=63 << 20, has_side_effects=True)


def dense_forward(n, turn, lengths, vectors, inputs, weights, heads, states):
    _, slots, width = inputs.shape
    ff = weights["up"].shape[1]
    outs = (
        S(inputs.shape, bf16), S((slots, width), bf16), S((slots, width), f32), S((heads, slots, slots), bf16),
        S((slots, width), bf16), S((slots, width), bf16), S((slots, width), f32), S((slots, ff), bf16),
    )
    rows = vmem(slots, width)
    old = [] if states is None else [states]
    return pl.pallas_call(
        functools.partial(dense_forward_kernel, n, turn),
        out_shape=outs,
        in_specs=[scalars, inside if n else anywhere] + [anywhere] * (7 + len(old)),
        out_specs=[anywhere] * 8,
        input_output_aliases={9: 0} if old else {},
        scratch_shapes=[] if n == 0 else [
            rows, vmem(width, width), vmem(width, heads * slots), vmem(width, width), vmem(width, width), vmem(width, ff),
            vmem(ff, width), rows, vmem(slots, width, dtype=f32), vmem(heads, slots, slots), rows, rows,
            vmem(slots, width, dtype=f32), vmem(slots, ff), rows, rows, rows, vmem(slots, ff), pltpu.SemaphoreType.DMA((20,)),
        ],
        compiler_params=own_params(),
        name=f"dense_forward_{n}",
    )(lengths, vectors, inputs, *[weights[k] for k in ("first", "second", "value", "out", "up", "down")], *old)


def dense_backward(n, turn, lengths, vectors, inputs, c, kept, weights, grads_in, old):
    p, att, v, o, y, m = kept
    heads = att.shape[0]
    _, slots, width = inputs.shape
    ff = weights["up"].shape[1]
    names = ("down", "up", "out", "value", "first", "second")
    outs = (S(inputs.shape, bf16), S(vectors.shape, f32)) + tuple(S(weights[name].shape, bf16) for name in names)
    rows = vmem(slots, width)
    square = vmem(width, width)
    aliases = {16: 0}
    aliases.update({17 + n: 2 + n for n in range(len(old))})
    return pl.pallas_call(
        functools.partial(dense_backward_kernel, n, turn),
        out_shape=outs,
        in_specs=[scalars, inside if n else anywhere] + [anywhere] * (15 + len(old)),
        out_specs=[anywhere] * 8,
        input_output_aliases=aliases,
        scratch_shapes=[] if n == 0 else [
            rows, rows, vmem(slots, width, dtype=f32), vmem(heads, slots, slots), rows, rows,
            vmem(slots, width, dtype=f32), vmem(slots, ff), square, square, square, vmem(width, 2 * ff),
            rows, rows, rows, rows, rows, rows, rows, vmem(slots, width, dtype=f32), vmem(slots, width, dtype=f32), rows,
            vmem(slots, 2 * ff), vmem(tile_slots, unit_cols, 2 * width), vmem(tile_slots, unit_cols, 2 * width),
            pltpu.VMEM(vectors.shape, f32),
            pltpu.SemaphoreType.DMA((24,)), pltpu.SemaphoreType.DMA((tile_slots,)), pltpu.SemaphoreType.DMA((tile_slots,)),
        ],
        compiler_params=own_params(),
        name=f"dense_backward_{n}",
    )(
        lengths, vectors, inputs, c, p, att, v, o, y, m,
        *[weights[k] for k in ("first", "second", "value", "out", "up", "down")], grads_in, *old,
    )


def random_step(n, turn, lengths, vectors, x, cotangent, att, weights, states, old):
    heads, slots, _ = att.shape
    width = x.shape[1]
    ff = weights["up"].shape[1]
    narrow = S((slots, width), bf16)
    broad = S((slots, ff), bf16)
    outs = (
        S(cotangent.shape, bf16), S(cotangent.shape, bf16), narrow, S(vectors.shape, f32), S(att.shape, bf16),
        broad, narrow, narrow, broad, narrow, narrow, narrow, narrow,
    )
    rows = vmem(slots, width)
    square = vmem(width, width)
    deep = vmem(slots, width, dtype=f32)
    pair = vmem(2, 2, slots, slots)
    return pl.pallas_call(
        functools.partial(random_kernel, n, turn),
        out_shape=outs,
        in_specs=[scalars, inside if n else anywhere] + [anywhere] * (8 + len(old)),
        out_specs=[anywhere] * 13,
        input_output_aliases={9: 0, 10: 1, 11: 4} if old else {9: 0},
        scratch_shapes=[] if n == 0 else [
            rows, rows, vmem(heads, slots, slots), rows, rows, deep, vmem(slots, ff), square, square,
            vmem(width, ff), vmem(ff, width), rows, rows, rows, rows, rows, deep, deep, rows, rows,
            vmem(slots, ff), vmem(slots, ff), pair, pair, pltpu.VMEM(vectors.shape, f32),
            pltpu.SemaphoreType.DMA((28,)), pltpu.SemaphoreType.DMA((2, 2)),
        ],
        compiler_params=own_params(),
        name=f"random_step_{n}",
    )(lengths, vectors, x, cotangent, att, *[weights[k] for k in ("value", "out", "up", "down")], states, *old)


def weight_scratch(count, slots, width, ff):
    tall = vmem(count * slots, width)
    broad = vmem(count * slots, ff)
    return [
        tall, broad, tall, tall, broad, tall, tall, tall, vmem(tile_slots, unit_cols, 2 * width),
        pltpu.SemaphoreType.DMA((8 * count,)), pltpu.SemaphoreType.DMA((tile_slots,)),
    ]


def weights_kernel(count, *refs):
    kept = [refs[8 * k : 8 * k + 8] for k in range(count)]

    @pl.when(lax.axis_index(section_axis) == 1)
    def _():
        down, up, out, value, *scratch = refs[8 * count :]
        for step in weight_steps(kept, (out, value, down, up), *scratch):
            step()


def random_weights(kept, weights):
    slots, width = kept[0][1].shape
    ff = kept[0][0].shape[1]
    names = ("down", "up", "out", "value")
    return pl.pallas_call(
        functools.partial(weights_kernel, len(kept)),
        out_shape=tuple(S(weights[name].shape, bf16) for name in names),
        in_specs=[anywhere] * (8 * len(kept)),
        out_specs=[anywhere] * 4,
        scratch_shapes=weight_scratch(len(kept), slots, width, ff),
        compiler_params=own_params(),
        name="random_weights",
    )(*[a for item in kept for a in item])


def deliver_kernel(arrays, random_in, small, *refs):
    ins, outs = refs[:arrays], refs[arrays + 1 : 2 * arrays + 1]
    random_ref = refs[arrays]
    vectors = refs[2 * arrays + 1 : 2 * arrays + 1 + vector_count]
    narrow, wide, sems, random_sems = refs[2 * arrays + 1 + vector_count :]
    slots, rows, _ = narrow.shape
    count = random_in.shape[0] // rows

    def part(n):
        return pl.ds(pl.multiple_of(n * rows, rows), rows)

    def load(n):
        slot = lax.rem(n, slots)
        return pltpu.make_async_copy(random_in.at[part(n)], narrow.at[slot], random_sems.at[0, slot])

    def store(n):
        slot = lax.rem(n, slots)
        return pltpu.make_async_copy(wide.at[slot], random_ref.at[part(n)], random_sems.at[1, slot])

    for n in range(slots - 1):
        load(n).start()
    copies = [pltpu.make_async_copy(a, b, sems.at[n]) for n, (a, b) in enumerate(zip(ins, outs))]
    for copy in copies:
        copy.start()
    for row, ref in enumerate(vectors):
        ref[...] = small[row : row + 1, : ref.shape[1]]

    def turn(n, carry):
        @pl.when(n + slots - 1 < count)
        def _():
            load(n + slots - 1).start()

        load(n).wait()

        @pl.when(n >= slots)
        def _():
            store(n - slots).wait()

        wide[lax.rem(n, slots)] = narrow[lax.rem(n, slots)].astype(f32)
        store(n).start()
        return carry

    lax.fori_loop(0, count, turn, 0)
    for n in range(count - slots, count):
        store(n).wait()
    for copy in copies:
        copy.wait()


def deliver(random, small, extents, arrays):
    rows, cols = random.shape
    slots = 4
    inside = pl.BlockSpec(memory_space=pltpu.VMEM)
    return pl.pallas_call(
        functools.partial(deliver_kernel, len(arrays)),
        out_shape=(S(random.shape, f32),)
        + tuple(S(a.shape, f32) for a in arrays)
        + tuple(S((1, extent), f32) for extent in extents),
        in_specs=[anywhere, inside] + [inside] * len(arrays),
        out_specs=[anywhere] * (1 + len(arrays)) + [inside] * len(extents),
        scratch_shapes=[
            vmem(slots, rows // 12, cols), vmem(slots, rows // 12, cols, dtype=f32),
            pltpu.SemaphoreType.DMA((len(arrays),)), pltpu.SemaphoreType.DMA((2, slots)),
        ],
        compiler_params=own_params(),
        name="deliver",
    )(random, small, *arrays)


def run_layers(inputs, cotangent, lengths, weights, vectors, logits, finish_random):
    count, slots, _ = inputs.shape
    heads = logits.shape[0]
    states = None
    firsts, seconds = [], []
    for turn in range(count):

        def forward(n):
            return dense_forward(n, turn, lengths, vectors, inputs, weights, heads, states)

        states, z, *kept = by_length(0, lengths, turn, slots, forward)
        firsts.append(kept)
        seconds.append(passed_along(z, section_axis, 1))
    atts = [
        by_length(1, lengths, turn, slots, lambda n: random_attention(n, turn, lengths, logits)) for turn in range(count)
    ]
    seconds[0], *atts = lax.optimization_barrier((seconds[0], *atts))
    old, backs, random_tables, random_kept = [], [], [], []
    for turn in range(count):

        def step(n):
            return random_step(n, turn, lengths, vectors, seconds[turn], cotangent, atts[turn], weights, states, old)

        states, grads_in, dx, table, random_grad, *kept = by_length(1, lengths, turn, slots, step)
        old = [grads_in, random_grad]
        backs.append(passed_along(dx, section_axis, -1))
        random_tables.append(table)
        random_kept.append(kept)
    random_grad, *grads = finish_random(random_grad, random_kept, weights)
    dense_tables = []
    for turn in range(count):

        def backward(n):
            return dense_backward(
                n, turn, lengths, vectors, inputs, backs[turn], firsts[turn], weights, grads_in, grads
            )

        grads_in, table, *grads = by_length(0, lengths, turn, slots, backward, long_late=True)
        dense_tables.append(table)
    grads = dict(zip(("down", "up", "out", "value", "first", "second"), grads))
    return states, grads_in, grads, random_grad, dense_tables, random_tables


def random_finish_kernel(dp, count, random_in, *refs):
    kept = [refs[8 * k : 8 * k + 8] for k in range(count)]
    refs = refs[8 * count :]
    random_ref, down, up, out, value = refs[:5]
    grads = (out, value, down, up)
    (
        own, sib, ring, own_sems, sib_send, sib_recv, ring_send, ring_recv,
    ) = refs[5:13]
    begin, *meanwhile = weight_steps(kept, grads, *refs[13:])
    place = Place(dp)
    reach, chips = place.reach, place.chips
    block = random_in.shape[0] // (2 * chips)
    strip = block // 2
    away = (reach,) + tuple(o for t in range(reach - 1, 0, -1) for o in (t, -t)) + (0,)
    spot_of = {o: n for n, o in enumerate(away)}
    spot_of[-reach] = 0

    def part(ref, o, core):
        return ref.at[pl.ds(pl.multiple_of((core * chips + place.chip_at(o)) * block, block), block)]

    def load(o):
        return pltpu.make_async_copy(part(random_in, o, place.core), own.at[spot_of[o]], own_sems.at[spot_of[o]])

    def lend(o):
        at = spot_of[o]
        return remote(part(random_in, o, 1 - place.core), sib.at[at], sib_send.at[at], sib_recv.at[at], place.sibling())

    def carried(i, way, step):
        return step > 0 or i == way

    def ring_copy(i, way, step):
        turn = 1 if way == 0 else -1
        rows = pl.ds(i * strip, strip)
        return remote(
            own.at[spot_of[turn * (reach - step)], rows], ring.at[way, step, rows],
            ring_send.at[way, step, i], ring_recv.at[way, step, i], place.along(turn),
        )

    @pl.when(place.section == 1)
    def _():
        place.greet()
        for o in away:
            lend(o).start()
            load(o).start()
        begin()
        for step in range(reach + 1):
            for i in (0, 1):
                for way in (0, 1):
                    o = (reach - step) * (1 if way == 0 else -1)
                    if step < reach and not carried(i, way, step) or step == reach and way == 1:
                        continue
                    if i == 0:
                        load(o).wait()
                        lend(o).wait_recv()
                    rows = pl.ds(i * strip, strip)
                    terms = [own.at[spot_of[o], rows], sib.at[spot_of[o], rows]]
                    for back in (0, 1) if step == reach else (way,):
                        if step > 0 and carried(i, back, step - 1):
                            ring_copy(i, back, step - 1).wait_recv()
                            terms.append(ring.at[back, step - 1, rows])
                    store_sum(own.at[spot_of[o], rows], terms, strip)
                    if step < reach:
                        ring_copy(i, way, step).start()
            if meanwhile and step < reach:
                meanwhile.pop(0)()
        keep = pltpu.make_async_copy(own.at[spot_of[0]], random_ref, own_sems.at[chips])
        keep.start()
        for work in meanwhile:
            work()
        for o in away:
            lend(o).wait_send()
        keep.wait()
        for i in (0, 1):
            for way in (0, 1):
                for step in range(reach):
                    if carried(i, way, step):
                        ring_copy(i, way, step).wait_send()


def random_finish(dp, random, kept, weights):
    chips = dp // 2
    reach = chips // 2
    block = (random.shape[0] // dp, random.shape[1])
    slots, width = kept[0][1].shape
    ff = kept[0][0].shape[1]
    count = len(kept)
    dma = pltpu.SemaphoreType.DMA
    names = ("down", "up", "out", "value")
    return pl.pallas_call(
        functools.partial(random_finish_kernel, dp, count),
        out_shape=(S(block, random.dtype),) + tuple(S(weights[name].shape, bf16) for name in names),
        in_specs=[anywhere] * (1 + 8 * count),
        out_specs=[anywhere] * 5,
        scratch_shapes=[
            pltpu.VMEM((chips,) + block, random.dtype),
            pltpu.VMEM((chips,) + block, random.dtype),
            pltpu.VMEM((2, reach) + block, random.dtype),
            dma((chips + 1,)),
            dma((chips,)),
            dma((chips,)),
            dma((2, reach, 2)),
            dma((2, reach, 2)),
        ] + weight_scratch(count, slots, width, ff),
        compiler_params=pltpu.CompilerParams(
            collective_id=2, has_side_effects=True, vmem_limit_bytes=63 << 20
        ),
        name="random_finish",
    )(random, *[a for item in kept for a in item])


def passed_along(x, axis, by):
    size = lax.axis_size(axis)
    pairs = [(i, i + by) for i in range(size) if 0 <= i + by < size]
    return lax.ppermute(x, axis, pairs)


def table_of(vectors, ff):
    return jnp.stack([jnp.pad(v.astype(f32), (0, ff - v.shape[0])) for v in vectors])


def per_device(
    inputs,
    cotangent,
    lengths,
    first_gain,
    first_shift,
    value_weight,
    out_weight,
    out_bias,
    second_gain,
    second_shift,
    up_weight,
    up_bias,
    down_weight,
    down_bias,
    synth_first,
    synth_bias,
    synth_second,
    random_logits,
):
    dp = lax.axis_size(dp_axis)
    is_dense = lax.axis_index(section_axis) == 0
    value_share, out_share, up_share, down_share = value_weight[0], out_weight[0], up_weight[0], down_weight[0]
    ff = up_share.shape[1]
    shares = [
        a.reshape(1, -1)
        for a in (first_gain, first_shift, out_bias, second_gain, second_shift, down_bias, up_bias, synth_bias)
    ]
    extents = tuple(a.shape[1] for a in shares)
    ringed = (
        dp % 4 == 0 and dp > 4 and value_share.shape[0] % 16 == 0 and synth_first.shape[0] % 8 == 0
        and max(extents) <= small_block[1]
    )
    if ringed:
        value, out, up, down, first, second, table = gather_weights(
            dp, value_share, out_share, up_share, down_share, synth_first, synth_second, shares
        )
    else:
        value, out, up, down = (
            lax.all_gather(a, dp_axis, axis=0, tiled=True) for a in (value_share, out_share, up_share, down_share)
        )
        first, second = (lax.all_gather(a, (section_axis, dp_axis), axis=0, tiled=True) for a in (synth_first, synth_second))
        axes = [dp_axis] * synth_row + [(section_axis, dp_axis)]
        table = table_of([lax.all_gather(a[0], axis, axis=0, tiled=True) for a, axis in zip(shares, axes)], ff)
    weights = dict(value=value, out=out, up=up, down=down, first=first, second=second)

    def finish_random(grad, kept, of):
        flat = grad.reshape(-1, grad.shape[-1])
        return random_finish(dp, flat, kept, of) if ringed else (flat, *random_weights(kept, of))

    states, grads_in, grads, random_grad, dense_tables, random_tables = run_layers(
        inputs, cotangent, lengths, weights, table, random_logits, finish_random
    )
    arrays = [grads[name] for name in ("value", "out", "up", "down", "first", "second")]
    if ringed:
        g_value, g_out, g_up, g_down, small, g_first, g_second, random_grad = reduce_grads(
            dp, *arrays, random_grad, dense_tables, random_tables, extents
        )
        random_total, g_value, g_out, g_up, g_down, g_first, g_second, *g_vectors = deliver(
            random_grad, small, extents, (g_value, g_out, g_up, g_down, g_first, g_second)
        )
        g_vectors = [v.reshape(-1) for v in g_vectors]
    else:
        g_value, g_out, g_up, g_down = (
            lax.psum_scatter(a, dp_axis, scatter_dimension=0, tiled=True).astype(f32) for a in arrays[:4]
        )
        g_first, g_second = (
            lax.psum_scatter(jnp.where(is_dense, a, jnp.zeros_like(a)), (section_axis, dp_axis), scatter_dimension=0, tiled=True).astype(f32)
            for a in arrays[4:]
        )
        grad_table = jnp.where(is_dense, sum(dense_tables), sum(random_tables))
        g_vectors = [
            lax.psum_scatter(grad_table[row, : dp * extents[row]], dp_axis, scatter_dimension=0, tiled=True)
            for row in range(synth_row)
        ]
        synth_grad = jnp.where(is_dense, grad_table[synth_row, : 2 * dp * extents[synth_row]], 0.0)
        g_vectors.append(lax.psum_scatter(synth_grad, (section_axis, dp_axis), scatter_dimension=0, tiled=True))
        random_total = lax.psum(jnp.where(is_dense, jnp.zeros_like(random_grad), random_grad), (section_axis, dp_axis)).astype(f32)
    random_total = random_total.reshape(random_logits.shape)
    return (
        states[None],
        grads_in[None],
        g_vectors[FIRST_GAIN][None],
        g_vectors[FIRST_SHIFT][None],
        g_value[None],
        g_out[None],
        g_vectors[OUT_BIAS][None],
        g_vectors[SECOND_GAIN][None],
        g_vectors[SECOND_SHIFT][None],
        g_up[None],
        g_vectors[UP_BIAS][None],
        g_down[None],
        g_vectors[DOWN_BIAS][None],
        g_first,
        g_vectors[SYNTH_BIAS],
        g_second,
        random_total,
    )


def solution(mesh):
    in_specs = (
        P(dp_axis, None, None),
        P(dp_axis, None, None),
        P(dp_axis),
        P(section_axis, dp_axis),
        P(section_axis, dp_axis),
        P(section_axis, dp_axis, None),
        P(section_axis, dp_axis, None),
        P(section_axis, dp_axis),
        P(section_axis, dp_axis),
        P(section_axis, dp_axis),
        P(section_axis, dp_axis, None),
        P(section_axis, dp_axis),
        P(section_axis, dp_axis, None),
        P(section_axis, dp_axis),
        P((section_axis, dp_axis), None),
        P((section_axis, dp_axis)),
        P((section_axis, dp_axis), None),
        P(),
    )
    out_specs = (
        P(section_axis, dp_axis, None, None),
        P(section_axis, dp_axis, None, None),
        P(section_axis, dp_axis),
        P(section_axis, dp_axis),
        P(section_axis, dp_axis, None),
        P(section_axis, dp_axis, None),
        P(section_axis, dp_axis),
        P(section_axis, dp_axis),
        P(section_axis, dp_axis),
        P(section_axis, dp_axis, None),
        P(section_axis, dp_axis),
        P(section_axis, dp_axis, None),
        P(section_axis, dp_axis),
        P((section_axis, dp_axis), None),
        P((section_axis, dp_axis)),
        P((section_axis, dp_axis), None),
        P(),
    )
    return jax.shard_map(
        per_device, mesh=mesh, in_specs=in_specs, out_specs=out_specs, check_vma=False
    )
```
